32 devices in a mesh: member: 2 (over x), tile: 8 (over z, y), comp: 2 (over core).
Axes of the slice: x: 2, y: 2, z: 4, core: 2. Of those that a mesh axis runs over, the one named last changes fastest.
Arguments:
- prognostic_state: float32 [2, 256, 512, 128], P('comp', 'member', 'tile'), parts along dimension 1, may hold values from -6 to 6
- remapping_weight: bfloat16 [2, 512, 128, 128], P('comp', 'tile'), may hold values from -0.5 to 0.5
- diffusion: float32 [2, 256], P('comp', 'member'), parts along dimension 1, may hold values from 0.02 to 0.22
- column_op: float32 [2, 256, 128], P('comp', 'member'), parts along dimension 1, may hold values from -1 to 1
- couple_gain: float32 [2, 32], P('comp', 'member'), parts along dimension 1, may hold values from 0.3 to 1.5
- land_mask: int32 [512], P('tile'), may hold values 0 or 1
- dest_tile: int32 [2, 512, 1], replicated, may hold values from 0 to 7; in each aligned block of 64 rows (0 to 63, 64 to 127, ..., all dimensions but the last counted through in order) at most 16 rows name the same one
- dest_block: int32 [2, 512], replicated, may hold values from 0 to 63
Outputs:
- new_state: float32 [2, 256, 512, 128], P('comp', 'member', 'tile'), parts along dimension 1
The draws below stay inside these ranges and needn't reach their ends.
There are 2 independent parts, one for each index of `member`. The reference program is written for one: setup_inputs(seed, part) draws one part's arguments, and reference() takes and returns one part's arrays. A program takes and returns all parts, laid end to end along the dimension named above; an argument that names none is the same for every part. Nothing has to cross between parts.
Inputs may be any that keep to these rules, and one draw needn't show every extreme that they name: `dest_tile`: among the 64 grid rows of one tile of one component, no destination tile is named more than 16 times, a bound that some block reaches.
All inputs are finite; a program needn't handle non-finite values. No bound on the sum of `land_mask` on one device may be relied on, other than what follows from the above.
Results may differ from the reference program's by a relative error of at most 0.0026.
Values may be sent and summed in bfloat16 or wider, within the bound.
No kernel may reach another device: no remote copies, remote signals or barrier semaphores. Data moves between devices by JAX's collectives and lax.ppermute only.
A program may use at most 64 MiB of HBM per device.

```python
import math
import jax
import jax.numpy as jnp
import numpy as np
from jax import lax

NV = 16
SUB = 3
CY = 128
CX = 64
P_SIZE = 128
NX = 512
CAP = 16
N_TILE = 8


def draw_column_op(key, part):
    key = jax.random.fold_in(key, 11)
    first, second = jax.random.split(key)
    top = min(0.95, 1.0 - 0.56 / P_SIZE ** 0.5)
    diagonal = jax.random.uniform(first, (2, P_SIZE), jnp.float32, 0.55, top)
    spread = jax.random.truncated_normal(second, -2.0, 2.0, (2, P_SIZE, P_SIZE), jnp.float32) * (0.28 / P_SIZE ** 0.5)
    return spread + diagonal[:, :, None] * jnp.eye(P_SIZE, dtype=jnp.float32)[None]


def plant(array, rng, smallest, top_value):
    shape = array.shape
    index_at = [jax.random.randint(jax.random.fold_in(rng, axis), (), 0, shape[axis]) for axis in range(len(shape))]
    array = array.at[tuple(index_at)].set(smallest)
    longest = shape.index(max(shape))
    index_at[longest] = (index_at[longest] + 1) % shape[longest]
    return array.at[tuple(index_at)].set(top_value)


def block_scale(rng, shape, cuts, low, largest):
    loudness, own = 1.0, jax.random.fold_in(rng, 6)
    for dim, shards_of in cuts:
        steps = jnp.exp(jax.random.uniform(jax.random.fold_in(own, dim), (shards_of,), jnp.float32, low / len(cuts), largest / len(cuts)))
        loudness = loudness * jnp.repeat(steps, shape[dim] // shards_of).reshape([-1 if axis == dim else 1 for axis in range(len(shape))])
    return loudness


def shared_out(key, own, number, rows, amount, top, reach, lean):
    order = jax.random.permutation(key, amount)
    crowded, common = load_shares(amount, rows * top, reach, lean, True), load_shares(amount, rows * top, reach, lean, False)
    places = jnp.arange(amount)

    def named(sizes, turn):
        used = int((sizes > 0).sum())
        fixed = max(1, used // 4)
        shifted = fixed + (places - fixed + turn * (used - fixed)) % max(1, amount - fixed)
        return jnp.zeros((amount,), jnp.int32).at[order[jnp.where(places < fixed, places, shifted)]].set(jnp.asarray(sizes, jnp.int32))

    sizes = jnp.where(number % 4 == 0, named(crowded, number // 4), named(common, number - number // 4 - 1))
    mixed = jax.random.permutation(jax.random.fold_in(own, 3), amount)
    source_of, receiver = mixed[0:amount // 2 * 2:2], mixed[1:amount // 2 * 2:2]
    slack = jnp.minimum(sizes[source_of] - 1, reach - sizes[receiver]) // 2
    slack = jnp.where((source_of == order[0]) | (receiver == order[0]) | (sizes[receiver] == 0), 0, jnp.maximum(slack, 0))
    shifted = jax.random.randint(jax.random.fold_in(own, 4), (amount // 2,), 0, 1 << 20) % (slack + 1)
    sizes = sizes.at[source_of].add(-shifted).at[receiver].add(shifted)
    members = jnp.searchsorted(jnp.cumsum(sizes), jnp.arange(rows * top), side="right").astype(jnp.int32)
    listing = members.reshape(top, rows).T
    listing = listing[jax.random.permutation(jax.random.fold_in(own, 1), rows)]
    turn = jax.random.randint(jax.random.fold_in(own, 2), (rows, 1), 0, top)
    return jnp.take_along_axis(listing, (jnp.arange(top)[None, :] + turn) % top, axis=1)


def load_shares(count, total, limit, slope, full):
    loads = [(1 << 20) // math.isqrt(grade ** slope) + 1 for grade in range(1, count + 1)]
    largest = limit if full else min(limit, max(-(-total // count), total * loads[0] // sum(loads)))
    least = 1 if total - largest >= count - 1 else 0
    given, surplus = [largest] + [least] * (count - 1), total - largest - least * (count - 1)
    while surplus > 0:
        movable = [i for i in range(1, count) if given[i] < largest] or [i for i in range(1, count) if given[i] < limit]
        mass, left = sum([loads[i] for i in movable]), surplus
        for i in movable:
            more = min(limit - given[i], max(1, left * loads[i] // mass), surplus)
            given[i] = given[i] + more
            surplus = surplus - more
    return np.array(given)


def bell_draw(key, extent, scale, reach, shards=(), held_as=jnp.bfloat16):
    gain = block_scale(key, extent, shards, -0.22, 0.18) if shards else 1.0
    drawn = jax.random.normal(key, extent, jnp.float32) * scale * gain
    return jnp.minimum(jnp.maximum(drawn, -reach), reach).astype(held_as)


def setup_inputs(seed: int = 0, part: int = 0) -> dict:
    key_list = jax.random.split(jax.random.key(seed), 9)
    part_splits = jax.random.split(jax.random.fold_in(key_list[8], part), 9)
    prognostic_state = bell_draw(part_splits[0], (2, P_SIZE, NX, CY), 1.0, 6.0, ((0, 2), (2, 8)), jnp.float32)
    remapping_weight = bell_draw(key_list[1], (2, NX, CY, CY), CY ** -0.5, 0.5, ((0, 2), (1, 8)))
    diffusion = jnp.clip(jnp.exp(math.log(0.22) - 2.3978953 * jax.random.uniform(part_splits[2], (2, P_SIZE), jnp.float32) ** block_scale(part_splits[2], (2, P_SIZE), ((0, 2),), -0.2, 0.2)), 0.02, 0.22)
    column_op = draw_column_op(jax.random.fold_in(jax.random.fold_in(key_list[8], part), 71), part)
    couple_gain = jnp.clip(jnp.exp(math.log(1.5) - 1.60943787 * jax.random.uniform(part_splits[4], (2, NV), jnp.float32) ** block_scale(part_splits[4], (2, NV), ((0, 2),), -0.2, 0.2)), 0.3, 1.5)
    land_mask = plant((jax.random.randint(key_list[5], (NX,), 0, 4) < 3).astype(jnp.int32), jax.random.fold_in(key_list[5], 1), 0, 1)
    dest_tile_keys = jax.random.split(jax.random.fold_in(key_list[6], 1), 2 * NX // CX)
    dest_tile_turns = jax.random.permutation(jax.random.fold_in(key_list[6], 3), 2 * NX // CX)
    dest_tile = jax.vmap(lambda own, number: shared_out(jax.random.fold_in(key_list[6], 2), own, number, CX, N_TILE, 1, CAP, 2))(dest_tile_keys, dest_tile_turns).reshape((2, NX, 1))
    dest_block = plant(jax.random.randint(key_list[7], (2, NX), 0, CX), jax.random.fold_in(key_list[7], 1), 0, CX - 1).astype(jnp.int32)
    return {"prognostic_state": prognostic_state, "remapping_weight": remapping_weight, "diffusion": diffusion, "column_op": column_op, "couple_gain": couple_gain, "land_mask": land_mask, "dest_tile": dest_tile, "dest_block": dest_block}


def contribution(prognostic_state, remapping_weight, component_kind):
    surface_layer = prognostic_state[component_kind, :NV].astype(jnp.bfloat16)
    remap_contribution = jnp.einsum('mop,ops->oms', surface_layer.astype(jnp.float32), remapping_weight[component_kind].astype(jnp.float32))
    return remap_contribution.astype(jnp.bfloat16)


def reference(prognostic_state, remapping_weight, diffusion, column_op, couple_gain, land_mask, dest_tile, dest_block):
    results = []
    for component_kind in range(2):
        source = 1 - component_kind
        remap_contribution = contribution(prognostic_state, remapping_weight, source)
        target_row = (dest_tile[source, :, 0] * CX + dest_block[source]).astype(jnp.int32)
        summed = jax.ops.segment_sum(remap_contribution.astype(jnp.float32), target_row, num_segments=NX)
        surface_forcing = jnp.transpose(summed, (1, 0, 2))
        if component_kind == 0:
            active = jnp.ones((NX,), jnp.float32)
        else:
            active = land_mask.astype(jnp.float32)
        field = prognostic_state[component_kind]
        for substep in range(SUB):
            row_before = jnp.roll(field, 1, axis=1)
            row_after = jnp.roll(field, -1, axis=1)
            cell_before = jnp.pad(field, ((0, 0), (0, 0), (1, 0)))[:, :, :-1]
            cell_after = jnp.pad(field, ((0, 0), (0, 0), (0, 1)))[:, :, 1:]
            laplace = (row_before + row_after + cell_before + cell_after) - 4.0 * field
            stepped = field + active[None, :, None] * diffusion[component_kind][:, None, None] * laplace
            field = jnp.dot(column_op[component_kind], stepped.reshape(P_SIZE, -1), precision=lax.Precision.HIGHEST).reshape(stepped.shape)
        field = field.at[:NV].add(couple_gain[component_kind][:, None, None] * surface_forcing)
        results.append(field)
    return jnp.stack(results)
```

```python
import functools

import jax
import jax.numpy as jnp
from jax import lax
from jax.experimental import pallas as pl
from jax.experimental.pallas import tpu as pltpu
from jax.sharding import PartitionSpec as P

SUB = 3
CHUNK = 8
VMEM_LIMIT = 56 * 1024 * 1024


def send_kernel(
    cap,
    tiles,
    pos_ref,
    dest_ref,
    land_ref,
    state_ref,
    weight_ref,
    out_ref,
    head_ref,
    tail_ref,
    surface,
    weights,
    first,
    last,
    slot_ref,
    count_ref,
    sems,
):
    rows, fields = surface.shape[0] // out_ref.shape[1], out_ref.shape[1]
    depth = first.shape[0] // CHUNK
    chunks = rows // CHUNK
    comp, tile = pos_ref[0], pos_ref[1]
    get_surface = pltpu.make_async_copy(
        state_ref.at[pl.ds(0, fields)], surface.reshape(fields, rows, 128), sems.at[0]
    )
    get_surface.start()
    get_weight = [
        pltpu.make_async_copy(
            weight_ref.at[pl.ds(i * CHUNK, CHUNK)], weights.at[pl.ds(i * CHUNK, CHUNK)], sems.at[3 + i]
        )
        for i in range(chunks)
    ]
    for copy in get_weight:
        copy.start()
    get_first = pltpu.make_async_copy(
        state_ref.at[:, pl.ds(0, CHUNK)], first.reshape(depth, CHUNK, 128), sems.at[1]
    )
    get_last = pltpu.make_async_copy(
        state_ref.at[:, pl.ds(rows - CHUNK, CHUNK)], last.reshape(depth, CHUNK, 128), sems.at[2]
    )
    get_first.start()
    get_last.start()

    for t in range(tiles):
        count_ref[t] = 0

    def place(j, carry):
        d = dest_ref[comp * (tiles * rows) + tile * rows + j]
        n = count_ref[d]
        slot_ref[j] = d * cap + n
        count_ref[d] = n + 1
        return carry

    lax.fori_loop(0, rows, place, 0, unroll=8)

    get_surface.wait()
    for i in range(chunks):
        get_weight[i].wait()
        for j in range(i * CHUNK, (i + 1) * CHUNK):
            values = surface[pl.ds(j, fields, stride=rows), :].astype(jnp.bfloat16)
            block = jnp.dot(values, weights[j], preferred_element_type=jnp.float32)
            out_ref[slot_ref[j]] = block.astype(jnp.bfloat16)

    get_first.wait()
    get_last.wait()
    row_of = lax.broadcasted_iota(jnp.int32, (16, 128), 0)
    for source, target, base, offset in (
        (first, head_ref, 0, 0),
        (last, tail_ref, CHUNK - SUB, rows - SUB),
    ):
        flags = jnp.zeros((16, 128), jnp.float32)
        for r in range(SUB):
            target[pl.ds(r * depth, depth), :] = source[
                pl.ds(base + r, depth, stride=CHUNK), :
            ].astype(jnp.bfloat16)
            flag = jnp.where(comp == 1, land_ref[offset + r], 1).astype(jnp.float32)
            flags = jnp.where(row_of == r, flag, flags)
        target[pl.ds(SUB * depth, 16), :] = flags.astype(jnp.bfloat16)


def field_kernel(
    cap,
    tiles,
    pos_ref,
    dest_ref,
    block_ref,
    land_ref,
    state_ref,
    before_ref,
    after_ref,
    diffusion_ref,
    column_ref,
    out_ref,
    target_ref,
    natural,
    u0,
    u1,
    result,
    coef,
    left,
    flags,
    halves,
    in_sems,
    out_sems,
):
    depth, rows = coef.shape[2], natural.shape[0] // coef.shape[2]
    chunks = rows // CHUNK
    comp, tile = pos_ref[0], pos_ref[1]
    partner = 1 - comp
    loads = [
        pltpu.make_async_copy(
            state_ref.at[:, pl.ds(i * CHUNK, CHUNK)],
            natural.reshape(depth, rows, 128).at[:, pl.ds(i * CHUNK, CHUNK)],
            in_sems.at[i],
        )
        for i in range(chunks)
    ]
    for copy in loads:
        copy.start()

    def clear(i, carry):
        target_ref[i] = rows
        return carry

    lax.fori_loop(0, target_ref.shape[0], clear, 0, unroll=8)

    def scan_tile(s, carry):
        def scan(j, n):
            at = partner * (tiles * rows) + s * rows + j
            mine = dest_ref[at] == tile
            target_ref[s * cap + n] = jnp.where(mine, block_ref[at], rows)
            return n + mine.astype(jnp.int32)

        lax.fori_loop(0, rows, scan, 0, unroll=8)
        return carry

    lax.fori_loop(0, tiles, scan_tile, 0)

    rate = jnp.transpose(jnp.broadcast_to(diffusion_ref[...], (depth, depth)))
    coef[0, 0] = jnp.ones_like(rate)
    coef[0, 1] = jnp.zeros_like(rate)
    coef[1, 0] = 1.0 - 4.0 * rate
    coef[1, 1] = rate
    column = column_ref[...]
    high = column.astype(jnp.bfloat16)
    low = (column - high.astype(jnp.float32)).astype(jnp.bfloat16)
    left[:, 0:depth] = high
    left[:, depth : 2 * depth] = high
    left[:, 2 * depth : 3 * depth] = low

    def own_flag(i, carry):
        flags[i + SUB] = jnp.where(comp == 1, land_ref[i], 1)
        return carry

    lax.fori_loop(0, rows, own_flag, 0, unroll=8)
    for r in range(SUB):
        flags[r] = jnp.max(before_ref[pl.ds(SUB * depth, 16), :][r : r + 1, :].astype(jnp.float32)).astype(jnp.int32)
        flags[rows + SUB + r] = jnp.max(
            after_ref[pl.ds(SUB * depth, 16), :][r : r + 1, :].astype(jnp.float32)
        ).astype(jnp.int32)
        u0[r] = before_ref[pl.ds(r * depth, depth), :].astype(jnp.float32)
        u0[rows + SUB + r] = after_ref[pl.ds(r * depth, depth), :].astype(jnp.float32)
    for i in range(chunks):
        loads[i].wait()

        def relayout(k, carry, i=i):
            x = i * CHUNK + k
            u0[x + SUB] = natural[pl.ds(x, depth, stride=rows), :]
            return carry

        lax.fori_loop(0, CHUNK, relayout, 0, unroll=2)

    lane = lax.broadcasted_iota(jnp.int32, (16, 128), 1)
    not_first = lane > 0
    not_last = lane < 127

    def stencil(source, x, half, side):
        active = flags[x]
        for k in range(0, depth, 16):
            centre = source[x, pl.ds(k, 16), :]
            near = source[x - 1, pl.ds(k, 16), :] + source[x + 1, pl.ds(k, 16), :]
            near += jnp.where(not_first, pltpu.roll(centre, 1, 1), 0.0)
            near += jnp.where(not_last, pltpu.roll(centre, 127, 1), 0.0)
            stepped = coef[active, 0, pl.ds(k, 16), :] * centre + coef[active, 1, pl.ds(k, 16), :] * near
            high = stepped.astype(jnp.bfloat16)
            halves[half, pl.ds(k, 16), pl.ds(side * 128, 128)] = high
            halves[half, pl.ds(depth + k, 16), pl.ds(side * 128, 128)] = (
                stepped - high.astype(jnp.float32)
            ).astype(jnp.bfloat16)

    def column_product(half):
        both = jnp.dot(
            left[:, 0 : 2 * depth], halves[half], preferred_element_type=jnp.float32
        )
        return both + jnp.dot(
            left[:, 2 * depth : 3 * depth], halves[half, 0:depth, :], preferred_element_type=jnp.float32
        )

    def pair(source, x, half, store):
        stencil(source, x, half, 0)
        stencil(source, x + 1, half, 1)
        mixed = column_product(half)
        store(x, mixed[:, 0:128])
        store(x + 1, mixed[:, 128:256])

    def keep(target):
        def store(x, values):
            target[x] = values

        return store

    def finish(x, values):
        result[pl.ds(x - SUB, depth, stride=rows), :] = values

    source, target = u0, u1
    for substep in range(SUB - 1):
        start, pairs = substep + 1, (rows + 2 * SUB - 2 * (substep + 1)) // 2

        def body(i, carry, source=source, target=target, start=start):
            pair(source, start + 4 * i, 0, keep(target))
            pair(source, start + 4 * i + 2, 1, keep(target))
            return carry

        lax.fori_loop(0, pairs // 2, body, 0)
        if pairs % 2:
            pair(source, start + 2 * (pairs - 1), 0, keep(target))
        source, target = target, source

    stores = []
    for i in range(chunks):

        def body(k, carry, i=i):
            x = SUB + i * CHUNK + 4 * k
            pair(source, x, 0, finish)
            pair(source, x + 2, 1, finish)
            return carry

        lax.fori_loop(0, CHUNK // 4, body, 0)
        copy = pltpu.make_async_copy(
            result.reshape(depth, rows, 128).at[:, pl.ds(i * CHUNK, CHUNK)],
            out_ref.at[:, pl.ds(i * CHUNK, CHUNK)],
            out_sems.at[i],
        )
        copy.start()
        stores.append(copy)
    for copy in stores:
        copy.wait()


def forcing_kernel(target_ref, gain_ref, arrived_ref, field_ref, out_ref, total, field, sems):
    slots, fields, _ = arrived_ref.shape
    rows = field.shape[1]
    load = pltpu.make_async_copy(field_ref.at[pl.ds(0, fields)], field, sems.at[0])
    load.start()
    total[...] = jnp.zeros_like(total)

    def add(s, carry):
        at = pl.ds(pl.multiple_of(target_ref[s] * fields, fields), fields)
        total[at, :] += arrived_ref[s].astype(jnp.float32)
        return carry

    lax.fori_loop(0, slots, add, 0, unroll=8)
    load.wait()
    for f in range(fields):
        field[f] += gain_ref[f] * total[pl.ds(f, rows, stride=fields), :]
    store = pltpu.make_async_copy(field, out_ref.at[pl.ds(0, fields)], sems.at[1])
    store.start()
    store.wait()


def on_device(
    prognostic_state,
    remapping_weight,
    diffusion,
    column_op,
    couple_gain,
    land_mask,
    dest_tile,
    dest_block,
):
    comp_index = lax.axis_index("comp")
    tile_index = lax.axis_index("tile")
    tiles = lax.axis_size("tile")
    state = prognostic_state[0]
    depth, rows, cells = state.shape
    fields = couple_gain.shape[1]
    cap = max(2, 2 * rows // tiles)
    slots = tiles * cap
    chunks = rows // CHUNK
    halo_rows = SUB * depth + 16
    position = jnp.stack([comp_index, tile_index]).astype(jnp.int32)
    routes = dest_tile.reshape(-1)
    places = dest_block.reshape(-1)

    smem = pl.BlockSpec(memory_space=pltpu.SMEM)
    vmem = pl.BlockSpec(memory_space=pltpu.VMEM)
    anywhere = pl.BlockSpec(memory_space=pl.ANY)
    params = pltpu.CompilerParams(vmem_limit_bytes=VMEM_LIMIT)

    outgoing, head, tail = pl.pallas_call(
        functools.partial(send_kernel, cap, tiles),
        out_shape=(
            jax.ShapeDtypeStruct((slots, fields, cells), jnp.bfloat16),
            jax.ShapeDtypeStruct((halo_rows, cells), jnp.bfloat16),
            jax.ShapeDtypeStruct((halo_rows, cells), jnp.bfloat16),
        ),
        in_specs=[smem, smem, smem, anywhere, anywhere],
        out_specs=(vmem, vmem, vmem),
        scratch_shapes=[
            pltpu.VMEM((fields * rows, cells), jnp.float32),
            pltpu.VMEM((rows, cells, cells), jnp.bfloat16),
            pltpu.VMEM((depth * CHUNK, cells), jnp.float32),
            pltpu.VMEM((depth * CHUNK, cells), jnp.float32),
            pltpu.SMEM((rows,), jnp.int32),
            pltpu.SMEM((tiles,), jnp.int32),
            pltpu.SemaphoreType.DMA((3 + chunks,)),
        ],
        compiler_params=params,
        name="remap_and_pack",
    )(position, routes, land_mask, state, remapping_weight[0])

    ring = [(i, (i + 1) % tiles) for i in range(tiles)]
    before = lax.ppermute(tail, "tile", ring)
    after = lax.ppermute(head, "tile", [(b, a) for a, b in ring])
    arrived = lax.all_to_all(outgoing, "tile", split_axis=0, concat_axis=0, tiled=True)
    received = lax.ppermute(arrived, "comp", [(0, 1), (1, 0)])

    field, target = pl.pallas_call(
        functools.partial(field_kernel, cap, tiles),
        out_shape=(
            jax.ShapeDtypeStruct((depth, rows, cells), jnp.float32),
            jax.ShapeDtypeStruct((slots + 8,), jnp.int32),
        ),
        in_specs=[smem, smem, smem, smem, anywhere, vmem, vmem, vmem, vmem],
        out_specs=(anywhere, smem),
        scratch_shapes=[
            pltpu.VMEM((depth * rows, cells), jnp.float32),
            pltpu.VMEM((rows + 2 * SUB, depth, cells), jnp.float32),
            pltpu.VMEM((rows + 2 * SUB, depth, cells), jnp.float32),
            pltpu.VMEM((depth * rows, cells), jnp.float32),
            pltpu.VMEM((2, 2, depth, cells), jnp.float32),
            pltpu.VMEM((depth, 3 * depth), jnp.bfloat16),
            pltpu.SMEM((rows + 2 * SUB,), jnp.int32),
            pltpu.VMEM((2, 2 * depth, 2 * cells), jnp.bfloat16),
            pltpu.SemaphoreType.DMA((chunks,)),
            pltpu.SemaphoreType.DMA((chunks,)),
        ],
        compiler_params=params,
        cost_estimate=pl.CostEstimate(
            flops=18 * depth * depth * rows * cells,
            bytes_accessed=8 * depth * rows * cells,
            transcendentals=0,
        ),
        name="substeps",
    )(position, routes, places, land_mask, state, before, after, diffusion, column_op[0])

    new_state = pl.pallas_call(
        forcing_kernel,
        out_shape=jax.ShapeDtypeStruct((depth, rows, cells), jnp.float32),
        in_specs=[smem, smem, vmem, anywhere],
        out_specs=anywhere,
        input_output_aliases={3: 0},
        scratch_shapes=[
            pltpu.VMEM(((rows + 1) * fields, cells), jnp.float32),
            pltpu.VMEM((fields, rows, cells), jnp.float32),
            pltpu.SemaphoreType.DMA((2,)),
        ],
        compiler_params=params,
        name="add_forcing",
    )(target, couple_gain.reshape(-1), received, field)
    return new_state[None]


def solution(mesh):
    placed = (
        P("comp", "member", "tile", None),
        P("comp", "tile", None, None),
        P("comp", "member"),
        P("comp", "member", None),
        P("comp", "member"),
        P("tile"),
        P(),
        P(),
    )
    return jax.shard_map(
        on_device,
        mesh=mesh,
        in_specs=placed,
        out_specs=P("comp", "member", "tile", None),
        check_vma=False,
    )
```

```python
import functools

import jax
import jax.numpy as jnp
from jax import lax
from jax.experimental import pallas as pl
from jax.experimental.pallas import tpu as pltpu
from jax.sharding import PartitionSpec as P

SUB = 3
CHUNK = 8
GROUP = 8
EDGE = 8


def halo_kernel(cap, dest_ref, block_ref, land_ref, state_ref, head_ref, tail_ref, target_ref, slabs, sems):
    _, depth, cells = slabs.shape
    rows = state_ref.shape[1]
    comp, tile = lax.axis_index("comp"), lax.axis_index("tile")
    loads = []
    for r in range(2 * SUB):
        x = r if r < SUB else rows - 2 * SUB + r
        loads.append(pltpu.make_async_copy(state_ref.at[:, x, :], slabs.at[r], sems.at[r]))
        loads[-1].start()

    lines = dest_ref.shape[0] // 2
    dest = dest_ref[pl.ds((1 - comp) * lines, lines), :]
    both = [jnp.concatenate([block_ref[c : c + 1, pl.ds(e * 128, 128)] for e in range(lines)], axis=0) for c in range(2)]
    place = jnp.where(comp == 1, both[0], both[1])
    mine = dest == tile
    earlier = lax.broadcasted_iota(jnp.int32, (128, 128), 0)
    later = lax.broadcasted_iota(jnp.int32, (128, 128), 1)
    before = (earlier < later) & (lax.div(earlier, rows) == lax.div(later, rows))
    rank = jnp.dot(
        mine.astype(jnp.float32).astype(jnp.bfloat16),
        before.astype(jnp.float32).astype(jnp.bfloat16),
        preferred_element_type=jnp.float32,
    )
    lane = lax.broadcasted_iota(jnp.int32, (lines, 128), 1)
    offset = (place - rows).astype(jnp.float32)
    target = jnp.zeros((lines, 128), jnp.float32)
    for h in range(128 // rows):
        here = mine & (lax.div(lane, rows) == h)
        for r in range(cap):
            found = jnp.sum(jnp.where(here & (rank == r), offset, 0.0), axis=1, keepdims=True)
            target = jnp.where(lane == h * cap + r, found, target)
    target_ref[...] = target.astype(jnp.int32) + rows

    row_of = lax.broadcasted_iota(jnp.int32, (16, 128), 0)
    for out_ref, base, offset in ((head_ref, 0, 0), (tail_ref, SUB, rows - SUB)):
        flags = jnp.zeros((16, 128), jnp.float32)
        for r in range(SUB):
            flag = jnp.where(comp == 1, land_ref[offset + r], 1).astype(jnp.float32)
            flags = jnp.where(row_of == r, flag, flags)
        out_ref[pl.ds(SUB * depth, 16), :] = flags.astype(jnp.bfloat16)
        for r in range(SUB):
            loads[base + r].wait()
            out_ref[pl.ds(r * depth, depth), :] = slabs[base + r].astype(jnp.bfloat16)


def send_kernel(cap, tiles, dest_ref, state_ref, weight_ref, out_ref, surface, weights, slot_ref, count_ref, sems):
    fields, rows = out_ref.shape[1], weights.shape[0]
    chunks = rows // CHUNK
    comp, tile = lax.axis_index("comp"), lax.axis_index("tile")
    get_surface = pltpu.make_async_copy(
        state_ref.at[pl.ds(0, fields)], surface.reshape(fields, rows, 128), sems.at[0]
    )
    get_surface.start()
    get_weight = [
        pltpu.make_async_copy(
            weight_ref.at[pl.ds(i * CHUNK, CHUNK)], weights.at[pl.ds(i * CHUNK, CHUNK)], sems.at[1 + i]
        )
        for i in range(chunks)
    ]
    for copy in get_weight:
        copy.start()

    for t in range(tiles):
        count_ref[t] = 0

    def place(j, carry):
        d = dest_ref[comp * (tiles * rows) + tile * rows + j]
        n = count_ref[d]
        slot_ref[j] = d * cap + n
        count_ref[d] = n + 1
        return carry

    lax.fori_loop(0, rows, place, 0, unroll=8)

    get_surface.wait()
    for i in range(chunks):
        get_weight[i].wait()
        for j in range(i * CHUNK, (i + 1) * CHUNK):
            values = surface[pl.ds(j, fields, stride=rows), :].astype(jnp.bfloat16)
            block = jnp.dot(values, weights[j], preferred_element_type=jnp.float32)
            out_ref[slot_ref[j]] = block.astype(jnp.bfloat16)


def field_kernel(land_ref, state_ref, before_ref, after_ref, diffusion_ref, column_ref,
    out_ref, top_ref, slabs, u0, u1, coef, right, flags, half0, half1, in_sems, out_sems):
    depth, rows, cells = state_ref.shape
    groups = rows // GROUP
    comp, fields = lax.axis_index("comp"), top_ref.shape[1]
    inside = pl.ds(EDGE, cells)
    below = pl.ds(fields, depth - fields)

    def load(x, carry):
        pltpu.make_async_copy(state_ref.at[:, x, :], slabs.at[x], in_sems.at[x // GROUP]).start()
        return carry
    lax.fori_loop(0, rows, load, 0, unroll=8)

    rate = diffusion_ref[...]
    coef[0, 0] = jnp.ones_like(coef[0, 0])
    coef[0, 1] = jnp.zeros_like(coef[0, 0])
    coef[1, 0] = jnp.broadcast_to(1.0 - 4.0 * rate, (16, depth))
    coef[1, 1] = jnp.broadcast_to(rate, (16, depth))
    column = jnp.transpose(column_ref[...])
    high = column.astype(jnp.bfloat16)
    low = (column - high.astype(jnp.float32)).astype(jnp.bfloat16)
    right[0:depth, 0:depth] = high
    right[depth : 2 * depth, 0:depth] = high
    right[0:depth, depth : 2 * depth] = low
    right[depth : 2 * depth, depth : 2 * depth] = jnp.zeros_like(low)

    def own_flag(i, carry):
        flags[i + SUB] = jnp.where(comp == 1, land_ref[i], 1)
        return carry
    lax.fori_loop(0, rows, own_flag, 0, unroll=8)
    for r in range(SUB):
        flags[r] = jnp.max(before_ref[pl.ds(SUB * depth, 16), :][r : r + 1, :].astype(jnp.float32)).astype(jnp.int32)
        flags[rows + SUB + r] = jnp.max(
            after_ref[pl.ds(SUB * depth, 16), :][r : r + 1, :].astype(jnp.float32)
        ).astype(jnp.int32)
        u0[r, inside, :] = jnp.transpose(before_ref[pl.ds(r * depth, depth), :].astype(jnp.float32))
        u0[rows + SUB + r, inside, :] = jnp.transpose(after_ref[pl.ds(r * depth, depth), :].astype(jnp.float32))
    for r in range(rows + 2 * SUB, flags.shape[0]):
        flags[r] = 0
    def border(x, carry):
        zeros = jnp.zeros((EDGE, depth), jnp.float32)
        for u in (u0, u1):
            u[x, pl.ds(0, EDGE), :] = zeros
            u[x, pl.ds(EDGE + cells, EDGE), :] = zeros
        return carry
    lax.fori_loop(0, u0.shape[0], border, 0, unroll=2)

    def wait_in(g):
        pltpu.make_async_copy(
            slabs.at[pl.ds(g * GROUP, GROUP)], slabs.at[pl.ds(g * GROUP, GROUP)], in_sems.at[g]
        ).wait()

    def turn(s):
        u0[s + SUB, inside, :] = jnp.transpose(slabs[s])

    def stencil(source, x, half):
        for side in range(GROUP):
            active = flags[x + side]
            keep, spread = coef[active, 0], coef[active, 1]
            for k in range(0, cells, 16):
                at = pl.ds(EDGE + k, 16)
                near = source[x + side - 1, at, :] + source[x + side + 1, at, :]
                near += source[x + side, pl.ds(EDGE + k - 1, 16), :] + source[x + side, pl.ds(EDGE + k + 1, 16), :]
                stepped = keep * source[x + side, at, :] + spread * near
                high = stepped.astype(jnp.bfloat16)
                half[pl.ds(side * cells + k, 16), 0:depth] = high
                half[pl.ds(side * cells + k, 16), depth : 2 * depth] = (
                    stepped - high.astype(jnp.float32)
                ).astype(jnp.bfloat16)

    def product(half, count, store):
        mixed = jnp.dot(half[0 : count * cells], right[...], preferred_element_type=jnp.float32)
        mixed = mixed[:, 0:depth] + mixed[:, depth : 2 * depth]
        for side in range(count):
            store(side, mixed[side * cells : (side + 1) * cells])

    def keep_in(target, x):
        def store(side, values):
            target[x + side, inside, :] = values
        return store

    def finish(x):
        def store(side, values):
            turned = jnp.transpose(values)
            top_ref[x + side] = turned[0:fields]
            slabs[x + side] = turned
        return store

    def send_out(x):
        for side in range(GROUP):
            pltpu.make_async_copy(
                slabs.at[x + side, below, :], out_ref.at[below, x + side, :], out_sems.at[lax.div(x, GROUP)]
            ).start()

    wait_in(0)
    wait_in(1)
    for s in range(2 * GROUP - 1):
        turn(s)
    span = 2 * GROUP
    bodies = rows // span

    stencil(u0, 1, half0)
    def body1(i, carry):
        x = 1 + span * i
        @pl.when(2 * i + 3 < groups)
        def _():
            wait_in(2 * i + 2)
            wait_in(2 * i + 3)
        product(half0, GROUP, keep_in(u1, x))
        stencil(u0, x + GROUP, half1)
        for s in range(GROUP):
            turn(jnp.minimum(span * i + span - 1 + s, rows - 1))
        product(half1, GROUP, keep_in(u1, x + GROUP))
        stencil(u0, x + span, half0)
        for s in range(GROUP, span):
            turn(jnp.minimum(span * i + span - 1 + s, rows - 1))
        return carry
    lax.fori_loop(0, bodies, body1, 0)
    product(half0, 4, keep_in(u1, rows + 1))

    stencil(u1, 2, half0)
    def body2(i, carry):
        x = 2 + span * i
        product(half0, GROUP, keep_in(u0, x))
        stencil(u1, x + GROUP, half1)
        product(half1, GROUP, keep_in(u0, x + GROUP))
        stencil(u1, x + span, half0)
        return carry
    lax.fori_loop(0, bodies, body2, 0)
    product(half0, 2, keep_in(u0, rows + 2))

    stencil(u0, SUB, half0)
    def body3(i, carry):
        x = span * i
        product(half0, GROUP, finish(x))
        stencil(u0, SUB + x + GROUP, half1)
        send_out(x)
        product(half1, GROUP, finish(x + GROUP))
        stencil(u0, SUB + x + span, half0)
        send_out(x + GROUP)
        return carry
    lax.fori_loop(0, bodies, body3, 0)

    def wait_out(i, carry):
        part = slabs.at[pl.ds(0, GROUP), below, :]
        pltpu.make_async_copy(part, part, out_sems.at[i]).wait()
        return carry
    lax.fori_loop(0, groups, wait_out, 0)


def forcing_kernel(target_ref, gain_ref, arrived_ref, top_ref, field_ref, out_ref, total, top, result, sems):
    slots, fields, _ = arrived_ref.shape
    rows, _, cells = top_ref.shape
    load = pltpu.make_async_copy(top_ref, top.reshape(rows, fields, cells), sems.at[0])
    load.start()
    total[...] = jnp.zeros_like(total)

    lines = target_ref.shape[0]
    count = slots // lines

    def add(e, carry):
        for s in range(count):
            at = pl.ds(pl.multiple_of(target_ref[e, s] * fields, fields), fields)
            total[at, :] += arrived_ref[e * count + s].astype(jnp.float32)
        return carry

    lax.fori_loop(0, lines, add, 0)
    load.wait()
    for f in range(fields):
        at = pl.ds(f, rows, stride=fields)
        result[f] = top[at, :] + gain_ref[f] * total[at, :]
    store = pltpu.make_async_copy(result, out_ref.at[pl.ds(0, fields)], sems.at[1])
    store.start()
    store.wait()


def on_device(
    prognostic_state,
    remapping_weight,
    diffusion,
    column_op,
    couple_gain,
    land_mask,
    dest_tile,
    dest_block,
):
    tiles = lax.axis_size("tile")
    state = prognostic_state[0]
    depth, rows, cells = state.shape
    fields = couple_gain.shape[1]
    cap = max(2, 2 * rows // tiles)
    slots = tiles * cap
    chunks = rows // CHUNK
    halo_rows = SUB * depth + 16
    routes = dest_tile.reshape(-1)
    lines = tiles * rows // 128

    smem = pl.BlockSpec(memory_space=pltpu.SMEM)
    vmem = pl.BlockSpec(memory_space=pltpu.VMEM)
    anywhere = pl.BlockSpec(memory_space=pltpu.HBM)

    head, tail, target = pl.pallas_call(
        functools.partial(halo_kernel, cap),
        out_shape=(
            jax.ShapeDtypeStruct((halo_rows, cells), jnp.bfloat16),
            jax.ShapeDtypeStruct((halo_rows, cells), jnp.bfloat16),
            jax.ShapeDtypeStruct((lines, 128), jnp.int32),
        ),
        in_specs=[vmem, vmem, smem, anywhere],
        out_specs=(vmem, vmem, vmem),
        scratch_shapes=[pltpu.VMEM((2 * SUB, depth, cells), jnp.float32), pltpu.SemaphoreType.DMA((2 * SUB,))],
        compiler_params=pltpu.CompilerParams(vmem_limit_bytes=60 << 20),
        name="boundary_rows",
    )(routes.reshape(2 * lines, 128), dest_block, land_mask, state)

    ring = [(i, (i + 1) % tiles) for i in range(tiles)]
    before = lax.ppermute(tail, "tile", ring)
    after = lax.ppermute(head, "tile", [(b, a) for a, b in ring])

    routes, target = lax.optimization_barrier((routes, target))
    outgoing = pl.pallas_call(
        functools.partial(send_kernel, cap, tiles),
        out_shape=jax.ShapeDtypeStruct((slots, fields, cells), jnp.bfloat16),
        in_specs=[smem, anywhere, anywhere],
        out_specs=vmem,
        scratch_shapes=[
            pltpu.VMEM((fields * rows, cells), jnp.float32),
            pltpu.VMEM((rows, cells, cells), jnp.bfloat16),
            pltpu.SMEM((rows,), jnp.int32),
            pltpu.SMEM((tiles,), jnp.int32),
            pltpu.SemaphoreType.DMA((1 + chunks,)),
        ],
        compiler_params=pltpu.CompilerParams(vmem_limit_bytes=60 << 20),
        cost_estimate=pl.CostEstimate(
            flops=2 * rows * fields * cells * cells, bytes_accessed=8 << 20, transcendentals=0
        ),
        name="remap_and_pack",
    )(routes, state, remapping_weight[0])
    before, after, outgoing = lax.optimization_barrier((before, after, outgoing))

    swapped = lax.ppermute(outgoing, "comp", [(0, 1), (1, 0)])
    before, after, swapped = lax.optimization_barrier((before, after, swapped))
    arrived = lax.all_to_all(swapped, "tile", split_axis=0, concat_axis=0, tiled=True)

    total_rows = rows + 2 * SUB + GROUP
    field, top = pl.pallas_call(
        field_kernel,
        out_shape=(
            jax.ShapeDtypeStruct((depth, rows, cells), jnp.float32),
            jax.ShapeDtypeStruct((rows, fields, cells), jnp.float32),
        ),
        in_specs=[smem, anywhere, vmem, vmem, vmem, vmem],
        out_specs=(anywhere, vmem),
        scratch_shapes=[
            pltpu.VMEM((rows, depth, cells), jnp.float32),
            pltpu.VMEM((total_rows, cells + 2 * EDGE, depth), jnp.float32),
            pltpu.VMEM((total_rows, cells + 2 * EDGE, depth), jnp.float32),
            pltpu.VMEM((2, 2, 16, depth), jnp.float32),
            pltpu.VMEM((2 * depth, 2 * depth), jnp.bfloat16),
            pltpu.SMEM((total_rows,), jnp.int32),
            pltpu.VMEM((GROUP * cells, 2 * depth), jnp.bfloat16),
            pltpu.VMEM((GROUP * cells, 2 * depth), jnp.bfloat16),
            pltpu.SemaphoreType.DMA((rows // GROUP,)),
            pltpu.SemaphoreType.DMA((rows // GROUP,)),
        ],
        compiler_params=pltpu.CompilerParams(vmem_limit_bytes=61 << 20),
        cost_estimate=pl.CostEstimate(
            flops=18 * depth * depth * rows * cells,
            bytes_accessed=8 * depth * rows * cells,
            transcendentals=0,
        ),
        name="substeps",
    )(land_mask, state, before, after, diffusion, column_op[0])

    new_state = pl.pallas_call(
        forcing_kernel,
        out_shape=jax.ShapeDtypeStruct((depth, rows, cells), jnp.float32),
        in_specs=[smem, smem, vmem, anywhere, anywhere],
        out_specs=anywhere,
        input_output_aliases={4: 0},
        scratch_shapes=[
            pltpu.VMEM(((rows + 1) * fields, cells), jnp.float32),
            pltpu.VMEM((rows * fields, cells), jnp.float32),
            pltpu.VMEM((fields, rows, cells), jnp.float32),
            pltpu.SemaphoreType.DMA((2,)),
        ],
        compiler_params=pltpu.CompilerParams(vmem_limit_bytes=16 << 20),
        name="add_forcing",
    )(target, couple_gain.reshape(-1), arrived, top, field)
    return new_state[None]


def solution(mesh):
    placed = (
        P("comp", "member", "tile", None),
        P("comp", "tile", None, None),
        P("comp", "member"),
        P("comp", "member", None),
        P("comp", "member"),
        P("tile"),
        P(),
        P(),
    )
    return jax.shard_map(
        on_device,
        mesh=mesh,
        in_specs=placed,
        out_specs=P("comp", "member", "tile", None),
        check_vma=False,
    )
```

```python
import functools

import jax
import jax.numpy as jnp
from jax import lax
from jax.experimental import pallas as pl
from jax.experimental.pallas import tpu as pltpu
from jax.sharding import PartitionSpec as P

SUB = 3
CHUNK = 8
GROUP = 8
EDGE = 8


def copies(pairs, sems, first):
    started = [pltpu.make_async_copy(a, b, sems.at[first + i]) for i, (a, b) in enumerate(pairs)]
    for copy in started:
        copy.start()
    return started


def halo_kernel(
    cap, dest_hbm, block_hbm, land_hbm, state_ref, head_ref, tail_ref, target_ref, surface_ref, dest_ref, block_ref, land_ref, slabs, sems
):
    _, depth, cells = slabs.shape
    rows = state_ref.shape[1]
    comp, tile = lax.axis_index("comp"), lax.axis_index("tile")
    tables = copies(((dest_hbm, dest_ref), (block_hbm, block_ref), (land_hbm, land_ref)), sems, 0)
    ends = [*range(SUB), *range(rows - SUB, rows)]
    loads = copies([(state_ref.at[:, x, :], slabs.at[r]) for r, x in enumerate(ends)], sems, 3)
    (surface,) = copies([(state_ref.at[pl.ds(0, surface_ref.shape[0])], surface_ref)], sems, 3 + 2 * SUB)
    for copy in tables:
        copy.wait()

    lines = dest_ref.shape[0] // 2
    dest = dest_ref[pl.ds((1 - comp) * lines, lines), :]
    both = [jnp.concatenate([block_ref[c : c + 1, pl.ds(e * 128, 128)] for e in range(lines)], axis=0) for c in range(2)]
    place = jnp.where(comp == 1, both[0], both[1])
    mine = dest == tile
    earlier = lax.broadcasted_iota(jnp.int32, (128, 128), 0)
    later = lax.broadcasted_iota(jnp.int32, (128, 128), 1)
    before = (earlier < later) & (lax.div(earlier, rows) == lax.div(later, rows))
    rank = jnp.dot(
        mine.astype(jnp.float32).astype(jnp.bfloat16),
        before.astype(jnp.float32).astype(jnp.bfloat16),
        preferred_element_type=jnp.float32,
    )
    lane = lax.broadcasted_iota(jnp.int32, (lines, 128), 1)
    offset = (place - rows).astype(jnp.float32)
    target = jnp.zeros((lines, 128), jnp.float32)
    for h in range(128 // rows):
        here = mine & (lax.div(lane, rows) == h)
        for r in range(cap):
            found = jnp.sum(jnp.where(here & (rank == r), offset, 0.0), axis=1, keepdims=True)
            target = jnp.where(lane == h * cap + r, found, target)
    target_ref[...] = target.astype(jnp.int32) + rows

    row_of = lax.broadcasted_iota(jnp.int32, (16, 128), 0)
    for out_ref, base, offset in ((head_ref, 0, 0), (tail_ref, SUB, rows - SUB)):
        flags = jnp.zeros((16, 128), jnp.float32)
        for r in range(SUB):
            flag = jnp.where(comp == 1, land_ref[offset + r], 1).astype(jnp.float32)
            flags = jnp.where(row_of == r, flag, flags)
        out_ref[pl.ds(SUB * depth, 16), :] = flags.astype(jnp.bfloat16)
        for r in range(SUB):
            loads[base + r].wait()
            out_ref[pl.ds(r * depth, depth), :] = slabs[base + r].astype(jnp.bfloat16)
    surface.wait()


def send_kernel(cap, tiles, dest_hbm, surface_ref, weight_ref, out_ref, dest_ref, surface, weights, blocks, count_ref, sems):
    fields, rows = out_ref.shape[1], weights.shape[0]
    chunks = rows // CHUNK
    comp, tile = lax.axis_index("comp"), lax.axis_index("tile")
    parts = [pl.ds(i * CHUNK, CHUNK) for i in range(chunks)]
    get_dest, get_surface, *_ = copies(
        [(dest_hbm, dest_ref), (surface_ref, surface.reshape(fields, rows, 128))]
        + [(weight_ref.at[part], weights.at[part]) for part in parts],
        sems,
        0,
    )

    get_surface.wait()

    def remap(i, carry):
        pltpu.make_async_copy(weight_ref.at[parts[0]], weights.at[parts[0]], sems.at[2 + i]).wait()
        for k in range(CHUNK):
            j = i * CHUNK + k
            values = surface[pl.ds(j, fields, stride=rows), :].astype(jnp.bfloat16)
            block = jnp.dot(values, weights[j], preferred_element_type=jnp.float32)
            blocks[j] = block.astype(jnp.bfloat16)
        return carry

    lax.fori_loop(0, chunks, remap, 0)

    for t in range(tiles):
        count_ref[t] = 0
    get_dest.wait()

    def place(j, carry):
        d = dest_ref[(1 - comp) * (tiles * rows) + tile * rows + j]
        n = count_ref[d]
        out_ref[d * cap + n] = blocks[j]
        count_ref[d] = n + 1
        return carry

    lax.fori_loop(0, rows, place, 0, unroll=8)


def field_kernel(
    land_hbm,
    state_ref,
    before_hbm,
    after_hbm,
    diffusion_hbm,
    column_hbm,
    out_ref,
    top_ref,
    land_ref,
    before_ref,
    after_ref,
    diffusion_ref,
    column_ref,
    slabs,
    u0,
    u1,
    coef,
    right,
    flags,
    half0,
    half1,
    small_sems,
    in_sems,
    out_sems,
):
    depth, rows, cells = state_ref.shape
    groups = rows // GROUP
    comp, fields = lax.axis_index("comp"), top_ref.shape[1]
    inside = pl.ds(EDGE, cells)
    below = pl.ds(fields, depth - fields)

    def load(x, carry):
        pltpu.make_async_copy(state_ref.at[:, x, :], slabs.at[x], in_sems.at[lax.div(x, GROUP)]).start()
        return carry

    small = copies(
        (
            (diffusion_hbm, diffusion_ref),
            (column_hbm, column_ref),
            (land_hbm, land_ref),
            (before_hbm, before_ref),
            (after_hbm, after_ref),
        ),
        small_sems,
        0,
    )
    lax.fori_loop(0, rows, load, 0, unroll=4)

    def border(x, carry):
        zeros = jnp.zeros((EDGE, depth), jnp.float32)
        for u in (u0, u1):
            u[x, pl.ds(0, EDGE), :] = zeros
            u[x, pl.ds(EDGE + cells, EDGE), :] = zeros
        return carry
    lax.fori_loop(0, u0.shape[0], border, 0, unroll=2)
    for copy in small:
        copy.wait()

    rate = diffusion_ref[...]
    coef[0, 0] = jnp.ones_like(coef[0, 0])
    coef[0, 1] = jnp.zeros_like(coef[0, 0])
    coef[1, 0] = jnp.broadcast_to(1.0 - 4.0 * rate, (16, depth))
    coef[1, 1] = jnp.broadcast_to(rate, (16, depth))
    column = jnp.transpose(column_ref[...])
    high = column.astype(jnp.bfloat16)
    low = (column - high.astype(jnp.float32)).astype(jnp.bfloat16)
    right[0:depth, 0:depth] = high
    right[depth : 2 * depth, 0:depth] = high
    right[0:depth, depth : 2 * depth] = low
    right[depth : 2 * depth, depth : 2 * depth] = jnp.zeros_like(low)

    def own_flag(i, carry):
        flags[i + SUB] = jnp.where(comp == 1, land_ref[i], 1)
        return carry
    lax.fori_loop(0, rows, own_flag, 0, unroll=8)
    for r in range(SUB):
        flags[r] = jnp.max(before_ref[pl.ds(SUB * depth, 16), :][r : r + 1, :].astype(jnp.float32)).astype(jnp.int32)
        flags[rows + SUB + r] = jnp.max(
            after_ref[pl.ds(SUB * depth, 16), :][r : r + 1, :].astype(jnp.float32)
        ).astype(jnp.int32)
        u0[r, inside, :] = jnp.transpose(before_ref[pl.ds(r * depth, depth), :].astype(jnp.float32))
        u0[rows + SUB + r, inside, :] = jnp.transpose(after_ref[pl.ds(r * depth, depth), :].astype(jnp.float32))
    for r in range(rows + 2 * SUB, flags.shape[0]):
        flags[r] = 0

    def wait_in(g):
        pltpu.make_async_copy(
            slabs.at[pl.ds(g * GROUP, GROUP)], slabs.at[pl.ds(g * GROUP, GROUP)], in_sems.at[g]
        ).wait()

    def turn(s):
        u0[s + SUB, inside, :] = jnp.transpose(slabs[s])

    def stencil(source, x, half):
        for side in range(GROUP):
            active = flags[x + side]
            keep, spread = coef[active, 0], coef[active, 1]
            for k in range(0, cells, 16):
                at = pl.ds(EDGE + k, 16)
                near = source[x + side - 1, at, :] + source[x + side + 1, at, :]
                near += source[x + side, pl.ds(EDGE + k - 1, 16), :] + source[x + side, pl.ds(EDGE + k + 1, 16), :]
                stepped = keep * source[x + side, at, :] + spread * near
                high = stepped.astype(jnp.bfloat16)
                half[pl.ds(side * cells + k, 16), 0:depth] = high
                half[pl.ds(side * cells + k, 16), depth : 2 * depth] = (
                    stepped - high.astype(jnp.float32)
                ).astype(jnp.bfloat16)

    def product(half, count, store):
        mixed = jnp.dot(half[0 : count * cells], right[...], preferred_element_type=jnp.float32)
        mixed = mixed[:, 0:depth] + mixed[:, depth : 2 * depth]
        for side in range(count):
            store(side, mixed[side * cells : (side + 1) * cells])

    def keep_in(target, x):
        def store(side, values):
            target[x + side, inside, :] = values
        return store

    def finish(x):
        def store(side, values):
            turned = jnp.transpose(values)
            top_ref[x + side] = turned[0:fields]
            slabs[x + side] = turned
        return store

    def send_out(x):
        for side in range(GROUP):
            pltpu.make_async_copy(
                slabs.at[x + side, below, :], out_ref.at[below, x + side, :], out_sems.at[lax.div(x, GROUP)]
            ).start()

    wait_in(0)
    wait_in(1)
    for s in range(2 * GROUP - 1):
        turn(s)
    span = 2 * GROUP
    bodies = rows // span

    stencil(u0, 1, half0)
    def body1(i, carry):
        x = 1 + span * i
        @pl.when(2 * i + 3 < groups)
        def _():
            wait_in(2 * i + 2)
            wait_in(2 * i + 3)
        product(half0, GROUP, keep_in(u1, x))
        stencil(u0, x + GROUP, half1)
        for s in range(GROUP):
            turn(jnp.minimum(span * i + span - 1 + s, rows - 1))
        product(half1, GROUP, keep_in(u1, x + GROUP))
        stencil(u0, x + span, half0)
        for s in range(GROUP, span):
            turn(jnp.minimum(span * i + span - 1 + s, rows - 1))
        return carry
    lax.fori_loop(0, bodies, body1, 0)
    product(half0, 4, keep_in(u1, rows + 1))

    stencil(u1, 2, half0)
    def body2(i, carry):
        x = 2 + span * i
        product(half0, GROUP, keep_in(u0, x))
        stencil(u1, x + GROUP, half1)
        product(half1, GROUP, keep_in(u0, x + GROUP))
        stencil(u1, x + span, half0)
        return carry
    lax.fori_loop(0, bodies, body2, 0)
    product(half0, 2, keep_in(u0, rows + 2))

    stencil(u0, SUB, half0)
    def body3(i, carry):
        x = span * i
        product(half0, GROUP, finish(x))
        stencil(u0, SUB + x + GROUP, half1)
        send_out(x)
        product(half1, GROUP, finish(x + GROUP))
        stencil(u0, SUB + x + span, half0)
        send_out(x + GROUP)
        return carry
    lax.fori_loop(0, bodies, body3, 0)

    def wait_out(i, carry):
        part = slabs.at[pl.ds(0, GROUP), below, :]
        pltpu.make_async_copy(part, part, out_sems.at[i]).wait()
        return carry
    lax.fori_loop(0, groups, wait_out, 0)


def forcing_kernel(target_hbm, gain_hbm, arrived_ref, top_ref, field_ref, out_ref, target_ref, gain_ref, total, top, result, sems):
    slots, fields, _ = arrived_ref.shape
    rows, _, cells = top_ref.shape
    get_target, get_gain, get_top = copies(
        ((target_hbm, target_ref), (gain_hbm, gain_ref), (top_ref, top.reshape(rows, fields, cells))), sems, 0
    )

    def clear(x, carry):
        total[pl.ds(pl.multiple_of(x * fields, fields), fields), :] = jnp.zeros((fields, cells), jnp.float32)
        return carry

    lax.fori_loop(0, rows, clear, 0, unroll=4)
    get_target.wait()

    lines = target_ref.shape[0]
    count = slots // lines

    def add(e, carry):
        for s in range(count):
            at = pl.ds(pl.multiple_of(target_ref[e, s] * fields, fields), fields)
            total[at, :] += arrived_ref[e * count + s].astype(jnp.float32)
        return carry

    lax.fori_loop(0, lines, add, 0)
    get_gain.wait()
    get_top.wait()

    def combine(f, carry):
        at = pl.ds(f, rows, stride=fields)
        result[f] = top[at, :] + gain_ref[f] * total[at, :]
        return carry

    lax.fori_loop(0, fields, combine, 0, unroll=2)
    store = pltpu.make_async_copy(result, out_ref.at[pl.ds(0, fields)], sems.at[3])
    store.start()
    store.wait()


def on_device(
    prognostic_state,
    remapping_weight,
    diffusion,
    column_op,
    couple_gain,
    land_mask,
    dest_tile,
    dest_block,
):
    tiles = lax.axis_size("tile")
    in_hbm = functools.partial(pltpu.with_memory_space_constraint, memory_space=pltpu.HBM)
    state = in_hbm(prognostic_state[0])
    depth, rows, cells = state.shape
    fields = couple_gain.shape[1]
    cap = max(2, 2 * rows // tiles)
    slots = tiles * cap
    chunks = rows // CHUNK
    halo_rows = SUB * depth + 16
    routes = in_hbm(dest_tile.reshape(-1))
    lines = tiles * rows // 128

    vmem = pl.BlockSpec(memory_space=pltpu.VMEM)
    anywhere = pl.BlockSpec(memory_space=pltpu.HBM)

    partner = [(0, 1), (1, 0)]
    weight = lax.ppermute(remapping_weight[0], "comp", partner)

    head, tail, target, surface = pl.pallas_call(
        functools.partial(halo_kernel, cap),
        out_shape=(
            jax.ShapeDtypeStruct((halo_rows, cells), jnp.bfloat16),
            jax.ShapeDtypeStruct((halo_rows, cells), jnp.bfloat16),
            jax.ShapeDtypeStruct((lines, 128), jnp.int32),
            jax.ShapeDtypeStruct((fields, rows, cells), jnp.float32),
        ),
        in_specs=[anywhere] * 4,
        out_specs=(vmem, vmem, vmem, vmem),
        scratch_shapes=[
            pltpu.VMEM((2 * lines, 128), jnp.int32),
            pltpu.VMEM(dest_block.shape, jnp.int32),
            pltpu.SMEM(land_mask.shape, jnp.int32),
            pltpu.VMEM((2 * SUB, depth, cells), jnp.float32),
            pltpu.SemaphoreType.DMA((4 + 2 * SUB,)),
        ],
        compiler_params=pltpu.CompilerParams(vmem_limit_bytes=32 << 20),
        name="boundary_rows",
    )(in_hbm(dest_tile.reshape(2 * lines, 128)), in_hbm(dest_block), in_hbm(land_mask), state)

    surface = lax.ppermute(surface, "comp", partner)
    ring = [(i, (i + 1) % tiles) for i in range(tiles)]
    before = lax.ppermute(tail, "tile", ring)
    after = lax.ppermute(head, "tile", [(b, a) for a, b in ring])

    outgoing = pl.pallas_call(
        functools.partial(send_kernel, cap, tiles),
        out_shape=jax.ShapeDtypeStruct((slots, fields, cells), jnp.bfloat16),
        in_specs=[anywhere] * 3,
        out_specs=vmem,
        scratch_shapes=[
            pltpu.SMEM(routes.shape, jnp.int32),
            pltpu.VMEM((fields * rows, cells), jnp.float32),
            pltpu.VMEM((rows, cells, cells), jnp.bfloat16),
            pltpu.VMEM((rows, fields, cells), jnp.bfloat16),
            pltpu.SMEM((tiles,), jnp.int32),
            pltpu.SemaphoreType.DMA((2 + chunks,)),
        ],
        compiler_params=pltpu.CompilerParams(vmem_limit_bytes=32 << 20),
        cost_estimate=pl.CostEstimate(
            flops=2 * rows * fields * cells * cells, bytes_accessed=8 << 20, transcendentals=0
        ),
        name="remap_and_pack",
    )(routes, surface, weight)
    before, after, outgoing = lax.optimization_barrier((before, after, outgoing))
    arrived = lax.all_to_all(outgoing, "tile", split_axis=0, concat_axis=0, tiled=True)

    total_rows = rows + 2 * SUB + GROUP
    field, top = pl.pallas_call(
        field_kernel,
        out_shape=(
            jax.ShapeDtypeStruct((depth, rows, cells), jnp.float32),
            jax.ShapeDtypeStruct((rows, fields, cells), jnp.float32),
        ),
        in_specs=[anywhere] * 6,
        out_specs=(anywhere, vmem),
        scratch_shapes=[
            pltpu.SMEM((rows,), jnp.int32),
            pltpu.VMEM((halo_rows, cells), jnp.bfloat16),
            pltpu.VMEM((halo_rows, cells), jnp.bfloat16),
            pltpu.VMEM((1, depth), jnp.float32),
            pltpu.VMEM((depth, depth), jnp.float32),
            pltpu.VMEM((rows, depth, cells), jnp.float32),
            pltpu.VMEM((total_rows, cells + 2 * EDGE, depth), jnp.float32),
            pltpu.VMEM((total_rows, cells + 2 * EDGE, depth), jnp.float32),
            pltpu.VMEM((2, 2, 16, depth), jnp.float32),
            pltpu.VMEM((2 * depth, 2 * depth), jnp.bfloat16),
            pltpu.SMEM((total_rows,), jnp.int32),
            pltpu.VMEM((GROUP * cells, 2 * depth), jnp.bfloat16),
            pltpu.VMEM((GROUP * cells, 2 * depth), jnp.bfloat16),
            pltpu.SemaphoreType.DMA((5,)),
            pltpu.SemaphoreType.DMA((rows // GROUP,)),
            pltpu.SemaphoreType.DMA((rows // GROUP,)),
        ],
        compiler_params=pltpu.CompilerParams(vmem_limit_bytes=32 << 20),
        cost_estimate=pl.CostEstimate(
            flops=18 * depth * depth * rows * cells,
            bytes_accessed=8 * depth * rows * cells,
            transcendentals=0,
        ),
        name="substeps",
    )(in_hbm(land_mask), state, before, after, in_hbm(diffusion), in_hbm(column_op[0]))

    new_state = pl.pallas_call(
        forcing_kernel,
        out_shape=jax.ShapeDtypeStruct((depth, rows, cells), jnp.float32),
        in_specs=[anywhere, anywhere, vmem, anywhere, anywhere],
        out_specs=anywhere,
        input_output_aliases={4: 0},
        scratch_shapes=[
            pltpu.SMEM((lines, 128), jnp.int32),
            pltpu.SMEM((fields,), jnp.float32),
            pltpu.VMEM(((rows + 1) * fields, cells), jnp.float32),
            pltpu.VMEM((rows * fields, cells), jnp.float32),
            pltpu.VMEM((fields, rows, cells), jnp.float32),
            pltpu.SemaphoreType.DMA((4,)),
        ],
        compiler_params=pltpu.CompilerParams(vmem_limit_bytes=32 << 20),
        name="add_forcing",
    )(target, couple_gain.reshape(-1), arrived, top, field)
    return new_state[None]


def solution(mesh):
    placed = (
        P("comp", "member", "tile", None),
        P("comp", "tile", None, None),
        P("comp", "member"),
        P("comp", "member", None),
        P("comp", "member"),
        P("tile"),
        P(),
        P(),
    )
    return jax.shard_map(
        on_device,
        mesh=mesh,
        in_specs=placed,
        out_specs=P("comp", "member", "tile", None),
        check_vma=False,
    )
```

```python
import functools

import jax
import jax.numpy as jnp
from jax import lax
from jax.experimental import pallas as pl
from jax.experimental.pallas import tpu as pltpu
from jax.sharding import PartitionSpec as P

SUB = 3
CHUNK = 8
GROUP = 8
EDGE = 8


def copies(pairs, sems, first):
    started = [pltpu.make_async_copy(a, b, sems.at[first + i]) for i, (a, b) in enumerate(pairs)]
    for copy in started:
        copy.start()
    return started


def halo_kernel(land_hbm, state_ref, head_ref, tail_ref, surface_ref, land_ref, slabs, sems):
    _, depth, cells = slabs.shape
    fields, rows, _ = surface_ref.shape
    comp = lax.axis_index("comp")
    ends = [*range(SUB), *range(rows - SUB, rows)]
    pairs = [(land_hbm, land_ref)] + [(state_ref.at[:, x, :], slabs.at[r]) for r, x in enumerate(ends)]
    get_land, *loads, surface = copies(pairs + [(state_ref.at[pl.ds(0, fields)], surface_ref)], sems, 0)
    get_land.wait()
    row_of = lax.broadcasted_iota(jnp.int32, (16, 128), 0)
    for out_ref, base, offset in ((head_ref, 0, 0), (tail_ref, SUB, rows - SUB)):
        flags = jnp.zeros((16, 128), jnp.float32)
        for r in range(SUB):
            flag = jnp.where(comp == 1, land_ref[offset + r], 1).astype(jnp.float32)
            flags = jnp.where(row_of == r, flag, flags)
        out_ref[pl.ds(SUB * depth, 16), :] = flags.astype(jnp.bfloat16)
        for r in range(SUB):
            loads[base + r].wait()
            out_ref[pl.ds(r * depth, depth), :] = slabs[base + r].astype(jnp.bfloat16)
    surface.wait()


def arrivals(cap, rows, comp, tile, dest_ref, block_ref):
    lines = dest_ref.shape[0] // 2
    dest = dest_ref[pl.ds((1 - comp) * lines, lines), :]
    both = [jnp.concatenate([block_ref[c : c + 1, pl.ds(e * 128, 128)] for e in range(lines)], axis=0) for c in range(2)]
    place = jnp.where(comp == 1, both[0], both[1])
    mine = dest == tile
    earlier = lax.broadcasted_iota(jnp.int32, (128, 128), 0)
    later = lax.broadcasted_iota(jnp.int32, (128, 128), 1)
    before = (earlier < later) & (lax.div(earlier, rows) == lax.div(later, rows))
    rank = jnp.dot(
        mine.astype(jnp.float32).astype(jnp.bfloat16),
        before.astype(jnp.float32).astype(jnp.bfloat16),
        preferred_element_type=jnp.float32,
    )
    lane = lax.broadcasted_iota(jnp.int32, (lines, 128), 1)
    offset = (place - rows).astype(jnp.float32)
    target = jnp.zeros((lines, 128), jnp.float32)
    for h in range(128 // rows):
        here = mine & (lax.div(lane, rows) == h)
        for r in range(cap):
            found = jnp.sum(jnp.where(here & (rank == r), offset, 0.0), axis=1, keepdims=True)
            target = jnp.where(lane == h * cap + r, found, target)
    return target.astype(jnp.int32) + rows


def send_kernel(
    cap,
    tiles,
    dest_hbm,
    lines_hbm,
    block_hbm,
    surface_ref,
    weight_ref,
    out_ref,
    target_ref,
    dest_ref,
    lines_ref,
    block_ref,
    blocks,
    count_ref,
    sems,
):
    fields, rows, cells = surface_ref.shape
    comp, tile = lax.axis_index("comp"), lax.axis_index("tile")
    tables = copies(((dest_hbm, dest_ref), (lines_hbm, lines_ref), (block_hbm, block_ref)), sems, 0)
    lines = surface_ref.reshape(fields * rows, cells)

    def remap(i, carry):
        for k in range(CHUNK):
            j = i * CHUNK + k
            values = lines[pl.ds(j, fields, stride=rows), :].astype(jnp.bfloat16)
            block = jnp.dot(values, weight_ref[j], preferred_element_type=jnp.float32)
            blocks[j] = block.astype(jnp.bfloat16)
        return carry

    lax.fori_loop(0, rows // CHUNK, remap, 0)

    for t in range(tiles):
        count_ref[t] = 0
    for copy in tables:
        copy.wait()

    def place(j, carry):
        d = dest_ref[(1 - comp) * (tiles * rows) + tile * rows + j]
        n = count_ref[d]
        out_ref[d * cap + n] = blocks[j]
        count_ref[d] = n + 1
        return carry

    lax.fori_loop(0, rows, place, 0, unroll=8)
    target_ref[...] = arrivals(cap, rows, comp, tile, lines_ref, block_ref)


def field_kernel(
    land_hbm,
    state_ref,
    before_hbm,
    after_hbm,
    diffusion_hbm,
    column_hbm,
    out_ref,
    top_ref,
    land_ref,
    before_ref,
    after_ref,
    diffusion_ref,
    column_ref,
    slabs,
    u0,
    u1,
    coef,
    right,
    flags,
    half0,
    half1,
    small_sems,
    in_sems,
    out_sems,
):
    depth, rows, cells = state_ref.shape
    groups = rows // GROUP
    comp, fields = lax.axis_index("comp"), top_ref.shape[1]
    inside = pl.ds(EDGE, cells)
    below = pl.ds(fields, depth - fields)

    def load(x, carry):
        pltpu.make_async_copy(state_ref.at[:, x, :], slabs.at[x], in_sems.at[lax.div(x, GROUP)]).start()
        return carry

    small = copies(
        (
            (diffusion_hbm, diffusion_ref),
            (column_hbm, column_ref),
            (land_hbm, land_ref),
            (before_hbm, before_ref),
            (after_hbm, after_ref),
        ),
        small_sems,
        0,
    )
    lax.fori_loop(0, rows, load, 0, unroll=4)

    def border(x, carry):
        zeros = jnp.zeros((EDGE, depth), jnp.float32)
        for u in (u0, u1):
            u[x, pl.ds(0, EDGE), :] = zeros
            u[x, pl.ds(EDGE + cells, EDGE), :] = zeros
        return carry
    lax.fori_loop(0, u0.shape[0], border, 0, unroll=2)
    for copy in small:
        copy.wait()

    rate = diffusion_ref[...]
    coef[0, 0] = jnp.ones_like(coef[0, 0])
    coef[0, 1] = jnp.zeros_like(coef[0, 0])
    coef[1, 0] = jnp.broadcast_to(1.0 - 4.0 * rate, (16, depth))
    coef[1, 1] = jnp.broadcast_to(rate, (16, depth))
    column = jnp.transpose(column_ref[...])
    high = column.astype(jnp.bfloat16)
    low = (column - high.astype(jnp.float32)).astype(jnp.bfloat16)
    right[0:depth, 0:depth] = high
    right[depth : 2 * depth, 0:depth] = high
    right[0:depth, depth : 2 * depth] = low
    right[depth : 2 * depth, depth : 2 * depth] = jnp.zeros_like(low)

    def own_flag(i, carry):
        flags[i + SUB] = jnp.where(comp == 1, land_ref[i], 1)
        return carry
    lax.fori_loop(0, rows, own_flag, 0, unroll=8)
    for r in range(SUB):
        flags[r] = jnp.max(before_ref[pl.ds(SUB * depth, 16), :][r : r + 1, :].astype(jnp.float32)).astype(jnp.int32)
        flags[rows + SUB + r] = jnp.max(
            after_ref[pl.ds(SUB * depth, 16), :][r : r + 1, :].astype(jnp.float32)
        ).astype(jnp.int32)
        u0[r, inside, :] = jnp.transpose(before_ref[pl.ds(r * depth, depth), :].astype(jnp.float32))
        u0[rows + SUB + r, inside, :] = jnp.transpose(after_ref[pl.ds(r * depth, depth), :].astype(jnp.float32))
    for r in range(rows + 2 * SUB, flags.shape[0]):
        flags[r] = 0

    def wait_in(g):
        pltpu.make_async_copy(
            slabs.at[pl.ds(g * GROUP, GROUP)], slabs.at[pl.ds(g * GROUP, GROUP)], in_sems.at[g]
        ).wait()

    def turn(s):
        u0[s + SUB, inside, :] = jnp.transpose(slabs[s])

    def stencil(source, x, half):
        for side in range(GROUP):
            active = flags[x + side]
            keep, spread = coef[active, 0], coef[active, 1]
            for k in range(0, cells, 16):
                at = pl.ds(EDGE + k, 16)
                near = source[x + side - 1, at, :] + source[x + side + 1, at, :]
                near += source[x + side, pl.ds(EDGE + k - 1, 16), :] + source[x + side, pl.ds(EDGE + k + 1, 16), :]
                stepped = keep * source[x + side, at, :] + spread * near
                high = stepped.astype(jnp.bfloat16)
                half[pl.ds(side * cells + k, 16), 0:depth] = high
                half[pl.ds(side * cells + k, 16), depth : 2 * depth] = (
                    stepped - high.astype(jnp.float32)
                ).astype(jnp.bfloat16)

    def product(half, count, store):
        mixed = jnp.dot(half[0 : count * cells], right[...], preferred_element_type=jnp.float32)
        mixed = mixed[:, 0:depth] + mixed[:, depth : 2 * depth]
        for side in range(count):
            store(side, mixed[side * cells : (side + 1) * cells])

    def keep_in(target, x):
        def store(side, values):
            target[x + side, inside, :] = values
        return store

    def finish(x):
        def store(side, values):
            turned = jnp.transpose(values)
            top_ref[x + side] = turned[0:fields]
            slabs[x + side] = turned
        return store

    def send_out(x):
        for side in range(GROUP):
            pltpu.make_async_copy(
                slabs.at[x + side, below, :], out_ref.at[below, x + side, :], out_sems.at[lax.div(x, GROUP)]
            ).start()

    wait_in(0)
    wait_in(1)
    for s in range(2 * GROUP - 1):
        turn(s)
    span = 2 * GROUP
    bodies = rows // span

    stencil(u0, 1, half0)
    def body1(i, carry):
        x = 1 + span * i
        @pl.when(2 * i + 3 < groups)
        def _():
            wait_in(2 * i + 2)
            wait_in(2 * i + 3)
        product(half0, GROUP, keep_in(u1, x))
        stencil(u0, x + GROUP, half1)
        for s in range(GROUP):
            turn(jnp.minimum(span * i + span - 1 + s, rows - 1))
        product(half1, GROUP, keep_in(u1, x + GROUP))
        stencil(u0, x + span, half0)
        for s in range(GROUP, span):
            turn(jnp.minimum(span * i + span - 1 + s, rows - 1))
        return carry
    lax.fori_loop(0, bodies, body1, 0)
    product(half0, 4, keep_in(u1, rows + 1))

    stencil(u1, 2, half0)
    def body2(i, carry):
        x = 2 + span * i
        product(half0, GROUP, keep_in(u0, x))
        stencil(u1, x + GROUP, half1)
        product(half1, GROUP, keep_in(u0, x + GROUP))
        stencil(u1, x + span, half0)
        return carry
    lax.fori_loop(0, bodies, body2, 0)
    product(half0, 2, keep_in(u0, rows + 2))

    stencil(u0, SUB, half0)
    def body3(i, carry):
        x = span * i
        product(half0, GROUP, finish(x))
        stencil(u0, SUB + x + GROUP, half1)
        send_out(x)
        product(half1, GROUP, finish(x + GROUP))
        stencil(u0, SUB + x + span, half0)
        send_out(x + GROUP)
        return carry
    lax.fori_loop(0, bodies, body3, 0)

    def wait_out(i, carry):
        part = slabs.at[pl.ds(0, GROUP), below, :]
        pltpu.make_async_copy(part, part, out_sems.at[i]).wait()
        return carry
    lax.fori_loop(0, groups, wait_out, 0)


def forcing_kernel(target_hbm, gain_hbm, arrived_ref, top_ref, field_ref, out_ref, target_ref, gain_ref, total, result, sems):
    slots, fields, _ = arrived_ref.shape
    rows, _, cells = top_ref.shape
    own = total.reshape(rows + 1, fields, cells).at[pl.ds(0, rows)]
    loads = copies(((target_hbm, target_ref), (gain_hbm, gain_ref), (top_ref, own)), sems, 0)
    total[pl.ds(rows * fields, fields), :] = jnp.zeros((fields, cells), jnp.float32)
    for copy in loads:
        copy.wait()

    field_of = lax.broadcasted_iota(jnp.int32, (fields, cells), 0)
    gain = jnp.zeros((fields, cells), jnp.float32)
    for f in range(fields):
        gain = jnp.where(field_of == f, gain_ref[0, f], gain)
    lines = target_ref.shape[0]
    count = slots // lines

    def add(e, carry):
        for s in range(count):
            at = pl.ds(pl.multiple_of(target_ref[e, s] * fields, fields), fields)
            total[at, :] += gain * arrived_ref[e * count + s].astype(jnp.float32)
        return carry

    lax.fori_loop(0, lines, add, 0)
    stores = []
    for first in range(0, fields, 4):
        part = pl.ds(first, 4)
        for f in range(first, first + 4):
            result[f] = total[pl.ds(f, rows, stride=fields), :]
        stores += copies(((result.at[part], out_ref.at[part]),), sems, 3 + first // 4)
    for copy in stores:
        copy.wait()


def on_device(
    prognostic_state,
    remapping_weight,
    diffusion,
    column_op,
    couple_gain,
    land_mask,
    dest_tile,
    dest_block,
):
    tiles = lax.axis_size("tile")
    in_hbm = functools.partial(pltpu.with_memory_space_constraint, memory_space=pltpu.HBM)
    state = in_hbm(prognostic_state[0])
    depth, rows, cells = state.shape
    fields = couple_gain.shape[1]
    cap = max(2, 2 * rows // tiles)
    slots = tiles * cap
    halo_rows = SUB * depth + 16
    routes = in_hbm(dest_tile.reshape(-1))
    lines = tiles * rows // 128

    vmem = pl.BlockSpec(memory_space=pltpu.VMEM)
    anywhere = pl.BlockSpec(memory_space=pltpu.HBM)

    partner = [(0, 1), (1, 0)]
    weight = lax.ppermute(remapping_weight[0], "comp", partner)

    head, tail, surface = pl.pallas_call(
        halo_kernel,
        out_shape=(
            jax.ShapeDtypeStruct((halo_rows, cells), jnp.bfloat16),
            jax.ShapeDtypeStruct((halo_rows, cells), jnp.bfloat16),
            jax.ShapeDtypeStruct((fields, rows, cells), jnp.float32),
        ),
        in_specs=[anywhere] * 2,
        out_specs=(vmem, vmem, vmem),
        scratch_shapes=[
            pltpu.SMEM(land_mask.shape, jnp.int32),
            pltpu.VMEM((2 * SUB, depth, cells), jnp.float32),
            pltpu.SemaphoreType.DMA((2 + 2 * SUB,)),
        ],
        compiler_params=pltpu.CompilerParams(vmem_limit_bytes=32 << 20),
        name="boundary_rows",
    )(in_hbm(land_mask), state)

    surface = lax.ppermute(surface, "comp", partner)
    ring = [(i, (i + 1) % tiles) for i in range(tiles)]
    before = lax.ppermute(tail, "tile", ring)
    after = lax.ppermute(head, "tile", [(b, a) for a, b in ring])

    outgoing, target = pl.pallas_call(
        functools.partial(send_kernel, cap, tiles),
        out_shape=(
            jax.ShapeDtypeStruct((slots, fields, cells), jnp.bfloat16),
            jax.ShapeDtypeStruct((lines, 128), jnp.int32),
        ),
        in_specs=[anywhere, anywhere, anywhere, vmem, vmem],
        out_specs=(vmem, vmem),
        scratch_shapes=[
            pltpu.SMEM(routes.shape, jnp.int32),
            pltpu.VMEM((2 * lines, 128), jnp.int32),
            pltpu.VMEM(dest_block.shape, jnp.int32),
            pltpu.VMEM((rows, fields, cells), jnp.bfloat16),
            pltpu.SMEM((tiles,), jnp.int32),
            pltpu.SemaphoreType.DMA((3,)),
        ],
        compiler_params=pltpu.CompilerParams(vmem_limit_bytes=32 << 20),
        cost_estimate=pl.CostEstimate(
            flops=2 * rows * fields * cells * cells, bytes_accessed=8 << 20, transcendentals=0
        ),
        name="remap_and_pack",
    )(routes, in_hbm(dest_tile.reshape(2 * lines, 128)), in_hbm(dest_block), surface, weight)
    before, after, outgoing = lax.optimization_barrier((before, after, outgoing))
    arrived = lax.all_to_all(outgoing, "tile", split_axis=0, concat_axis=0, tiled=True)

    total_rows = rows + 2 * SUB + GROUP
    field, top = pl.pallas_call(
        field_kernel,
        out_shape=(
            jax.ShapeDtypeStruct((depth, rows, cells), jnp.float32),
            jax.ShapeDtypeStruct((rows, fields, cells), jnp.float32),
        ),
        in_specs=[anywhere] * 6,
        out_specs=(anywhere, vmem),
        scratch_shapes=[
            pltpu.SMEM((rows,), jnp.int32),
            pltpu.VMEM((halo_rows, cells), jnp.bfloat16),
            pltpu.VMEM((halo_rows, cells), jnp.bfloat16),
            pltpu.VMEM((1, depth), jnp.float32),
            pltpu.VMEM((depth, depth), jnp.float32),
            pltpu.VMEM((rows, depth, cells), jnp.float32),
            pltpu.VMEM((total_rows, cells + 2 * EDGE, depth), jnp.float32),
            pltpu.VMEM((total_rows, cells + 2 * EDGE, depth), jnp.float32),
            pltpu.VMEM((2, 2, 16, depth), jnp.float32),
            pltpu.VMEM((2 * depth, 2 * depth), jnp.bfloat16),
            pltpu.SMEM((total_rows,), jnp.int32),
            pltpu.VMEM((GROUP * cells, 2 * depth), jnp.bfloat16),
            pltpu.VMEM((GROUP * cells, 2 * depth), jnp.bfloat16),
            pltpu.SemaphoreType.DMA((5,)),
            pltpu.SemaphoreType.DMA((rows // GROUP,)),
            pltpu.SemaphoreType.DMA((rows // GROUP,)),
        ],
        compiler_params=pltpu.CompilerParams(vmem_limit_bytes=32 << 20),
        cost_estimate=pl.CostEstimate(
            flops=18 * depth * depth * rows * cells,
            bytes_accessed=8 * depth * rows * cells,
            transcendentals=0,
        ),
        name="substeps",
    )(in_hbm(land_mask), state, before, after, in_hbm(diffusion), in_hbm(column_op[0]))

    new_state = pl.pallas_call(
        forcing_kernel,
        out_shape=jax.ShapeDtypeStruct((depth, rows, cells), jnp.float32),
        in_specs=[anywhere, anywhere, vmem, anywhere, anywhere],
        out_specs=anywhere,
        input_output_aliases={4: 0},
        scratch_shapes=[
            pltpu.SMEM((lines, 128), jnp.int32),
            pltpu.SMEM(couple_gain.shape, jnp.float32),
            pltpu.VMEM(((rows + 1) * fields, cells), jnp.float32),
            pltpu.VMEM((fields, rows, cells), jnp.float32),
            pltpu.SemaphoreType.DMA((3 + fields // 4,)),
        ],
        compiler_params=pltpu.CompilerParams(vmem_limit_bytes=32 << 20),
        name="add_forcing",
    )(target, in_hbm(couple_gain), arrived, top, field)
    return new_state[None]


def solution(mesh):
    placed = (
        P("comp", "member", "tile", None),
        P("comp", "tile", None, None),
        P("comp", "member"),
        P("comp", "member", None),
        P("comp", "member"),
        P("tile"),
        P(),
        P(),
    )
    return jax.shard_map(
        on_device,
        mesh=mesh,
        in_specs=placed,
        out_specs=P("comp", "member", "tile", None),
        check_vma=False,
    )
```

```python
import functools

import jax
import jax.numpy as jnp
from jax import lax
from jax.experimental import pallas as pl
from jax.experimental.pallas import tpu as pltpu
from jax.sharding import PartitionSpec as P

SUB = 3
CHUNK = 16
GROUP = 8
EDGE = 8


def copies(pairs, sems, first):
    started = [pltpu.make_async_copy(a, b, sems.at[first + i]) for i, (a, b) in enumerate(pairs)]
    for copy in started:
        copy.start()
    return started


def halo_kernel(land_hbm, state_ref, head_ref, tail_ref, surface_ref, land_ref, slabs, top, sems):
    _, depth, cells = slabs.shape
    fields, rows, _ = surface_ref.shape
    comp = lax.axis_index("comp")
    ends = [*range(SUB), *range(rows - SUB, rows)]
    pairs = [(land_hbm, land_ref)] + [(state_ref.at[:, x, :], slabs.at[r]) for r, x in enumerate(ends)]
    get_land, *loads, surface = copies(pairs + [(state_ref.at[pl.ds(0, fields)], top)], sems, 0)
    get_land.wait()
    row_of = lax.broadcasted_iota(jnp.int32, (16, 128), 0)
    for out_ref, base, offset in ((head_ref, 0, 0), (tail_ref, SUB, rows - SUB)):
        flags = jnp.zeros((16, 128), jnp.float32)
        for r in range(SUB):
            flag = jnp.where(comp == 1, land_ref[offset + r], 1).astype(jnp.float32)
            flags = jnp.where(row_of == r, flag, flags)
        out_ref[pl.ds(SUB * depth, 16), :] = flags.astype(jnp.bfloat16)
        for r in range(SUB):
            loads[base + r].wait()
            out_ref[pl.ds(r * depth, depth), :] = slabs[base + r].astype(jnp.bfloat16)
    surface.wait()
    surface_ref[...] = top[...].astype(jnp.bfloat16)


def arrivals(cap, rows, comp, tile, dest_ref, block_ref):
    lines = dest_ref.shape[0] // 2
    dest = dest_ref[pl.ds((1 - comp) * lines, lines), :]
    both = [jnp.concatenate([block_ref[c : c + 1, pl.ds(e * 128, 128)] for e in range(lines)], axis=0) for c in range(2)]
    place = jnp.where(comp == 1, both[0], both[1])
    mine = dest == tile
    earlier = lax.broadcasted_iota(jnp.int32, (128, 128), 0)
    later = lax.broadcasted_iota(jnp.int32, (128, 128), 1)
    before = (earlier < later) & (lax.div(earlier, rows) == lax.div(later, rows))
    rank = jnp.dot(
        mine.astype(jnp.float32).astype(jnp.bfloat16),
        before.astype(jnp.float32).astype(jnp.bfloat16),
        preferred_element_type=jnp.float32,
    )
    lane = lax.broadcasted_iota(jnp.int32, (lines, 128), 1)
    offset = (place - rows).astype(jnp.float32)
    target = jnp.zeros((lines, 128), jnp.float32)
    for h in range(128 // rows):
        here = mine & (lax.div(lane, rows) == h)
        for r in range(cap):
            found = jnp.sum(jnp.where(here & (rank == r), offset, 0.0), axis=1, keepdims=True)
            target = jnp.where(lane == h * cap + r, found, target)
    return target.astype(jnp.int32) + rows


def send_kernel(cap, tiles, dest_hbm, surface_ref, weight_ref, out_ref, dest_ref, surface, blocks, count_ref, sem):
    fields, rows, cells = surface_ref.shape
    comp, tile = lax.axis_index("comp"), lax.axis_index("tile")
    get_dest = pltpu.make_async_copy(dest_hbm, dest_ref, sem)
    get_dest.start()
    surface[...] = surface_ref[...].astype(jnp.float32)
    lines = surface.reshape(fields * rows, cells)

    def remap(i, carry):
        for k in range(CHUNK):
            j = i * CHUNK + k
            values = lines[pl.ds(j, fields, stride=rows), :].astype(jnp.bfloat16)
            block = jnp.dot(values, weight_ref[j], preferred_element_type=jnp.float32)
            blocks[j] = block.astype(jnp.bfloat16)
        return carry

    lax.fori_loop(0, rows // CHUNK, remap, 0)

    for t in range(tiles):
        count_ref[t] = 0
    get_dest.wait()

    def place(j, carry):
        d = dest_ref[(1 - comp) * (tiles * rows) + tile * rows + j]
        n = count_ref[d]
        out_ref[d * cap + n] = blocks[j]
        count_ref[d] = n + 1
        return carry

    lax.fori_loop(0, rows, place, 0, unroll=8)


def field_kernel(
    cap,
    lines_hbm,
    block_hbm,
    land_hbm,
    state_ref,
    before_hbm,
    after_hbm,
    diffusion_hbm,
    column_hbm,
    out_ref,
    top_ref,
    target_ref,
    lines_ref,
    block_ref,
    land_ref,
    before_ref,
    after_ref,
    diffusion_ref,
    column_ref,
    slabs,
    u0,
    u1,
    coef,
    right,
    flags,
    half0,
    half1,
    small_sems,
    in_sems,
    out_sems,
):
    depth, rows, cells = state_ref.shape
    groups = rows // GROUP
    comp, fields = lax.axis_index("comp"), top_ref.shape[1]
    inside = pl.ds(EDGE, cells)
    below = pl.ds(fields, depth - fields)

    def load(x, carry):
        pltpu.make_async_copy(state_ref.at[:, x, :], slabs.at[x], in_sems.at[lax.div(x, GROUP)]).start()
        return carry

    small = copies(
        (
            (lines_hbm, lines_ref),
            (block_hbm, block_ref),
            (diffusion_hbm, diffusion_ref),
            (column_hbm, column_ref),
            (land_hbm, land_ref),
            (before_hbm, before_ref),
            (after_hbm, after_ref),
        ),
        small_sems,
        0,
    )
    lax.fori_loop(0, rows, load, 0, unroll=4)

    def border(x, carry):
        zeros = jnp.zeros((EDGE, depth), jnp.float32)
        for u in (u0, u1):
            u[x, pl.ds(0, EDGE), :] = zeros
            u[x, pl.ds(EDGE + cells, EDGE), :] = zeros
        return carry
    lax.fori_loop(0, u0.shape[0], border, 0, unroll=2)
    for copy in small:
        copy.wait()
    target_ref[...] = arrivals(cap, rows, comp, lax.axis_index("tile"), lines_ref, block_ref)

    rate = diffusion_ref[...]
    coef[0, 0] = jnp.ones_like(coef[0, 0])
    coef[0, 1] = jnp.zeros_like(coef[0, 0])
    coef[1, 0] = jnp.broadcast_to(1.0 - 4.0 * rate, (16, depth))
    coef[1, 1] = jnp.broadcast_to(rate, (16, depth))
    column = jnp.transpose(column_ref[...])
    high = column.astype(jnp.bfloat16)
    low = (column - high.astype(jnp.float32)).astype(jnp.bfloat16)
    right[0:depth, 0:depth] = high
    right[depth : 2 * depth, 0:depth] = high
    right[0:depth, depth : 2 * depth] = low
    right[depth : 2 * depth, depth : 2 * depth] = jnp.zeros_like(low)

    def own_flag(i, carry):
        flags[i + SUB] = jnp.where(comp == 1, land_ref[i], 1)
        return carry
    lax.fori_loop(0, rows, own_flag, 0, unroll=8)
    for r in range(SUB):
        flags[r] = jnp.max(before_ref[pl.ds(SUB * depth, 16), :][r : r + 1, :].astype(jnp.float32)).astype(jnp.int32)
        flags[rows + SUB + r] = jnp.max(
            after_ref[pl.ds(SUB * depth, 16), :][r : r + 1, :].astype(jnp.float32)
        ).astype(jnp.int32)
        u0[r, inside, :] = jnp.transpose(before_ref[pl.ds(r * depth, depth), :].astype(jnp.float32))
        u0[rows + SUB + r, inside, :] = jnp.transpose(after_ref[pl.ds(r * depth, depth), :].astype(jnp.float32))
    for r in range(rows + 2 * SUB, flags.shape[0]):
        flags[r] = 0

    def wait_in(g):
        pltpu.make_async_copy(
            slabs.at[pl.ds(g * GROUP, GROUP)], slabs.at[pl.ds(g * GROUP, GROUP)], in_sems.at[g]
        ).wait()

    def turn(s):
        u0[s + SUB, inside, :] = jnp.transpose(slabs[s])

    def stencil(source, x, half):
        for side in range(GROUP):
            active = flags[x + side]
            keep, spread = coef[active, 0], coef[active, 1]
            for k in range(0, cells, 16):
                at = pl.ds(EDGE + k, 16)
                near = source[x + side - 1, at, :] + source[x + side + 1, at, :]
                near += source[x + side, pl.ds(EDGE + k - 1, 16), :] + source[x + side, pl.ds(EDGE + k + 1, 16), :]
                stepped = keep * source[x + side, at, :] + spread * near
                high = stepped.astype(jnp.bfloat16)
                half[pl.ds(side * cells + k, 16), 0:depth] = high
                half[pl.ds(side * cells + k, 16), depth : 2 * depth] = (
                    stepped - high.astype(jnp.float32)
                ).astype(jnp.bfloat16)

    def product(half, count, store):
        mixed = jnp.dot(half[0 : count * cells], right[...], preferred_element_type=jnp.float32)
        mixed = mixed[:, 0:depth] + mixed[:, depth : 2 * depth]
        for side in range(count):
            store(side, mixed[side * cells : (side + 1) * cells])

    def keep_in(target, x):
        def store(side, values):
            target[x + side, inside, :] = values
        return store

    def finish(x):
        def store(side, values):
            turned = jnp.transpose(values)
            top_ref[x + side] = turned[0:fields]
            slabs[x + side] = turned
        return store

    def send_out(x):
        for side in range(GROUP):
            pltpu.make_async_copy(
                slabs.at[x + side, below, :], out_ref.at[below, x + side, :], out_sems.at[lax.div(x, GROUP)]
            ).start()

    wait_in(0)
    wait_in(1)
    for s in range(2 * GROUP - 1):
        turn(s)
    span = 2 * GROUP
    bodies = rows // span

    stencil(u0, 1, half0)
    def body1(i, carry):
        x = 1 + span * i
        @pl.when(2 * i + 3 < groups)
        def _():
            wait_in(2 * i + 2)
            wait_in(2 * i + 3)
        product(half0, GROUP, keep_in(u1, x))
        stencil(u0, x + GROUP, half1)
        for s in range(GROUP):
            turn(jnp.minimum(span * i + span - 1 + s, rows - 1))
        product(half1, GROUP, keep_in(u1, x + GROUP))
        stencil(u0, x + span, half0)
        for s in range(GROUP, span):
            turn(jnp.minimum(span * i + span - 1 + s, rows - 1))
        return carry
    lax.fori_loop(0, bodies, body1, 0)
    product(half0, 4, keep_in(u1, rows + 1))

    stencil(u1, 2, half0)
    def body2(i, carry):
        x = 2 + span * i
        product(half0, GROUP, keep_in(u0, x))
        stencil(u1, x + GROUP, half1)
        product(half1, GROUP, keep_in(u0, x + GROUP))
        stencil(u1, x + span, half0)
        return carry
    lax.fori_loop(0, bodies, body2, 0)
    product(half0, 2, keep_in(u0, rows + 2))

    stencil(u0, SUB, half0)
    def body3(i, carry):
        x = span * i
        product(half0, GROUP, finish(x))
        stencil(u0, SUB + x + GROUP, half1)
        send_out(x)
        product(half1, GROUP, finish(x + GROUP))
        stencil(u0, SUB + x + span, half0)
        send_out(x + GROUP)
        return carry
    lax.fori_loop(0, bodies, body3, 0)

    def wait_out(i, carry):
        part = slabs.at[pl.ds(0, GROUP), below, :]
        pltpu.make_async_copy(part, part, out_sems.at[i]).wait()
        return carry
    lax.fori_loop(0, groups, wait_out, 0)


def forcing_kernel(target_hbm, gain_hbm, arrived_ref, top_ref, field_ref, out_ref, target_ref, gain_ref, total, result, sems):
    slots, fields, _ = arrived_ref.shape
    rows, _, cells = top_ref.shape
    own = total.reshape(rows + 1, fields, cells).at[pl.ds(0, rows)]
    loads = copies(((target_hbm, target_ref), (gain_hbm, gain_ref), (top_ref, own)), sems, 0)
    total[pl.ds(rows * fields, fields), :] = jnp.zeros((fields, cells), jnp.float32)
    for copy in loads:
        copy.wait()

    field_of = lax.broadcasted_iota(jnp.int32, (fields, cells), 0)
    gain = jnp.zeros((fields, cells), jnp.float32)
    for f in range(fields):
        gain = jnp.where(field_of == f, gain_ref[0, f], gain)
    lines = target_ref.shape[0]
    count = slots // lines

    def add(e, carry):
        for s in range(count):
            at = pl.ds(pl.multiple_of(target_ref[e, s] * fields, fields), fields)
            total[at, :] += gain * arrived_ref[e * count + s].astype(jnp.float32)
        return carry

    lax.fori_loop(0, lines, add, 0)
    stores = []
    for first in range(0, fields, 4):
        part = pl.ds(first, 4)
        for f in range(first, first + 4):
            result[f] = total[pl.ds(f, rows, stride=fields), :]
        stores += copies(((result.at[part], out_ref.at[part]),), sems, 3 + first // 4)
    for copy in stores:
        copy.wait()


def on_device(
    prognostic_state,
    remapping_weight,
    diffusion,
    column_op,
    couple_gain,
    land_mask,
    dest_tile,
    dest_block,
):
    tiles = lax.axis_size("tile")
    in_hbm = functools.partial(pltpu.with_memory_space_constraint, memory_space=pltpu.HBM)
    state = in_hbm(prognostic_state[0])
    depth, rows, cells = state.shape
    fields = couple_gain.shape[1]
    cap = max(2, 2 * rows // tiles)
    slots = tiles * cap
    halo_rows = SUB * depth + 16
    routes = in_hbm(dest_tile.reshape(-1))
    lines = tiles * rows // 128

    vmem = pl.BlockSpec(memory_space=pltpu.VMEM)
    anywhere = pl.BlockSpec(memory_space=pltpu.HBM)

    partner = [(0, 1), (1, 0)]
    weight = lax.ppermute(remapping_weight[0], "comp", partner)

    head, tail, surface = pl.pallas_call(
        halo_kernel,
        out_shape=(
            jax.ShapeDtypeStruct((halo_rows, cells), jnp.bfloat16),
            jax.ShapeDtypeStruct((halo_rows, cells), jnp.bfloat16),
            jax.ShapeDtypeStruct((fields, rows, cells), jnp.bfloat16),
        ),
        in_specs=[anywhere] * 2,
        out_specs=(vmem, vmem, vmem),
        scratch_shapes=[
            pltpu.SMEM(land_mask.shape, jnp.int32),
            pltpu.VMEM((2 * SUB, depth, cells), jnp.float32),
            pltpu.VMEM((fields, rows, cells), jnp.float32),
            pltpu.SemaphoreType.DMA((2 + 2 * SUB,)),
        ],
        compiler_params=pltpu.CompilerParams(vmem_limit_bytes=32 << 20),
        name="boundary_rows",
    )(in_hbm(land_mask), state)

    surface = lax.ppermute(surface, "comp", partner)
    ring = [(i, (i + 1) % tiles) for i in range(tiles)]
    before = lax.ppermute(tail, "tile", ring)
    after = lax.ppermute(head, "tile", [(b, a) for a, b in ring])

    outgoing = pl.pallas_call(
        functools.partial(send_kernel, cap, tiles),
        out_shape=jax.ShapeDtypeStruct((slots, fields, cells), jnp.bfloat16),
        in_specs=[anywhere, vmem, vmem],
        out_specs=vmem,
        scratch_shapes=[
            pltpu.SMEM(routes.shape, jnp.int32),
            pltpu.VMEM((fields, rows, cells), jnp.float32),
            pltpu.VMEM((rows, fields, cells), jnp.bfloat16),
            pltpu.SMEM((tiles,), jnp.int32),
            pltpu.SemaphoreType.DMA,
        ],
        compiler_params=pltpu.CompilerParams(vmem_limit_bytes=32 << 20),
        cost_estimate=pl.CostEstimate(
            flops=2 * rows * fields * cells * cells, bytes_accessed=8 << 20, transcendentals=0
        ),
        name="remap_and_pack",
    )(routes, surface, weight)
    arrived = lax.all_to_all(outgoing, "tile", split_axis=0, concat_axis=0, tiled=True)

    total_rows = rows + 2 * SUB + GROUP
    field, top, target = pl.pallas_call(
        functools.partial(field_kernel, cap),
        out_shape=(
            jax.ShapeDtypeStruct((depth, rows, cells), jnp.float32),
            jax.ShapeDtypeStruct((rows, fields, cells), jnp.float32),
            jax.ShapeDtypeStruct((lines, 128), jnp.int32),
        ),
        in_specs=[anywhere] * 8,
        out_specs=(anywhere, vmem, vmem),
        scratch_shapes=[
            pltpu.VMEM((2 * lines, 128), jnp.int32),
            pltpu.VMEM(dest_block.shape, jnp.int32),
            pltpu.SMEM((rows,), jnp.int32),
            pltpu.VMEM((halo_rows, cells), jnp.bfloat16),
            pltpu.VMEM((halo_rows, cells), jnp.bfloat16),
            pltpu.VMEM((1, depth), jnp.float32),
            pltpu.VMEM((depth, depth), jnp.float32),
            pltpu.VMEM((rows, depth, cells), jnp.float32),
            pltpu.VMEM((total_rows, cells + 2 * EDGE, depth), jnp.float32),
            pltpu.VMEM((total_rows, cells + 2 * EDGE, depth), jnp.float32),
            pltpu.VMEM((2, 2, 16, depth), jnp.float32),
            pltpu.VMEM((2 * depth, 2 * depth), jnp.bfloat16),
            pltpu.SMEM((total_rows,), jnp.int32),
            pltpu.VMEM((GROUP * cells, 2 * depth), jnp.bfloat16),
            pltpu.VMEM((GROUP * cells, 2 * depth), jnp.bfloat16),
            pltpu.SemaphoreType.DMA((7,)),
            pltpu.SemaphoreType.DMA((rows // GROUP,)),
            pltpu.SemaphoreType.DMA((rows // GROUP,)),
        ],
        compiler_params=pltpu.CompilerParams(vmem_limit_bytes=32 << 20),
        cost_estimate=pl.CostEstimate(
            flops=120 * depth * depth * rows * cells,
            bytes_accessed=8 * depth * rows * cells,
            transcendentals=0,
        ),
        name="substeps",
    )(
        in_hbm(dest_tile.reshape(2 * lines, 128)),
        in_hbm(dest_block),
        in_hbm(land_mask),
        state,
        before,
        after,
        in_hbm(diffusion),
        in_hbm(column_op[0]),
    )

    new_state = pl.pallas_call(
        forcing_kernel,
        out_shape=jax.ShapeDtypeStruct((depth, rows, cells), jnp.float32),
        in_specs=[anywhere, anywhere, vmem, anywhere, anywhere],
        out_specs=anywhere,
        input_output_aliases={4: 0},
        scratch_shapes=[
            pltpu.SMEM((lines, 128), jnp.int32),
            pltpu.SMEM(couple_gain.shape, jnp.float32),
            pltpu.VMEM(((rows + 1) * fields, cells), jnp.float32),
            pltpu.VMEM((fields, rows, cells), jnp.float32),
            pltpu.SemaphoreType.DMA((3 + fields // 4,)),
        ],
        compiler_params=pltpu.CompilerParams(vmem_limit_bytes=32 << 20),
        name="add_forcing",
    )(target, in_hbm(couple_gain), arrived, top, field)
    return new_state[None]


def solution(mesh):
    placed = (
        P("comp", "member", "tile", None),
        P("comp", "tile", None, None),
        P("comp", "member"),
        P("comp", "member", None),
        P("comp", "member"),
        P("tile"),
        P(),
        P(),
    )
    return jax.shard_map(
        on_device,
        mesh=mesh,
        in_specs=placed,
        out_specs=P("comp", "member", "tile", None),
        check_vma=False,
    )
```

```python
import functools

import jax
import jax.numpy as jnp
from jax import lax
from jax.experimental import pallas as pl
from jax.experimental.pallas import tpu as pltpu
from jax.sharding import PartitionSpec as P

SUB = 3
CHUNK = 32
GROUP = 8
EDGE = 8
PART = 4


def copies(pairs, sems, first):
    started = [pltpu.make_async_copy(a, b, sems.at[first + i]) for i, (a, b) in enumerate(pairs)]
    for copy in started:
        copy.start()
    return started


def halo_kernel(land_hbm, state_ref, head_ref, tail_ref, surface_ref, land_ref, slabs, sems):
    _, depth, cells = slabs.shape
    fields, rows, _ = surface_ref.shape
    comp = lax.axis_index("comp")
    ends = [*range(SUB), *range(rows - SUB, rows)]
    pairs = [(land_hbm, land_ref)] + [(state_ref.at[:, x, :], slabs.at[r]) for r, x in enumerate(ends)]
    get_land, *loads, surface = copies(pairs + [(state_ref.at[pl.ds(0, fields)], surface_ref)], sems, 0)
    get_land.wait()
    row_of = lax.broadcasted_iota(jnp.int32, (16, 128), 0)
    for out_ref, base, offset in ((head_ref, 0, 0), (tail_ref, SUB, rows - SUB)):
        flags = jnp.zeros((16, 128), jnp.float32)
        for r in range(SUB):
            flag = jnp.where(comp == 1, land_ref[offset + r], 1).astype(jnp.float32)
            flags = jnp.where(row_of == r, flag, flags)
        out_ref[pl.ds(SUB * depth, 16), :] = flags.astype(jnp.bfloat16)
        for r in range(SUB):
            loads[base + r].wait()
            out_ref[pl.ds(r * depth, depth), :] = slabs[base + r].astype(jnp.bfloat16)
    surface.wait()


def arrivals(cap, rows, comp, tile, dest_ref, block_ref):
    lines = dest_ref.shape[0] // 2
    dest = dest_ref[pl.ds((1 - comp) * lines, lines), :]
    both = [jnp.concatenate([block_ref[c : c + 1, pl.ds(e * 128, 128)] for e in range(lines)], axis=0) for c in range(2)]
    place = jnp.where(comp == 1, both[0], both[1])
    mine = dest == tile
    earlier = lax.broadcasted_iota(jnp.int32, (128, 128), 0)
    later = lax.broadcasted_iota(jnp.int32, (128, 128), 1)
    before = (earlier < later) & (lax.div(earlier, rows) == lax.div(later, rows))
    rank = jnp.dot(
        mine.astype(jnp.float32).astype(jnp.bfloat16),
        before.astype(jnp.float32).astype(jnp.bfloat16),
        preferred_element_type=jnp.float32,
    )
    lane = lax.broadcasted_iota(jnp.int32, (lines, 128), 1)
    offset = (place - rows).astype(jnp.float32)
    target = jnp.zeros((lines, 128), jnp.float32)
    for h in range(128 // rows):
        here = mine & (lax.div(lane, rows) == h)
        for r in range(cap):
            found = jnp.sum(jnp.where(here & (rank == r), offset, 0.0), axis=1, keepdims=True)
            target = jnp.where(lane == h * cap + r, found, target)
    return target.astype(jnp.int32) + rows


def send_kernel(cap, tiles, dest_hbm, surface_ref, weight_ref, out_ref, dest_ref, blocks, count_ref, sem):
    fields, rows, cells = surface_ref.shape
    comp, tile = lax.axis_index("comp"), lax.axis_index("tile")
    get_dest = pltpu.make_async_copy(dest_hbm, dest_ref, sem)
    get_dest.start()
    lines = surface_ref.reshape(fields * rows, cells)

    def remap(i, carry):
        for k in range(CHUNK):
            j = i * CHUNK + k
            values = lines[pl.ds(j, fields, stride=rows), :].astype(jnp.bfloat16)
            block = jnp.dot(values, weight_ref[j], preferred_element_type=jnp.float32)
            blocks[j] = block.astype(jnp.bfloat16)
        return carry

    lax.fori_loop(0, rows // CHUNK, remap, 0)

    for t in range(tiles):
        count_ref[t] = 0
    get_dest.wait()

    def place(j, carry):
        d = dest_ref[comp * (tiles * rows) + tile * rows + j]
        n = count_ref[d]
        out_ref[d * cap + n] = blocks[j]
        count_ref[d] = n + 1
        return carry

    lax.fori_loop(0, rows, place, 0, unroll=8)


def field_kernel(
    cap,
    lines_hbm,
    block_hbm,
    land_hbm,
    gain_hbm,
    state_ref,
    before_hbm,
    after_hbm,
    diffusion_hbm,
    column_hbm,
    out_ref,
    top_ref,
    target_ref,
    gain_ref,
    lines_ref,
    block_ref,
    land_ref,
    factors,
    before_ref,
    after_ref,
    diffusion_ref,
    column_ref,
    slabs,
    u0,
    u1,
    coef,
    right,
    flags,
    half0,
    half1,
    small_sems,
    in_sems,
    out_sems,
):
    depth, rows, cells = state_ref.shape
    groups = rows // GROUP
    comp, fields = lax.axis_index("comp"), top_ref.shape[1]
    inside = pl.ds(EDGE, cells)
    below = pl.ds(fields, depth - fields)

    def load(x, carry):
        pltpu.make_async_copy(state_ref.at[:, x, :], slabs.at[x], in_sems.at[lax.div(x, GROUP)]).start()
        return carry

    small = copies(
        (
            (lines_hbm, lines_ref),
            (block_hbm, block_ref),
            (diffusion_hbm, diffusion_ref),
            (column_hbm, column_ref),
            (land_hbm, land_ref),
            (gain_hbm, factors),
            (before_hbm, before_ref),
            (after_hbm, after_ref),
        ),
        small_sems,
        0,
    )
    lax.fori_loop(0, rows, load, 0, unroll=4)

    def border(x, carry):
        zeros = jnp.zeros((EDGE, depth), jnp.float32)
        for u in (u0, u1):
            u[x, pl.ds(0, EDGE), :] = zeros
            u[x, pl.ds(EDGE + cells, EDGE), :] = zeros
        return carry
    lax.fori_loop(0, u0.shape[0], border, 0, unroll=2)
    for copy in small:
        copy.wait()
    target_ref[...] = arrivals(cap, rows, comp, lax.axis_index("tile"), lines_ref, block_ref)
    field_of = lax.broadcasted_iota(jnp.int32, (fields, cells), 0)
    gain = jnp.zeros((fields, cells), jnp.float32)
    for f in range(fields):
        gain = jnp.where(field_of == f, factors[0, f], gain)
    gain_ref[...] = gain

    rate = diffusion_ref[...]
    coef[0, 0] = jnp.ones_like(coef[0, 0])
    coef[0, 1] = jnp.zeros_like(coef[0, 0])
    coef[1, 0] = jnp.broadcast_to(1.0 - 4.0 * rate, (16, depth))
    coef[1, 1] = jnp.broadcast_to(rate, (16, depth))
    column = jnp.transpose(column_ref[...])
    high = column.astype(jnp.bfloat16)
    low = (column - high.astype(jnp.float32)).astype(jnp.bfloat16)
    right[0:depth, 0:depth] = high
    right[depth : 2 * depth, 0:depth] = high
    right[0:depth, depth : 2 * depth] = low
    right[depth : 2 * depth, depth : 2 * depth] = jnp.zeros_like(low)

    def own_flag(i, carry):
        flags[i + SUB] = jnp.where(comp == 1, land_ref[i], 1)
        return carry
    lax.fori_loop(0, rows, own_flag, 0, unroll=8)
    for r in range(SUB):
        flags[r] = jnp.max(before_ref[pl.ds(SUB * depth, 16), :][r : r + 1, :].astype(jnp.float32)).astype(jnp.int32)
        flags[rows + SUB + r] = jnp.max(
            after_ref[pl.ds(SUB * depth, 16), :][r : r + 1, :].astype(jnp.float32)
        ).astype(jnp.int32)
        u0[r, inside, :] = jnp.transpose(before_ref[pl.ds(r * depth, depth), :].astype(jnp.float32))
        u0[rows + SUB + r, inside, :] = jnp.transpose(after_ref[pl.ds(r * depth, depth), :].astype(jnp.float32))
    for r in range(rows + 2 * SUB, flags.shape[0]):
        flags[r] = 0

    def wait_in(g):
        pltpu.make_async_copy(
            slabs.at[pl.ds(g * GROUP, GROUP)], slabs.at[pl.ds(g * GROUP, GROUP)], in_sems.at[g]
        ).wait()

    def turn(s):
        u0[s + SUB, inside, :] = jnp.transpose(slabs[s])

    def stencil(source, x, half):
        for side in range(GROUP):
            active = flags[x + side]
            keep, spread = coef[active, 0], coef[active, 1]
            for k in range(0, cells, 16):
                at = pl.ds(EDGE + k, 16)
                near = source[x + side - 1, at, :] + source[x + side + 1, at, :]
                near += source[x + side, pl.ds(EDGE + k - 1, 16), :] + source[x + side, pl.ds(EDGE + k + 1, 16), :]
                stepped = keep * source[x + side, at, :] + spread * near
                high = stepped.astype(jnp.bfloat16)
                half[pl.ds(side * cells + k, 16), 0:depth] = high
                half[pl.ds(side * cells + k, 16), depth : 2 * depth] = (
                    stepped - high.astype(jnp.float32)
                ).astype(jnp.bfloat16)

    def product(half, count, store):
        mixed = jnp.dot(half[0 : count * cells], right[...], preferred_element_type=jnp.float32)
        mixed = mixed[:, 0:depth] + mixed[:, depth : 2 * depth]
        for side in range(count):
            store(side, mixed[side * cells : (side + 1) * cells])

    def keep_in(target, x):
        def store(side, values):
            target[x + side, inside, :] = values
        return store

    def finish(x):
        def store(side, values):
            turned = jnp.transpose(values)
            top_ref[x + side] = turned[0:fields]
            slabs[x + side] = turned
        return store

    def send_out(x):
        for side in range(GROUP):
            pltpu.make_async_copy(
                slabs.at[x + side, below, :], out_ref.at[below, x + side, :], out_sems.at[lax.div(x, GROUP)]
            ).start()

    wait_in(0)
    wait_in(1)
    for s in range(2 * GROUP - 1):
        turn(s)
    span = 2 * GROUP
    bodies = rows // span

    stencil(u0, 1, half0)
    def body1(i, carry):
        x = 1 + span * i
        @pl.when(2 * i + 3 < groups)
        def _():
            wait_in(2 * i + 2)
            wait_in(2 * i + 3)
        product(half0, GROUP, keep_in(u1, x))
        stencil(u0, x + GROUP, half1)
        for s in range(GROUP):
            turn(jnp.minimum(span * i + span - 1 + s, rows - 1))
        product(half1, GROUP, keep_in(u1, x + GROUP))
        stencil(u0, x + span, half0)
        for s in range(GROUP, span):
            turn(jnp.minimum(span * i + span - 1 + s, rows - 1))
        return carry
    lax.fori_loop(0, bodies, body1, 0)
    product(half0, 4, keep_in(u1, rows + 1))

    stencil(u1, 2, half0)
    def body2(i, carry):
        x = 2 + span * i
        product(half0, GROUP, keep_in(u0, x))
        stencil(u1, x + GROUP, half1)
        product(half1, GROUP, keep_in(u0, x + GROUP))
        stencil(u1, x + span, half0)
        return carry
    lax.fori_loop(0, bodies, body2, 0)
    product(half0, 2, keep_in(u0, rows + 2))

    stencil(u0, SUB, half0)
    def body3(i, carry):
        x = span * i
        product(half0, GROUP, finish(x))
        stencil(u0, SUB + x + GROUP, half1)
        send_out(x)
        product(half1, GROUP, finish(x + GROUP))
        stencil(u0, SUB + x + span, half0)
        send_out(x + GROUP)
        return carry
    lax.fori_loop(0, bodies, body3, 0)

    def wait_out(i, carry):
        part = slabs.at[pl.ds(0, GROUP), below, :]
        pltpu.make_async_copy(part, part, out_sems.at[i]).wait()
        return carry
    lax.fori_loop(0, groups, wait_out, 0)


def forcing_kernel(target_hbm, gain_ref, arrived_ref, top_ref, field_ref, out_ref, target_ref, total, result, sems):
    slots, fields, _ = arrived_ref.shape
    rows, _, cells = top_ref.shape
    (get_target,) = copies(((target_hbm, target_ref),), sems, 0)

    def begin(x, carry):
        total[pl.ds(pl.multiple_of(x * fields, fields), fields), :] = top_ref[x]
        return carry

    lax.fori_loop(0, rows, begin, 0, unroll=8)
    total[pl.ds(rows * fields, fields), :] = jnp.zeros((fields, cells), jnp.float32)
    gain = gain_ref[...]
    get_target.wait()
    lines = target_ref.shape[0]
    count = slots // lines

    def add(e, carry):
        for s in range(count):
            at = pl.ds(pl.multiple_of(target_ref[e, s] * fields, fields), fields)
            total[at, :] += gain * arrived_ref[e * count + s].astype(jnp.float32)
        return carry

    lax.fori_loop(0, lines, add, 0)

    def store(i):
        part = pl.ds(i * PART, PART)
        return pltpu.make_async_copy(result.at[part], out_ref.at[part], sems.at[1 + i])

    def finish(i, carry):
        for k in range(PART):
            result[i * PART + k] = total[pl.ds(i * PART + k, rows, stride=fields), :]
        store(i).start()
        return carry

    def wait(i, carry):
        store(i).wait()
        return carry

    lax.fori_loop(0, fields // PART, finish, 0)
    lax.fori_loop(0, fields // PART, wait, 0)


def on_device(
    prognostic_state,
    remapping_weight,
    diffusion,
    column_op,
    couple_gain,
    land_mask,
    dest_tile,
    dest_block,
):
    tiles = lax.axis_size("tile")
    in_hbm = functools.partial(pltpu.with_memory_space_constraint, memory_space=pltpu.HBM)
    state = in_hbm(prognostic_state[0])
    depth, rows, cells = state.shape
    fields = couple_gain.shape[1]
    cap = max(2, 2 * rows // tiles)
    slots = tiles * cap
    halo_rows = SUB * depth + 16
    routes = in_hbm(dest_tile.reshape(-1))
    lines = tiles * rows // 128

    vmem = pl.BlockSpec(memory_space=pltpu.VMEM)
    anywhere = pl.BlockSpec(memory_space=pltpu.HBM)

    head, tail, surface = pl.pallas_call(
        halo_kernel,
        out_shape=(
            jax.ShapeDtypeStruct((halo_rows, cells), jnp.bfloat16),
            jax.ShapeDtypeStruct((halo_rows, cells), jnp.bfloat16),
            jax.ShapeDtypeStruct((fields, rows, cells), jnp.float32),
        ),
        in_specs=[anywhere] * 2,
        out_specs=(vmem, vmem, vmem),
        scratch_shapes=[
            pltpu.SMEM(land_mask.shape, jnp.int32),
            pltpu.VMEM((2 * SUB, depth, cells), jnp.float32),
            pltpu.SemaphoreType.DMA((2 + 2 * SUB,)),
        ],
        compiler_params=pltpu.CompilerParams(vmem_limit_bytes=32 << 20),
        name="boundary_rows",
    )(in_hbm(land_mask), state)

    ring = [(i, (i + 1) % tiles) for i in range(tiles)]
    before = lax.ppermute(tail, "tile", ring)
    after = lax.ppermute(head, "tile", [(b, a) for a, b in ring])

    outgoing = pl.pallas_call(
        functools.partial(send_kernel, cap, tiles),
        out_shape=jax.ShapeDtypeStruct((slots, fields, cells), jnp.bfloat16),
        in_specs=[anywhere, vmem, vmem],
        out_specs=vmem,
        scratch_shapes=[
            pltpu.SMEM(routes.shape, jnp.int32),
            pltpu.VMEM((rows, fields, cells), jnp.bfloat16),
            pltpu.SMEM((tiles,), jnp.int32),
            pltpu.SemaphoreType.DMA,
        ],
        compiler_params=pltpu.CompilerParams(vmem_limit_bytes=32 << 20),
        cost_estimate=pl.CostEstimate(
            flops=2 * rows * fields * cells * cells, bytes_accessed=8 << 20, transcendentals=0
        ),
        name="remap_and_pack",
    )(routes, surface, remapping_weight[0])
    swapped = lax.ppermute(outgoing, "comp", [(0, 1), (1, 0)])
    arrived = lax.all_to_all(swapped, "tile", split_axis=0, concat_axis=0, tiled=True)

    total_rows = rows + 2 * SUB + GROUP
    field, top, target, gain = pl.pallas_call(
        functools.partial(field_kernel, cap),
        out_shape=(
            jax.ShapeDtypeStruct((depth, rows, cells), jnp.float32),
            jax.ShapeDtypeStruct((rows, fields, cells), jnp.float32),
            jax.ShapeDtypeStruct((lines, 128), jnp.int32),
            jax.ShapeDtypeStruct((fields, cells), jnp.float32),
        ),
        in_specs=[anywhere] * 9,
        out_specs=(anywhere, vmem, vmem, vmem),
        scratch_shapes=[
            pltpu.VMEM((2 * lines, 128), jnp.int32),
            pltpu.VMEM(dest_block.shape, jnp.int32),
            pltpu.SMEM((rows,), jnp.int32),
            pltpu.SMEM(couple_gain.shape, jnp.float32),
            pltpu.VMEM((halo_rows, cells), jnp.bfloat16),
            pltpu.VMEM((halo_rows, cells), jnp.bfloat16),
            pltpu.VMEM((1, depth), jnp.float32),
            pltpu.VMEM((depth, depth), jnp.float32),
            pltpu.VMEM((rows, depth, cells), jnp.float32),
            pltpu.VMEM((total_rows, cells + 2 * EDGE, depth), jnp.float32),
            pltpu.VMEM((total_rows, cells + 2 * EDGE, depth), jnp.float32),
            pltpu.VMEM((2, 2, 16, depth), jnp.float32),
            pltpu.VMEM((2 * depth, 2 * depth), jnp.bfloat16),
            pltpu.SMEM((total_rows,), jnp.int32),
            pltpu.VMEM((GROUP * cells, 2 * depth), jnp.bfloat16),
            pltpu.VMEM((GROUP * cells, 2 * depth), jnp.bfloat16),
            pltpu.SemaphoreType.DMA((8,)),
            pltpu.SemaphoreType.DMA((rows // GROUP,)),
            pltpu.SemaphoreType.DMA((rows // GROUP,)),
        ],
        compiler_params=pltpu.CompilerParams(vmem_limit_bytes=32 << 20),
        cost_estimate=pl.CostEstimate(
            flops=120 * depth * depth * rows * cells,
            bytes_accessed=8 * depth * rows * cells,
            transcendentals=0,
        ),
        name="substeps",
    )(
        in_hbm(dest_tile.reshape(2 * lines, 128)),
        in_hbm(dest_block),
        in_hbm(land_mask),
        in_hbm(couple_gain),
        state,
        before,
        after,
        in_hbm(diffusion),
        in_hbm(column_op[0]),
    )

    new_state = pl.pallas_call(
        forcing_kernel,
        out_shape=jax.ShapeDtypeStruct((depth, rows, cells), jnp.float32),
        in_specs=[anywhere, vmem, vmem, vmem, anywhere],
        out_specs=anywhere,
        input_output_aliases={4: 0},
        scratch_shapes=[
            pltpu.SMEM((lines, 128), jnp.int32),
            pltpu.VMEM(((rows + 1) * fields, cells), jnp.float32),
            pltpu.VMEM((fields, rows, cells), jnp.float32),
            pltpu.SemaphoreType.DMA((1 + fields // PART,)),
        ],
        compiler_params=pltpu.CompilerParams(vmem_limit_bytes=32 << 20),
        name="add_forcing",
    )(target, gain, arrived, top, field)
    return new_state[None]


def solution(mesh):
    placed = (
        P("comp", "member", "tile", None),
        P("comp", "tile", None, None),
        P("comp", "member"),
        P("comp", "member", None),
        P("comp", "member"),
        P("tile"),
        P(),
        P(),
    )
    return jax.shard_map(
        on_device,
        mesh=mesh,
        in_specs=placed,
        out_specs=P("comp", "member", "tile", None),
        check_vma=False,
    )
```

```python
import functools

import jax
import jax.numpy as jnp
from jax import lax
from jax.experimental import pallas as pl
from jax.experimental.pallas import tpu as pltpu
from jax.sharding import PartitionSpec as P

SUB = 3
CHUNK = 32
GROUP = 8
EDGE = 8
PART = 4


def copies(pairs, sems, first):
    started = [pltpu.make_async_copy(a, b, sems.at[first + i]) for i, (a, b) in enumerate(pairs)]
    for copy in started:
        copy.start()
    return started


def arrivals(cap, rows, comp, tile, dest_ref, block_ref):
    lines = dest_ref.shape[0] // 2
    dest = dest_ref[pl.ds((1 - comp) * lines, lines), :]
    both = [jnp.concatenate([block_ref[c : c + 1, pl.ds(e * 128, 128)] for e in range(lines)], axis=0) for c in range(2)]
    place = jnp.where(comp == 1, both[0], both[1])
    mine = dest == tile
    earlier = lax.broadcasted_iota(jnp.int32, (128, 128), 0)
    later = lax.broadcasted_iota(jnp.int32, (128, 128), 1)
    before = (earlier < later) & (lax.div(earlier, rows) == lax.div(later, rows))
    rank = jnp.dot(
        mine.astype(jnp.float32).astype(jnp.bfloat16),
        before.astype(jnp.float32).astype(jnp.bfloat16),
        preferred_element_type=jnp.float32,
    )
    lane = lax.broadcasted_iota(jnp.int32, (lines, 128), 1)
    offset = (place - rows).astype(jnp.float32)
    target = jnp.zeros((lines, 128), jnp.float32)
    for h in range(128 // rows):
        here = mine & (lax.div(lane, rows) == h)
        for r in range(cap):
            found = jnp.sum(jnp.where(here & (rank == r), offset, 0.0), axis=1, keepdims=True)
            target = jnp.where(lane == h * cap + r, found, target)
    return target.astype(jnp.int32) + rows


def send_kernel(
    cap,
    tiles,
    dest_hbm,
    land_hbm,
    state_ref,
    weight_hbm,
    out_ref,
    head_ref,
    tail_ref,
    dest_ref,
    land_ref,
    surface,
    weights,
    slabs,
    blocks,
    count_ref,
    sems,
):
    rows, fields, cells = blocks.shape
    depth = slabs.shape[1]
    chunks = rows // CHUNK
    comp, tile = lax.axis_index("comp"), lax.axis_index("tile")
    ends = [*range(SUB), *range(rows - SUB, rows)]
    parts = [pl.ds(i * CHUNK, CHUNK) for i in range(chunks)]
    pairs = [
        (land_hbm, land_ref),
        (dest_hbm, dest_ref),
        (state_ref.at[pl.ds(0, fields)], surface.reshape(fields, rows, cells)),
        (weight_hbm.at[parts[0]], weights.at[parts[0]]),
    ]
    pairs += [(state_ref.at[:, x, :], slabs.at[r]) for r, x in enumerate(ends)]
    pairs += [(weight_hbm.at[part], weights.at[part]) for part in parts[1:]]
    get_land, get_dest, get_surface, first, *others = copies(pairs, sems, 0)
    loads, get_weight = others[: 2 * SUB], [first, *others[2 * SUB :]]

    get_land.wait()
    row_of = lax.broadcasted_iota(jnp.int32, (16, 128), 0)
    for ref, offset in ((head_ref, 0), (tail_ref, rows - SUB)):
        flags = jnp.zeros((16, 128), jnp.float32)
        for r in range(SUB):
            flag = jnp.where(comp == 1, land_ref[offset + r], 1).astype(jnp.float32)
            flags = jnp.where(row_of == r, flag, flags)
        ref[pl.ds(SUB * depth, 16), :] = flags.astype(jnp.bfloat16)
    for t in range(tiles):
        count_ref[t] = 0

    def remap(i, carry):
        for k in range(CHUNK):
            j = i * CHUNK + k
            values = surface[pl.ds(j, fields, stride=rows), :].astype(jnp.bfloat16)
            block = jnp.dot(values, weights[j], preferred_element_type=jnp.float32)
            blocks[j] = block.astype(jnp.bfloat16)
        return carry

    def place(j, carry):
        d = dest_ref[comp * (tiles * rows) + tile * rows + j]
        n = count_ref[d]
        out_ref[d * cap + n] = blocks[j]
        count_ref[d] = n + 1
        return carry

    def round_row(r, carry):
        @pl.when(r < SUB)
        def _():
            head_ref[pl.ds(pl.multiple_of(r * depth, depth), depth), :] = slabs[r].astype(jnp.bfloat16)

        @pl.when(r >= SUB)
        def _():
            at = pl.ds(pl.multiple_of((r - SUB) * depth, depth), depth)
            tail_ref[at, :] = slabs[r].astype(jnp.bfloat16)

        return carry

    get_surface.wait()

    def chunk(i, carry):
        pltpu.make_async_copy(weight_hbm.at[parts[0]], weights.at[parts[0]], weight_sem(i)).wait()
        return remap(i, carry)

    def weight_sem(i):
        return sems.at[jnp.where(i == 0, 3, 3 + 2 * SUB + i)]

    lax.fori_loop(0, chunks, chunk, 0)
    for copy in loads:
        copy.wait()
    lax.fori_loop(0, 2 * SUB, round_row, 0)
    get_dest.wait()
    lax.fori_loop(0, rows, place, 0, unroll=8)


def field_kernel(
    cap,
    lines_hbm,
    block_hbm,
    land_hbm,
    gain_hbm,
    state_ref,
    before_hbm,
    after_hbm,
    diffusion_hbm,
    column_hbm,
    out_ref,
    top_ref,
    target_ref,
    gain_ref,
    lines_ref,
    block_ref,
    land_ref,
    factors,
    before_ref,
    after_ref,
    diffusion_ref,
    column_ref,
    slabs,
    u0,
    u1,
    coef,
    right,
    flags,
    half0,
    half1,
    small_sems,
    in_sems,
    out_sems,
):
    depth, rows, cells = state_ref.shape
    groups = rows // GROUP
    comp, fields = lax.axis_index("comp"), top_ref.shape[1]
    inside = pl.ds(EDGE, cells)
    below = pl.ds(fields, depth - fields)

    def load(x, carry):
        pltpu.make_async_copy(state_ref.at[:, x, :], slabs.at[x], in_sems.at[lax.div(x, GROUP)]).start()
        return carry

    small = copies(
        (
            (lines_hbm, lines_ref),
            (block_hbm, block_ref),
            (diffusion_hbm, diffusion_ref),
            (column_hbm, column_ref),
            (land_hbm, land_ref),
            (gain_hbm, factors),
            (before_hbm, before_ref),
            (after_hbm, after_ref),
        ),
        small_sems,
        0,
    )
    lax.fori_loop(0, rows, load, 0, unroll=4)

    def border(x, carry):
        zeros = jnp.zeros((EDGE, depth), jnp.float32)
        for u in (u0, u1):
            u[x, pl.ds(0, EDGE), :] = zeros
            u[x, pl.ds(EDGE + cells, EDGE), :] = zeros
        return carry
    lax.fori_loop(0, u0.shape[0], border, 0, unroll=2)
    for copy in small:
        copy.wait()
    target_ref[...] = arrivals(cap, rows, comp, lax.axis_index("tile"), lines_ref, block_ref)
    field_of = lax.broadcasted_iota(jnp.int32, (fields, cells), 0)
    gain = jnp.zeros((fields, cells), jnp.float32)
    for f in range(fields):
        gain = jnp.where(field_of == f, factors[0, f], gain)
    gain_ref[...] = gain

    rate = diffusion_ref[...]
    coef[0, 0] = jnp.ones_like(coef[0, 0])
    coef[0, 1] = jnp.zeros_like(coef[0, 0])
    coef[1, 0] = jnp.broadcast_to(1.0 - 4.0 * rate, (16, depth))
    coef[1, 1] = jnp.broadcast_to(rate, (16, depth))
    column = jnp.transpose(column_ref[...])
    high = column.astype(jnp.bfloat16)
    low = (column - high.astype(jnp.float32)).astype(jnp.bfloat16)
    right[0:depth, 0:depth] = high
    right[depth : 2 * depth, 0:depth] = high
    right[0:depth, depth : 2 * depth] = low
    right[depth : 2 * depth, depth : 2 * depth] = jnp.zeros_like(low)

    def own_flag(i, carry):
        flags[i + SUB] = jnp.where(comp == 1, land_ref[i], 1)
        return carry
    lax.fori_loop(0, rows, own_flag, 0, unroll=8)
    for r in range(SUB):
        flags[r] = jnp.max(before_ref[pl.ds(SUB * depth, 16), :][r : r + 1, :].astype(jnp.float32)).astype(jnp.int32)
        flags[rows + SUB + r] = jnp.max(
            after_ref[pl.ds(SUB * depth, 16), :][r : r + 1, :].astype(jnp.float32)
        ).astype(jnp.int32)
        u0[r, inside, :] = jnp.transpose(before_ref[pl.ds(r * depth, depth), :].astype(jnp.float32))
        u0[rows + SUB + r, inside, :] = jnp.transpose(after_ref[pl.ds(r * depth, depth), :].astype(jnp.float32))
    for r in range(rows + 2 * SUB, flags.shape[0]):
        flags[r] = 0

    def wait_in(g):
        pltpu.make_async_copy(
            slabs.at[pl.ds(g * GROUP, GROUP)], slabs.at[pl.ds(g * GROUP, GROUP)], in_sems.at[g]
        ).wait()

    def turn(s):
        u0[s + SUB, inside, :] = jnp.transpose(slabs[s])

    def stencil(source, x, half):
        for side in range(GROUP):
            active = flags[x + side]
            keep, spread = coef[active, 0], coef[active, 1]
            for k in range(0, cells, 16):
                at = pl.ds(EDGE + k, 16)
                near = source[x + side - 1, at, :] + source[x + side + 1, at, :]
                near += source[x + side, pl.ds(EDGE + k - 1, 16), :] + source[x + side, pl.ds(EDGE + k + 1, 16), :]
                stepped = keep * source[x + side, at, :] + spread * near
                high = stepped.astype(jnp.bfloat16)
                half[pl.ds(side * cells + k, 16), 0:depth] = high
                half[pl.ds(side * cells + k, 16), depth : 2 * depth] = (
                    stepped - high.astype(jnp.float32)
                ).astype(jnp.bfloat16)

    def product(half, count, store):
        mixed = jnp.dot(half[0 : count * cells], right[...], preferred_element_type=jnp.float32)
        mixed = mixed[:, 0:depth] + mixed[:, depth : 2 * depth]
        for side in range(count):
            store(side, mixed[side * cells : (side + 1) * cells])

    def keep_in(target, x):
        def store(side, values):
            target[x + side, inside, :] = values
        return store

    def finish(x):
        def store(side, values):
            turned = jnp.transpose(values)
            top_ref[x + side] = turned[0:fields]
            slabs[x + side] = turned
        return store

    def send_out(x):
        for side in range(GROUP):
            pltpu.make_async_copy(
                slabs.at[x + side, below, :], out_ref.at[below, x + side, :], out_sems.at[lax.div(x, GROUP)]
            ).start()

    wait_in(0)
    wait_in(1)
    for s in range(2 * GROUP - 1):
        turn(s)
    span = 2 * GROUP
    bodies = rows // span

    stencil(u0, 1, half0)
    def body1(i, carry):
        x = 1 + span * i
        @pl.when(2 * i + 3 < groups)
        def _():
            wait_in(2 * i + 2)
            wait_in(2 * i + 3)
        product(half0, GROUP, keep_in(u1, x))
        stencil(u0, x + GROUP, half1)
        for s in range(GROUP):
            turn(jnp.minimum(span * i + span - 1 + s, rows - 1))
        product(half1, GROUP, keep_in(u1, x + GROUP))
        stencil(u0, x + span, half0)
        for s in range(GROUP, span):
            turn(jnp.minimum(span * i + span - 1 + s, rows - 1))
        return carry
    lax.fori_loop(0, bodies, body1, 0)
    product(half0, 4, keep_in(u1, rows + 1))

    stencil(u1, 2, half0)
    def body2(i, carry):
        x = 2 + span * i
        product(half0, GROUP, keep_in(u0, x))
        stencil(u1, x + GROUP, half1)
        product(half1, GROUP, keep_in(u0, x + GROUP))
        stencil(u1, x + span, half0)
        return carry
    lax.fori_loop(0, bodies, body2, 0)
    product(half0, 2, keep_in(u0, rows + 2))

    stencil(u0, SUB, half0)
    def body3(i, carry):
        x = span * i
        product(half0, GROUP, finish(x))
        stencil(u0, SUB + x + GROUP, half1)
        send_out(x)
        product(half1, GROUP, finish(x + GROUP))
        stencil(u0, SUB + x + span, half0)
        send_out(x + GROUP)
        return carry
    lax.fori_loop(0, bodies, body3, 0)

    def wait_out(i, carry):
        part = slabs.at[pl.ds(0, GROUP), below, :]
        pltpu.make_async_copy(part, part, out_sems.at[i]).wait()
        return carry
    lax.fori_loop(0, groups, wait_out, 0)


def forcing_kernel(target_hbm, gain_ref, arrived_ref, top_ref, field_ref, out_ref, target_ref, total, result, sems):
    slots, fields, _ = arrived_ref.shape
    rows, _, cells = top_ref.shape
    (get_target,) = copies(((target_hbm, target_ref),), sems, 0)

    def begin(x, carry):
        total[pl.ds(pl.multiple_of(x * fields, fields), fields), :] = top_ref[x]
        return carry

    lax.fori_loop(0, rows, begin, 0, unroll=8)
    total[pl.ds(rows * fields, fields), :] = jnp.zeros((fields, cells), jnp.float32)
    gain = gain_ref[...]
    get_target.wait()
    lines = target_ref.shape[0]
    count = slots // lines

    def add(e, carry):
        for s in range(count):
            at = pl.ds(pl.multiple_of(target_ref[e, s] * fields, fields), fields)
            total[at, :] += gain * arrived_ref[e * count + s].astype(jnp.float32)
        return carry

    lax.fori_loop(0, lines, add, 0)

    def store(i):
        part = pl.ds(i * PART, PART)
        return pltpu.make_async_copy(result.at[part], out_ref.at[part], sems.at[1 + i])

    def finish(i, carry):
        for k in range(PART):
            result[i * PART + k] = total[pl.ds(i * PART + k, rows, stride=fields), :]
        store(i).start()
        return carry

    def wait(i, carry):
        store(i).wait()
        return carry

    lax.fori_loop(0, fields // PART, finish, 0)
    lax.fori_loop(0, fields // PART, wait, 0)


def on_device(
    prognostic_state,
    remapping_weight,
    diffusion,
    column_op,
    couple_gain,
    land_mask,
    dest_tile,
    dest_block,
):
    tiles = lax.axis_size("tile")
    in_hbm = functools.partial(pltpu.with_memory_space_constraint, memory_space=pltpu.HBM)
    state = in_hbm(prognostic_state[0])
    depth, rows, cells = state.shape
    fields = couple_gain.shape[1]
    cap = max(2, 2 * rows // tiles)
    slots = tiles * cap
    halo_rows = SUB * depth + 16
    routes = in_hbm(dest_tile.reshape(-1))
    lines = tiles * rows // 128

    vmem = pl.BlockSpec(memory_space=pltpu.VMEM)
    anywhere = pl.BlockSpec(memory_space=pltpu.HBM)

    outgoing, head, tail = pl.pallas_call(
        functools.partial(send_kernel, cap, tiles),
        out_shape=(
            jax.ShapeDtypeStruct((slots, fields, cells), jnp.bfloat16),
            jax.ShapeDtypeStruct((halo_rows, cells), jnp.bfloat16),
            jax.ShapeDtypeStruct((halo_rows, cells), jnp.bfloat16),
        ),
        in_specs=[anywhere] * 4,
        out_specs=(vmem, vmem, vmem),
        scratch_shapes=[
            pltpu.SMEM(routes.shape, jnp.int32),
            pltpu.SMEM(land_mask.shape, jnp.int32),
            pltpu.VMEM((fields * rows, cells), jnp.float32),
            pltpu.VMEM((rows, cells, cells), jnp.bfloat16),
            pltpu.VMEM((2 * SUB, depth, cells), jnp.float32),
            pltpu.VMEM((rows, fields, cells), jnp.bfloat16),
            pltpu.SMEM((tiles,), jnp.int32),
            pltpu.SemaphoreType.DMA((3 + 2 * SUB + rows // CHUNK,)),
        ],
        compiler_params=pltpu.CompilerParams(vmem_limit_bytes=32 << 20),
        cost_estimate=pl.CostEstimate(
            flops=2 * rows * fields * cells * cells, bytes_accessed=8 << 20, transcendentals=0
        ),
        name="remap_and_pack",
    )(routes, in_hbm(land_mask), state, in_hbm(remapping_weight[0]))

    ring = [(i, (i + 1) % tiles) for i in range(tiles)]
    before = lax.ppermute(tail, "tile", ring)
    after = lax.ppermute(head, "tile", [(b, a) for a, b in ring])

    swapped = lax.ppermute(outgoing, "comp", [(0, 1), (1, 0)])
    arrived = lax.all_to_all(swapped, "tile", split_axis=0, concat_axis=0, tiled=True)

    total_rows = rows + 2 * SUB + GROUP
    field, top, target, gain = pl.pallas_call(
        functools.partial(field_kernel, cap),
        out_shape=(
            jax.ShapeDtypeStruct((depth, rows, cells), jnp.float32),
            jax.ShapeDtypeStruct((rows, fields, cells), jnp.float32),
            jax.ShapeDtypeStruct((lines, 128), jnp.int32),
            jax.ShapeDtypeStruct((fields, cells), jnp.float32),
        ),
        in_specs=[anywhere] * 9,
        out_specs=(anywhere, vmem, vmem, vmem),
        scratch_shapes=[
            pltpu.VMEM((2 * lines, 128), jnp.int32),
            pltpu.VMEM(dest_block.shape, jnp.int32),
            pltpu.SMEM((rows,), jnp.int32),
            pltpu.SMEM(couple_gain.shape, jnp.float32),
            pltpu.VMEM((halo_rows, cells), jnp.bfloat16),
            pltpu.VMEM((halo_rows, cells), jnp.bfloat16),
            pltpu.VMEM((1, depth), jnp.float32),
            pltpu.VMEM((depth, depth), jnp.float32),
            pltpu.VMEM((rows, depth, cells), jnp.float32),
            pltpu.VMEM((total_rows, cells + 2 * EDGE, depth), jnp.float32),
            pltpu.VMEM((total_rows, cells + 2 * EDGE, depth), jnp.float32),
            pltpu.VMEM((2, 2, 16, depth), jnp.float32),
            pltpu.VMEM((2 * depth, 2 * depth), jnp.bfloat16),
            pltpu.SMEM((total_rows,), jnp.int32),
            pltpu.VMEM((GROUP * cells, 2 * depth), jnp.bfloat16),
            pltpu.VMEM((GROUP * cells, 2 * depth), jnp.bfloat16),
            pltpu.SemaphoreType.DMA((8,)),
            pltpu.SemaphoreType.DMA((rows // GROUP,)),
            pltpu.SemaphoreType.DMA((rows // GROUP,)),
        ],
        compiler_params=pltpu.CompilerParams(vmem_limit_bytes=32 << 20),
        cost_estimate=pl.CostEstimate(
            flops=120 * depth * depth * rows * cells,
            bytes_accessed=8 * depth * rows * cells,
            transcendentals=0,
        ),
        name="substeps",
    )(
        in_hbm(dest_tile.reshape(2 * lines, 128)),
        in_hbm(dest_block),
        in_hbm(land_mask),
        in_hbm(couple_gain),
        state,
        before,
        after,
        in_hbm(diffusion),
        in_hbm(column_op[0]),
    )

    new_state = pl.pallas_call(
        forcing_kernel,
        out_shape=jax.ShapeDtypeStruct((depth, rows, cells), jnp.float32),
        in_specs=[anywhere, vmem, vmem, vmem, anywhere],
        out_specs=anywhere,
        input_output_aliases={4: 0},
        scratch_shapes=[
            pltpu.SMEM((lines, 128), jnp.int32),
            pltpu.VMEM(((rows + 1) * fields, cells), jnp.float32),
            pltpu.VMEM((fields, rows, cells), jnp.float32),
            pltpu.SemaphoreType.DMA((1 + fields // PART,)),
        ],
        compiler_params=pltpu.CompilerParams(vmem_limit_bytes=32 << 20),
        name="add_forcing",
    )(target, gain, arrived, top, field)
    return new_state[None]


def solution(mesh):
    placed = (
        P("comp", "member", "tile", None),
        P("comp", "tile", None, None),
        P("comp", "member"),
        P("comp", "member", None),
        P("comp", "member"),
        P("tile"),
        P(),
        P(),
    )
    return jax.shard_map(
        on_device,
        mesh=mesh,
        in_specs=placed,
        out_specs=P("comp", "member", "tile", None),
        check_vma=False,
    )
```

```python
import functools

import jax
import jax.numpy as jnp
from jax import lax
from jax.experimental import pallas as pl
from jax.experimental.pallas import tpu as pltpu
from jax.sharding import PartitionSpec as P

SUB = 3
CHUNK = 32
GROUP = 8
EDGE = 8
PART = 4


def copies(pairs, sems, first):
    started = [pltpu.make_async_copy(a, b, sems.at[first + i]) for i, (a, b) in enumerate(pairs)]
    for copy in started:
        copy.start()
    return started


def arrivals(cap, rows, comp, tile, dest_ref, block_ref):
    lines = dest_ref.shape[0] // 2
    dest = dest_ref[pl.ds((1 - comp) * lines, lines), :]
    both = [jnp.concatenate([block_ref[c : c + 1, pl.ds(e * 128, 128)] for e in range(lines)], axis=0) for c in range(2)]
    place = jnp.where(comp == 1, both[0], both[1])
    mine = dest == tile
    earlier = lax.broadcasted_iota(jnp.int32, (128, 128), 0)
    later = lax.broadcasted_iota(jnp.int32, (128, 128), 1)
    before = (earlier < later) & (lax.div(earlier, rows) == lax.div(later, rows))
    rank = jnp.dot(
        mine.astype(jnp.float32).astype(jnp.bfloat16),
        before.astype(jnp.float32).astype(jnp.bfloat16),
        preferred_element_type=jnp.float32,
    )
    lane = lax.broadcasted_iota(jnp.int32, (lines, 128), 1)
    offset = (place - rows).astype(jnp.float32)
    target = jnp.zeros((lines, 128), jnp.float32)
    for h in range(128 // rows):
        here = mine & (lax.div(lane, rows) == h)
        for r in range(cap):
            found = jnp.sum(jnp.where(here & (rank == r), offset, 0.0), axis=1, keepdims=True)
            target = jnp.where(lane == h * cap + r, found, target)
    return target.astype(jnp.int32) + rows


def send_kernel(
    cap,
    tiles,
    dest_hbm,
    land_hbm,
    state_ref,
    weight_hbm,
    out_ref,
    head_ref,
    tail_ref,
    dest_ref,
    land_ref,
    surface,
    weights,
    slabs,
    blocks,
    count_ref,
    sems,
):
    rows, fields, cells = blocks.shape
    depth = slabs.shape[1]
    chunks = rows // CHUNK
    comp, tile = lax.axis_index("comp"), lax.axis_index("tile")
    ends = [*range(SUB), *range(rows - SUB, rows)]
    parts = [pl.ds(i * CHUNK, CHUNK) for i in range(chunks)]
    pairs = [
        (land_hbm, land_ref),
        (dest_hbm, dest_ref),
        (state_ref.at[pl.ds(0, fields)], surface.reshape(fields, rows, cells)),
        (weight_hbm.at[parts[0]], weights.at[parts[0]]),
    ]
    pairs += [(state_ref.at[:, x, :], slabs.at[r]) for r, x in enumerate(ends)]
    pairs += [(weight_hbm.at[part], weights.at[part]) for part in parts[1:]]
    get_land, get_dest, get_surface, first, *others = copies(pairs, sems, 0)
    loads, get_weight = others[: 2 * SUB], [first, *others[2 * SUB :]]

    get_land.wait()
    row_of = lax.broadcasted_iota(jnp.int32, (16, 128), 0)
    for ref, offset in ((head_ref, 0), (tail_ref, rows - SUB)):
        flags = jnp.zeros((16, 128), jnp.float32)
        for r in range(SUB):
            flag = jnp.where(comp == 1, land_ref[offset + r], 1).astype(jnp.float32)
            flags = jnp.where(row_of == r, flag, flags)
        ref[pl.ds(SUB * depth, 16), :] = flags.astype(jnp.bfloat16)
    for t in range(tiles):
        count_ref[t] = 0

    def remap(i, carry):
        for k in range(CHUNK):
            j = i * CHUNK + k
            values = surface[pl.ds(j, fields, stride=rows), :].astype(jnp.bfloat16)
            block = jnp.dot(values, weights[j], preferred_element_type=jnp.float32)
            blocks[j] = block.astype(jnp.bfloat16)
        return carry

    def place(j, carry):
        d = dest_ref[comp * (tiles * rows) + tile * rows + j]
        n = count_ref[d]
        out_ref[d * cap + n] = blocks[j]
        count_ref[d] = n + 1
        return carry

    def round_row(r, carry):
        @pl.when(r < SUB)
        def _():
            head_ref[pl.ds(pl.multiple_of(r * depth, depth), depth), :] = slabs[r].astype(jnp.bfloat16)

        @pl.when(r >= SUB)
        def _():
            at = pl.ds(pl.multiple_of((r - SUB) * depth, depth), depth)
            tail_ref[at, :] = slabs[r].astype(jnp.bfloat16)

        return carry

    get_surface.wait()

    def weight_sem(i):
        return sems.at[jnp.where(i == 0, 3, 3 + 2 * SUB + i)]

    get_dest.wait()

    def chunk(i, carry):
        pltpu.make_async_copy(weight_hbm.at[parts[0]], weights.at[parts[0]], weight_sem(i)).wait()
        remap(i, carry)
        lax.fori_loop(0, CHUNK, lambda k, c: place(i * CHUNK + k, c), 0, unroll=8)

        @pl.when(i == 0)
        def _():
            for copy in loads:
                copy.wait()
            lax.fori_loop(0, 2 * SUB, round_row, 0)

        return carry

    lax.fori_loop(0, chunks, chunk, 0)


def field_kernel(
    cap,
    lines_hbm,
    block_hbm,
    land_hbm,
    gain_hbm,
    state_ref,
    before_hbm,
    after_hbm,
    diffusion_hbm,
    column_hbm,
    out_ref,
    top_ref,
    target_ref,
    gain_ref,
    lines_ref,
    block_ref,
    land_ref,
    factors,
    before_ref,
    after_ref,
    diffusion_ref,
    column_ref,
    slabs,
    u0,
    u1,
    coef,
    right,
    flags,
    half0,
    half1,
    small_sems,
    in_sems,
    out_sems,
):
    depth, rows, cells = state_ref.shape
    groups = rows // GROUP
    comp, fields = lax.axis_index("comp"), top_ref.shape[1]
    inside = pl.ds(EDGE, cells)
    below = pl.ds(fields, depth - fields)

    def load(x, carry):
        pltpu.make_async_copy(state_ref.at[:, x, :], slabs.at[x], in_sems.at[lax.div(x, GROUP)]).start()
        return carry

    small = copies(
        (
            (lines_hbm, lines_ref),
            (block_hbm, block_ref),
            (diffusion_hbm, diffusion_ref),
            (column_hbm, column_ref),
            (land_hbm, land_ref),
            (gain_hbm, factors),
            (before_hbm, before_ref),
            (after_hbm, after_ref),
        ),
        small_sems,
        0,
    )
    lax.fori_loop(0, rows, load, 0, unroll=4)

    def border(x, carry):
        zeros = jnp.zeros((EDGE, depth), jnp.float32)
        for u in (u0, u1):
            u[x, pl.ds(0, EDGE), :] = zeros
            u[x, pl.ds(EDGE + cells, EDGE), :] = zeros
        return carry
    lax.fori_loop(0, u0.shape[0], border, 0, unroll=2)
    for copy in small:
        copy.wait()
    target_ref[...] = arrivals(cap, rows, comp, lax.axis_index("tile"), lines_ref, block_ref)
    field_of = lax.broadcasted_iota(jnp.int32, (fields, cells), 0)
    gain = jnp.zeros((fields, cells), jnp.float32)
    for f in range(fields):
        gain = jnp.where(field_of == f, factors[0, f], gain)
    gain_ref[...] = gain

    rate = diffusion_ref[...]
    coef[0, 0] = jnp.ones_like(coef[0, 0])
    coef[0, 1] = jnp.zeros_like(coef[0, 0])
    coef[1, 0] = jnp.broadcast_to(1.0 - 4.0 * rate, (16, depth))
    coef[1, 1] = jnp.broadcast_to(rate, (16, depth))
    column = jnp.transpose(column_ref[...])
    high = column.astype(jnp.bfloat16)
    low = (column - high.astype(jnp.float32)).astype(jnp.bfloat16)
    right[0:depth, 0:depth] = high
    right[depth : 2 * depth, 0:depth] = high
    right[0:depth, depth : 2 * depth] = low
    right[depth : 2 * depth, depth : 2 * depth] = jnp.zeros_like(low)

    def own_flag(i, carry):
        flags[i + SUB] = jnp.where(comp == 1, land_ref[i], 1)
        return carry
    lax.fori_loop(0, rows, own_flag, 0, unroll=8)
    for r in range(SUB):
        flags[r] = jnp.max(before_ref[pl.ds(SUB * depth, 16), :][r : r + 1, :].astype(jnp.float32)).astype(jnp.int32)
        flags[rows + SUB + r] = jnp.max(
            after_ref[pl.ds(SUB * depth, 16), :][r : r + 1, :].astype(jnp.float32)
        ).astype(jnp.int32)
        u0[r, inside, :] = jnp.transpose(before_ref[pl.ds(r * depth, depth), :].astype(jnp.float32))
        u0[rows + SUB + r, inside, :] = jnp.transpose(after_ref[pl.ds(r * depth, depth), :].astype(jnp.float32))
    for r in range(rows + 2 * SUB, flags.shape[0]):
        flags[r] = 0

    def wait_in(g):
        pltpu.make_async_copy(
            slabs.at[pl.ds(g * GROUP, GROUP)], slabs.at[pl.ds(g * GROUP, GROUP)], in_sems.at[g]
        ).wait()

    def turn(s):
        u0[s + SUB, inside, :] = jnp.transpose(slabs[s])

    def stencil(source, x, half):
        for side in range(GROUP):
            active = flags[x + side]
            keep, spread = coef[active, 0], coef[active, 1]
            for k in range(0, cells, 16):
                at = pl.ds(EDGE + k, 16)
                near = source[x + side - 1, at, :] + source[x + side + 1, at, :]
                near += source[x + side, pl.ds(EDGE + k - 1, 16), :] + source[x + side, pl.ds(EDGE + k + 1, 16), :]
                stepped = keep * source[x + side, at, :] + spread * near
                high = stepped.astype(jnp.bfloat16)
                half[pl.ds(side * cells + k, 16), 0:depth] = high
                half[pl.ds(side * cells + k, 16), depth : 2 * depth] = (
                    stepped - high.astype(jnp.float32)
                ).astype(jnp.bfloat16)

    def product(half, count, store):
        mixed = jnp.dot(half[0 : count * cells], right[...], preferred_element_type=jnp.float32)
        mixed = mixed[:, 0:depth] + mixed[:, depth : 2 * depth]
        for side in range(count):
            store(side, mixed[side * cells : (side + 1) * cells])

    def keep_in(target, x):
        def store(side, values):
            target[x + side, inside, :] = values
        return store

    def finish(x):
        def store(side, values):
            turned = jnp.transpose(values)
            top_ref[x + side] = turned[0:fields]
            slabs[x + side] = turned
        return store

    def send_out(x):
        for side in range(GROUP):
            pltpu.make_async_copy(
                slabs.at[x + side, below, :], out_ref.at[below, x + side, :], out_sems.at[lax.div(x, GROUP)]
            ).start()

    wait_in(0)
    wait_in(1)
    for s in range(2 * GROUP - 1):
        turn(s)
    span = 2 * GROUP
    bodies = rows // span

    stencil(u0, 1, half0)
    def body1(i, carry):
        x = 1 + span * i
        @pl.when(2 * i + 3 < groups)
        def _():
            wait_in(2 * i + 2)
            wait_in(2 * i + 3)
        product(half0, GROUP, keep_in(u1, x))
        stencil(u0, x + GROUP, half1)
        for s in range(GROUP):
            turn(jnp.minimum(span * i + span - 1 + s, rows - 1))
        product(half1, GROUP, keep_in(u1, x + GROUP))
        stencil(u0, x + span, half0)
        for s in range(GROUP, span):
            turn(jnp.minimum(span * i + span - 1 + s, rows - 1))
        return carry
    lax.fori_loop(0, bodies, body1, 0)
    product(half0, 4, keep_in(u1, rows + 1))

    stencil(u1, 2, half0)
    def body2(i, carry):
        x = 2 + span * i
        product(half0, GROUP, keep_in(u0, x))
        stencil(u1, x + GROUP, half1)
        product(half1, GROUP, keep_in(u0, x + GROUP))
        stencil(u1, x + span, half0)
        return carry
    lax.fori_loop(0, bodies, body2, 0)
    product(half0, 2, keep_in(u0, rows + 2))

    stencil(u0, SUB, half0)
    def body3(i, carry):
        x = span * i
        product(half0, GROUP, finish(x))
        stencil(u0, SUB + x + GROUP, half1)
        send_out(x)
        product(half1, GROUP, finish(x + GROUP))
        stencil(u0, SUB + x + span, half0)
        send_out(x + GROUP)
        return carry
    lax.fori_loop(0, bodies, body3, 0)

    def wait_out(i, carry):
        part = slabs.at[pl.ds(0, GROUP), below, :]
        pltpu.make_async_copy(part, part, out_sems.at[i]).wait()
        return carry
    lax.fori_loop(0, groups, wait_out, 0)


def forcing_kernel(target_hbm, gain_ref, arrived_ref, top_ref, field_ref, out_ref, target_ref, total, result, sems):
    slots, fields, _ = arrived_ref.shape
    rows, _, cells = top_ref.shape
    (get_target,) = copies(((target_hbm, target_ref),), sems, 0)

    def begin(x, carry):
        total[pl.ds(pl.multiple_of(x * fields, fields), fields), :] = top_ref[x]
        return carry

    lax.fori_loop(0, rows, begin, 0, unroll=8)
    total[pl.ds(rows * fields, fields), :] = jnp.zeros((fields, cells), jnp.float32)
    gain = gain_ref[...]
    get_target.wait()
    lines = target_ref.shape[0]
    count = slots // lines

    def add(e, carry):
        for s in range(count):
            at = pl.ds(pl.multiple_of(target_ref[e, s] * fields, fields), fields)
            total[at, :] += gain * arrived_ref[e * count + s].astype(jnp.float32)
        return carry

    lax.fori_loop(0, lines, add, 0)

    def store(i):
        part = pl.ds(i * PART, PART)
        return pltpu.make_async_copy(result.at[part], out_ref.at[part], sems.at[1 + i])

    def finish(i, carry):
        for k in range(PART):
            result[i * PART + k] = total[pl.ds(i * PART + k, rows, stride=fields), :]
        store(i).start()
        return carry

    def wait(i, carry):
        store(i).wait()
        return carry

    lax.fori_loop(0, fields // PART, finish, 0)
    lax.fori_loop(0, fields // PART, wait, 0)


def on_device(
    prognostic_state,
    remapping_weight,
    diffusion,
    column_op,
    couple_gain,
    land_mask,
    dest_tile,
    dest_block,
):
    tiles = lax.axis_size("tile")
    in_hbm = functools.partial(pltpu.with_memory_space_constraint, memory_space=pltpu.HBM)
    state = in_hbm(prognostic_state[0])
    depth, rows, cells = state.shape
    fields = couple_gain.shape[1]
    cap = max(2, 2 * rows // tiles)
    slots = tiles * cap
    halo_rows = SUB * depth + 16
    routes = in_hbm(dest_tile.reshape(-1))
    lines = tiles * rows // 128

    vmem = pl.BlockSpec(memory_space=pltpu.VMEM)
    anywhere = pl.BlockSpec(memory_space=pltpu.HBM)

    outgoing, head, tail = pl.pallas_call(
        functools.partial(send_kernel, cap, tiles),
        out_shape=(
            jax.ShapeDtypeStruct((slots, fields, cells), jnp.bfloat16),
            jax.ShapeDtypeStruct((halo_rows, cells), jnp.bfloat16),
            jax.ShapeDtypeStruct((halo_rows, cells), jnp.bfloat16),
        ),
        in_specs=[anywhere] * 4,
        out_specs=(vmem, vmem, vmem),
        scratch_shapes=[
            pltpu.SMEM(routes.shape, jnp.int32),
            pltpu.SMEM(land_mask.shape, jnp.int32),
            pltpu.VMEM((fields * rows, cells), jnp.float32),
            pltpu.VMEM((rows, cells, cells), jnp.bfloat16),
            pltpu.VMEM((2 * SUB, depth, cells), jnp.float32),
            pltpu.VMEM((rows, fields, cells), jnp.bfloat16),
            pltpu.SMEM((tiles,), jnp.int32),
            pltpu.SemaphoreType.DMA((3 + 2 * SUB + rows // CHUNK,)),
        ],
        compiler_params=pltpu.CompilerParams(vmem_limit_bytes=32 << 20),
        cost_estimate=pl.CostEstimate(
            flops=2 * rows * fields * cells * cells, bytes_accessed=8 << 20, transcendentals=0
        ),
        name="remap_and_pack",
    )(routes, in_hbm(land_mask), state, in_hbm(remapping_weight[0]))

    ring = [(i, (i + 1) % tiles) for i in range(tiles)]
    before = lax.ppermute(tail, "tile", ring)
    after = lax.ppermute(head, "tile", [(b, a) for a, b in ring])

    swapped = lax.ppermute(outgoing, "comp", [(0, 1), (1, 0)])
    arrived = lax.all_to_all(swapped, "tile", split_axis=0, concat_axis=0, tiled=True)

    total_rows = rows + 2 * SUB + GROUP
    field, top, target, gain = pl.pallas_call(
        functools.partial(field_kernel, cap),
        out_shape=(
            jax.ShapeDtypeStruct((depth, rows, cells), jnp.float32),
            jax.ShapeDtypeStruct((rows, fields, cells), jnp.float32),
            jax.ShapeDtypeStruct((lines, 128), jnp.int32),
            jax.ShapeDtypeStruct((fields, cells), jnp.float32),
        ),
        in_specs=[anywhere] * 9,
        out_specs=(anywhere, vmem, vmem, vmem),
        scratch_shapes=[
            pltpu.VMEM((2 * lines, 128), jnp.int32),
            pltpu.VMEM(dest_block.shape, jnp.int32),
            pltpu.SMEM((rows,), jnp.int32),
            pltpu.SMEM(couple_gain.shape, jnp.float32),
            pltpu.VMEM((halo_rows, cells), jnp.bfloat16),
            pltpu.VMEM((halo_rows, cells), jnp.bfloat16),
            pltpu.VMEM((1, depth), jnp.float32),
            pltpu.VMEM((depth, depth), jnp.float32),
            pltpu.VMEM((rows, depth, cells), jnp.float32),
            pltpu.VMEM((total_rows, cells + 2 * EDGE, depth), jnp.float32),
            pltpu.VMEM((total_rows, cells + 2 * EDGE, depth), jnp.float32),
            pltpu.VMEM((2, 2, 16, depth), jnp.float32),
            pltpu.VMEM((2 * depth, 2 * depth), jnp.bfloat16),
            pltpu.SMEM((total_rows,), jnp.int32),
            pltpu.VMEM((GROUP * cells, 2 * depth), jnp.bfloat16),
            pltpu.VMEM((GROUP * cells, 2 * depth), jnp.bfloat16),
            pltpu.SemaphoreType.DMA((8,)),
            pltpu.SemaphoreType.DMA((rows // GROUP,)),
            pltpu.SemaphoreType.DMA((rows // GROUP,)),
        ],
        compiler_params=pltpu.CompilerParams(vmem_limit_bytes=32 << 20),
        cost_estimate=pl.CostEstimate(
            flops=120 * depth * depth * rows * cells,
            bytes_accessed=8 * depth * rows * cells,
            transcendentals=0,
        ),
        name="substeps",
    )(
        in_hbm(dest_tile.reshape(2 * lines, 128)),
        in_hbm(dest_block),
        in_hbm(land_mask),
        in_hbm(couple_gain),
        state,
        before,
        after,
        in_hbm(diffusion),
        in_hbm(column_op[0]),
    )

    new_state = pl.pallas_call(
        forcing_kernel,
        out_shape=jax.ShapeDtypeStruct((depth, rows, cells), jnp.float32),
        in_specs=[anywhere, vmem, vmem, vmem, anywhere],
        out_specs=anywhere,
        input_output_aliases={4: 0},
        scratch_shapes=[
            pltpu.SMEM((lines, 128), jnp.int32),
            pltpu.VMEM(((rows + 1) * fields, cells), jnp.float32),
            pltpu.VMEM((fields, rows, cells), jnp.float32),
            pltpu.SemaphoreType.DMA((1 + fields // PART,)),
        ],
        compiler_params=pltpu.CompilerParams(vmem_limit_bytes=32 << 20),
        name="add_forcing",
    )(target, gain, arrived, top, field)
    return new_state[None]


def solution(mesh):
    placed = (
        P("comp", "member", "tile", None),
        P("comp", "tile", None, None),
        P("comp", "member"),
        P("comp", "member", None),
        P("comp", "member"),
        P("tile"),
        P(),
        P(),
    )
    return jax.shard_map(
        on_device,
        mesh=mesh,
        in_specs=placed,
        out_specs=P("comp", "member", "tile", None),
        check_vma=False,
    )
```

```python
import functools

import jax
import jax.numpy as jnp
from jax import lax
from jax.experimental import pallas as pl
from jax.experimental.pallas import tpu as pltpu
from jax.sharding import PartitionSpec as P

SUB = 3
CHUNK = 32
GROUP = 8
EDGE = 8
PART = 4


def copies(pairs, sems, first):
    started = [pltpu.make_async_copy(a, b, sems.at[first + i]) for i, (a, b) in enumerate(pairs)]
    for copy in started:
        copy.start()
    return started


def arrivals(cap, rows, comp, tile, dest_ref, block_ref):
    lines = dest_ref.shape[0] // 2
    dest = dest_ref[pl.ds((1 - comp) * lines, lines), :]
    both = [jnp.concatenate([block_ref[c : c + 1, pl.ds(e * 128, 128)] for e in range(lines)], axis=0) for c in range(2)]
    place = jnp.where(comp == 1, both[0], both[1])
    mine = dest == tile
    earlier = lax.broadcasted_iota(jnp.int32, (128, 128), 0)
    later = lax.broadcasted_iota(jnp.int32, (128, 128), 1)
    before = (earlier < later) & (lax.div(earlier, rows) == lax.div(later, rows))
    rank = jnp.dot(
        mine.astype(jnp.float32).astype(jnp.bfloat16),
        before.astype(jnp.float32).astype(jnp.bfloat16),
        preferred_element_type=jnp.float32,
    )
    lane = lax.broadcasted_iota(jnp.int32, (lines, 128), 1)
    offset = (place - rows).astype(jnp.float32)
    target = jnp.zeros((lines, 128), jnp.float32)
    for h in range(128 // rows):
        here = mine & (lax.div(lane, rows) == h)
        for r in range(cap):
            found = jnp.sum(jnp.where(here & (rank == r), offset, 0.0), axis=1, keepdims=True)
            target = jnp.where(lane == h * cap + r, found, target)
    return target.astype(jnp.int32) + rows


def send_kernel(
    cap,
    tiles,
    dest_hbm,
    land_hbm,
    state_ref,
    weight_hbm,
    out_ref,
    far_ref,
    near_ref,
    dest_ref,
    land_ref,
    surface,
    weights,
    slabs,
    blocks,
    count_ref,
    sems,
):
    rows, fields, cells = blocks.shape
    depth = slabs.shape[1]
    chunks = rows // CHUNK
    comp, tile = lax.axis_index("comp"), lax.axis_index("tile")
    ends = [*range(SUB), *range(rows - SUB, rows)]
    parts = [pl.ds(i * CHUNK, CHUNK) for i in range(chunks)]
    pairs = [
        (land_hbm, land_ref),
        (dest_hbm, dest_ref),
        (state_ref.at[pl.ds(0, fields)], surface.reshape(fields, rows, cells)),
        (weight_hbm.at[parts[0]], weights.at[parts[0]]),
    ]
    pairs += [(state_ref.at[:, x, :], slabs.at[r]) for r, x in enumerate(ends)]
    pairs += [(weight_hbm.at[part], weights.at[part]) for part in parts[1:]]
    get_land, get_dest, get_surface, first, *others = copies(pairs, sems, 0)
    loads, get_weight = others[: 2 * SUB], [first, *others[2 * SUB :]]

    get_land.wait()
    row_of = lax.broadcasted_iota(jnp.int32, (16, 128), 0)
    even = lax.rem(tile, 2) == 0
    for ref, last in ((far_ref, jnp.logical_not(even)), (near_ref, even)):
        flags = jnp.zeros((16, 128), jnp.float32)
        for r in range(SUB):
            flag = jnp.where(comp == 1, land_ref[jnp.where(last, rows - SUB, 0) + r], 1).astype(jnp.float32)
            flags = jnp.where(row_of == r, flag, flags)
        ref[pl.ds(SUB * depth, 16), :] = flags.astype(jnp.bfloat16)
    for t in range(tiles):
        count_ref[t] = 0

    def remap(i, carry):
        for k in range(CHUNK):
            j = i * CHUNK + k
            values = surface[pl.ds(j, fields, stride=rows), :].astype(jnp.bfloat16)
            block = jnp.dot(values, weights[j], preferred_element_type=jnp.float32)
            blocks[j] = block.astype(jnp.bfloat16)
        return carry

    def place(j, carry):
        d = dest_ref[comp * (tiles * rows) + tile * rows + j]
        n = count_ref[d]
        out_ref[d * cap + n] = blocks[j]
        count_ref[d] = n + 1
        return carry

    def round_row(r, carry):
        at = pl.ds(pl.multiple_of(r * depth, depth), depth)
        far_ref[at, :] = slabs[jnp.where(even, 0, SUB) + r].astype(jnp.bfloat16)
        near_ref[at, :] = slabs[jnp.where(even, SUB, 0) + r].astype(jnp.bfloat16)
        return carry

    get_surface.wait()

    def weight_sem(i):
        return sems.at[jnp.where(i == 0, 3, 3 + 2 * SUB + i)]

    get_dest.wait()

    def chunk(i, carry):
        pltpu.make_async_copy(weight_hbm.at[parts[0]], weights.at[parts[0]], weight_sem(i)).wait()
        remap(i, carry)
        lax.fori_loop(0, CHUNK, lambda k, c: place(i * CHUNK + k, c), 0, unroll=8)

        @pl.when(i == 0)
        def _():
            for copy in loads:
                copy.wait()
            lax.fori_loop(0, SUB, round_row, 0)

        return carry

    lax.fori_loop(0, chunks, chunk, 0)


def field_kernel(
    cap,
    lines_hbm,
    block_hbm,
    land_hbm,
    gain_hbm,
    state_ref,
    far_hbm,
    near_hbm,
    diffusion_hbm,
    column_hbm,
    out_ref,
    top_ref,
    target_ref,
    gain_ref,
    lines_ref,
    block_ref,
    land_ref,
    factors,
    halo_ref,
    diffusion_ref,
    column_ref,
    slabs,
    u0,
    u1,
    coef,
    right,
    flags,
    half0,
    half1,
    small_sems,
    in_sems,
    out_sems,
):
    depth, rows, cells = state_ref.shape
    groups = rows // GROUP
    comp, fields = lax.axis_index("comp"), top_ref.shape[1]
    even = lax.rem(lax.axis_index("tile"), 2) == 0
    before_ref, after_ref = halo_ref.at[0], halo_ref.at[1]
    inside = pl.ds(EDGE, cells)
    below = pl.ds(fields, depth - fields)

    def load(x, carry):
        pltpu.make_async_copy(state_ref.at[:, x, :], slabs.at[x], in_sems.at[lax.div(x, GROUP)]).start()
        return carry

    small = copies(
        (
            (lines_hbm, lines_ref),
            (block_hbm, block_ref),
            (diffusion_hbm, diffusion_ref),
            (column_hbm, column_ref),
            (land_hbm, land_ref),
            (gain_hbm, factors),
            (far_hbm, halo_ref.at[jnp.where(even, 0, 1)]),
            (near_hbm, halo_ref.at[jnp.where(even, 1, 0)]),
        ),
        small_sems,
        0,
    )
    lax.fori_loop(0, rows, load, 0, unroll=4)

    def border(x, carry):
        zeros = jnp.zeros((EDGE, depth), jnp.float32)
        for u in (u0, u1):
            u[x, pl.ds(0, EDGE), :] = zeros
            u[x, pl.ds(EDGE + cells, EDGE), :] = zeros
        return carry
    lax.fori_loop(0, u0.shape[0], border, 0, unroll=2)
    for copy in small:
        copy.wait()
    target_ref[...] = arrivals(cap, rows, comp, lax.axis_index("tile"), lines_ref, block_ref)
    field_of = lax.broadcasted_iota(jnp.int32, (fields, cells), 0)
    gain = jnp.zeros((fields, cells), jnp.float32)
    for f in range(fields):
        gain = jnp.where(field_of == f, factors[0, f], gain)
    gain_ref[...] = gain

    rate = diffusion_ref[...]
    coef[0, 0] = jnp.ones_like(coef[0, 0])
    coef[0, 1] = jnp.zeros_like(coef[0, 0])
    coef[1, 0] = jnp.broadcast_to(1.0 - 4.0 * rate, (16, depth))
    coef[1, 1] = jnp.broadcast_to(rate, (16, depth))
    column = jnp.transpose(column_ref[...])
    high = column.astype(jnp.bfloat16)
    low = (column - high.astype(jnp.float32)).astype(jnp.bfloat16)
    right[0:depth, 0:depth] = high
    right[depth : 2 * depth, 0:depth] = high
    right[0:depth, depth : 2 * depth] = low
    right[depth : 2 * depth, depth : 2 * depth] = jnp.zeros_like(low)

    def own_flag(i, carry):
        flags[i + SUB] = jnp.where(comp == 1, land_ref[i], 1)
        return carry
    lax.fori_loop(0, rows, own_flag, 0, unroll=8)
    for r in range(SUB):
        flags[r] = jnp.max(before_ref[pl.ds(SUB * depth, 16), :][r : r + 1, :].astype(jnp.float32)).astype(jnp.int32)
        flags[rows + SUB + r] = jnp.max(
            after_ref[pl.ds(SUB * depth, 16), :][r : r + 1, :].astype(jnp.float32)
        ).astype(jnp.int32)
        u0[r, inside, :] = jnp.transpose(before_ref[pl.ds(r * depth, depth), :].astype(jnp.float32))
        u0[rows + SUB + r, inside, :] = jnp.transpose(after_ref[pl.ds(r * depth, depth), :].astype(jnp.float32))
    for r in range(rows + 2 * SUB, flags.shape[0]):
        flags[r] = 0

    def wait_in(g):
        pltpu.make_async_copy(
            slabs.at[pl.ds(g * GROUP, GROUP)], slabs.at[pl.ds(g * GROUP, GROUP)], in_sems.at[g]
        ).wait()

    def turn(s):
        u0[s + SUB, inside, :] = jnp.transpose(slabs[s])

    def stencil(source, x, half):
        for side in range(GROUP):
            active = flags[x + side]
            keep, spread = coef[active, 0], coef[active, 1]
            for k in range(0, cells, 16):
                at = pl.ds(EDGE + k, 16)
                near = source[x + side - 1, at, :] + source[x + side + 1, at, :]
                near += source[x + side, pl.ds(EDGE + k - 1, 16), :] + source[x + side, pl.ds(EDGE + k + 1, 16), :]
                stepped = keep * source[x + side, at, :] + spread * near
                high = stepped.astype(jnp.bfloat16)
                half[pl.ds(side * cells + k, 16), 0:depth] = high
                half[pl.ds(side * cells + k, 16), depth : 2 * depth] = (
                    stepped - high.astype(jnp.float32)
                ).astype(jnp.bfloat16)

    def product(half, count, store):
        mixed = jnp.dot(half[0 : count * cells], right[...], preferred_element_type=jnp.float32)
        mixed = mixed[:, 0:depth] + mixed[:, depth : 2 * depth]
        for side in range(count):
            store(side, mixed[side * cells : (side + 1) * cells])

    def keep_in(target, x):
        def store(side, values):
            target[x + side, inside, :] = values
        return store

    def finish(x):
        def store(side, values):
            turned = jnp.transpose(values)
            top_ref[x + side] = turned[0:fields]
            slabs[x + side] = turned
        return store

    def send_out(x):
        for side in range(GROUP):
            pltpu.make_async_copy(
                slabs.at[x + side, below, :], out_ref.at[below, x + side, :], out_sems.at[lax.div(x, GROUP)]
            ).start()

    wait_in(0)
    wait_in(1)
    for s in range(2 * GROUP - 1):
        turn(s)
    span = 2 * GROUP
    bodies = rows // span

    stencil(u0, 1, half0)
    def body1(i, carry):
        x = 1 + span * i
        @pl.when(2 * i + 3 < groups)
        def _():
            wait_in(2 * i + 2)
            wait_in(2 * i + 3)
        product(half0, GROUP, keep_in(u1, x))
        stencil(u0, x + GROUP, half1)
        for s in range(GROUP):
            turn(jnp.minimum(span * i + span - 1 + s, rows - 1))
        product(half1, GROUP, keep_in(u1, x + GROUP))
        stencil(u0, x + span, half0)
        for s in range(GROUP, span):
            turn(jnp.minimum(span * i + span - 1 + s, rows - 1))
        return carry
    lax.fori_loop(0, bodies, body1, 0)
    product(half0, 4, keep_in(u1, rows + 1))

    stencil(u1, 2, half0)
    def body2(i, carry):
        x = 2 + span * i
        product(half0, GROUP, keep_in(u0, x))
        stencil(u1, x + GROUP, half1)
        product(half1, GROUP, keep_in(u0, x + GROUP))
        stencil(u1, x + span, half0)
        return carry
    lax.fori_loop(0, bodies, body2, 0)
    product(half0, 2, keep_in(u0, rows + 2))

    stencil(u0, SUB, half0)
    def body3(i, carry):
        x = span * i
        product(half0, GROUP, finish(x))
        stencil(u0, SUB + x + GROUP, half1)
        send_out(x)
        product(half1, GROUP, finish(x + GROUP))
        stencil(u0, SUB + x + span, half0)
        send_out(x + GROUP)
        return carry
    lax.fori_loop(0, bodies, body3, 0)

    def wait_out(i, carry):
        part = slabs.at[pl.ds(0, GROUP), below, :]
        pltpu.make_async_copy(part, part, out_sems.at[i]).wait()
        return carry
    lax.fori_loop(0, groups, wait_out, 0)


def forcing_kernel(target_hbm, gain_ref, arrived_ref, top_ref, field_ref, out_ref, target_ref, total, result, sems):
    slots, fields, _ = arrived_ref.shape
    rows, _, cells = top_ref.shape
    (get_target,) = copies(((target_hbm, target_ref),), sems, 0)

    def begin(x, carry):
        total[pl.ds(pl.multiple_of(x * fields, fields), fields), :] = top_ref[x]
        return carry

    lax.fori_loop(0, rows, begin, 0, unroll=8)
    total[pl.ds(rows * fields, fields), :] = jnp.zeros((fields, cells), jnp.float32)
    gain = gain_ref[...]
    get_target.wait()
    lines = target_ref.shape[0]
    count = slots // lines

    def add(e, carry):
        for s in range(count):
            at = pl.ds(pl.multiple_of(target_ref[e, s] * fields, fields), fields)
            total[at, :] += gain * arrived_ref[e * count + s].astype(jnp.float32)
        return carry

    lax.fori_loop(0, lines, add, 0)

    def store(i):
        part = pl.ds(i * PART, PART)
        return pltpu.make_async_copy(result.at[part], out_ref.at[part], sems.at[1 + i])

    def finish(i, carry):
        for k in range(PART):
            result[i * PART + k] = total[pl.ds(i * PART + k, rows, stride=fields), :]
        store(i).start()
        return carry

    def wait(i, carry):
        store(i).wait()
        return carry

    lax.fori_loop(0, fields // PART, finish, 0)
    lax.fori_loop(0, fields // PART, wait, 0)


def on_device(
    prognostic_state,
    remapping_weight,
    diffusion,
    column_op,
    couple_gain,
    land_mask,
    dest_tile,
    dest_block,
):
    tiles = lax.axis_size("tile")
    in_hbm = functools.partial(pltpu.with_memory_space_constraint, memory_space=pltpu.HBM)
    state = in_hbm(prognostic_state[0])
    depth, rows, cells = state.shape
    fields = couple_gain.shape[1]
    cap = max(2, 2 * rows // tiles)
    slots = tiles * cap
    halo_rows = SUB * depth + 16
    routes = in_hbm(dest_tile.reshape(-1))
    lines = tiles * rows // 128

    vmem = pl.BlockSpec(memory_space=pltpu.VMEM)
    anywhere = pl.BlockSpec(memory_space=pltpu.HBM)

    outgoing, far, near = pl.pallas_call(
        functools.partial(send_kernel, cap, tiles),
        out_shape=(
            jax.ShapeDtypeStruct((slots, fields, cells), jnp.bfloat16),
            jax.ShapeDtypeStruct((halo_rows, cells), jnp.bfloat16),
            jax.ShapeDtypeStruct((halo_rows, cells), jnp.bfloat16),
        ),
        in_specs=[anywhere] * 4,
        out_specs=(vmem, vmem, vmem),
        scratch_shapes=[
            pltpu.SMEM(routes.shape, jnp.int32),
            pltpu.SMEM(land_mask.shape, jnp.int32),
            pltpu.VMEM((fields * rows, cells), jnp.float32),
            pltpu.VMEM((rows, cells, cells), jnp.bfloat16),
            pltpu.VMEM((2 * SUB, depth, cells), jnp.float32),
            pltpu.VMEM((rows, fields, cells), jnp.bfloat16),
            pltpu.SMEM((tiles,), jnp.int32),
            pltpu.SemaphoreType.DMA((3 + 2 * SUB + rows // CHUNK,)),
        ],
        compiler_params=pltpu.CompilerParams(vmem_limit_bytes=32 << 20),
        cost_estimate=pl.CostEstimate(
            flops=2 * rows * fields * cells * cells, bytes_accessed=8 << 20, transcendentals=0
        ),
        name="remap_and_pack",
    )(routes, in_hbm(land_mask), state, in_hbm(remapping_weight[0]))

    odd = [(i, (i + 1) % tiles) for i in range(1, tiles, 2)]
    far = lax.ppermute(far, "tile", odd + [(b, a) for a, b in odd])
    near = lax.ppermute(near, "tile", [(i, i ^ 1) for i in range(tiles)])
    swapped = lax.ppermute(outgoing, "comp", [(0, 1), (1, 0)])
    arrived = lax.all_to_all(swapped, "tile", split_axis=0, concat_axis=0, tiled=True)

    total_rows = rows + 2 * SUB + GROUP
    field, top, target, gain = pl.pallas_call(
        functools.partial(field_kernel, cap),
        out_shape=(
            jax.ShapeDtypeStruct((depth, rows, cells), jnp.float32),
            jax.ShapeDtypeStruct((rows, fields, cells), jnp.float32),
            jax.ShapeDtypeStruct((lines, 128), jnp.int32),
            jax.ShapeDtypeStruct((fields, cells), jnp.float32),
        ),
        in_specs=[anywhere] * 9,
        out_specs=(anywhere, vmem, vmem, vmem),
        scratch_shapes=[
            pltpu.VMEM((2 * lines, 128), jnp.int32),
            pltpu.VMEM(dest_block.shape, jnp.int32),
            pltpu.SMEM((rows,), jnp.int32),
            pltpu.SMEM(couple_gain.shape, jnp.float32),
            pltpu.VMEM((2, halo_rows, cells), jnp.bfloat16),
            pltpu.VMEM((1, depth), jnp.float32),
            pltpu.VMEM((depth, depth), jnp.float32),
            pltpu.VMEM((rows, depth, cells), jnp.float32),
            pltpu.VMEM((total_rows, cells + 2 * EDGE, depth), jnp.float32),
            pltpu.VMEM((total_rows, cells + 2 * EDGE, depth), jnp.float32),
            pltpu.VMEM((2, 2, 16, depth), jnp.float32),
            pltpu.VMEM((2 * depth, 2 * depth), jnp.bfloat16),
            pltpu.SMEM((total_rows,), jnp.int32),
            pltpu.VMEM((GROUP * cells, 2 * depth), jnp.bfloat16),
            pltpu.VMEM((GROUP * cells, 2 * depth), jnp.bfloat16),
            pltpu.SemaphoreType.DMA((8,)),
            pltpu.SemaphoreType.DMA((rows // GROUP,)),
            pltpu.SemaphoreType.DMA((rows // GROUP,)),
        ],
        compiler_params=pltpu.CompilerParams(vmem_limit_bytes=32 << 20),
        cost_estimate=pl.CostEstimate(
            flops=120 * depth * depth * rows * cells,
            bytes_accessed=8 * depth * rows * cells,
            transcendentals=0,
        ),
        name="substeps",
    )(
        in_hbm(dest_tile.reshape(2 * lines, 128)),
        in_hbm(dest_block),
        in_hbm(land_mask),
        in_hbm(couple_gain),
        state,
        far,
        near,
        in_hbm(diffusion),
        in_hbm(column_op[0]),
    )

    new_state = pl.pallas_call(
        forcing_kernel,
        out_shape=jax.ShapeDtypeStruct((depth, rows, cells), jnp.float32),
        in_specs=[anywhere, vmem, vmem, vmem, anywhere],
        out_specs=anywhere,
        input_output_aliases={4: 0},
        scratch_shapes=[
            pltpu.SMEM((lines, 128), jnp.int32),
            pltpu.VMEM(((rows + 1) * fields, cells), jnp.float32),
            pltpu.VMEM((fields, rows, cells), jnp.float32),
            pltpu.SemaphoreType.DMA((1 + fields // PART,)),
        ],
        compiler_params=pltpu.CompilerParams(vmem_limit_bytes=32 << 20),
        name="add_forcing",
    )(target, gain, arrived, top, field)
    return new_state[None]


def solution(mesh):
    placed = (
        P("comp", "member", "tile", None),
        P("comp", "tile", None, None),
        P("comp", "member"),
        P("comp", "member", None),
        P("comp", "member"),
        P("tile"),
        P(),
        P(),
    )
    return jax.shard_map(
        on_device,
        mesh=mesh,
        in_specs=placed,
        out_specs=P("comp", "member", "tile", None),
        check_vma=False,
    )
```

```python
import functools

import jax
import jax.numpy as jnp
from jax import lax
from jax.experimental import pallas as pl
from jax.experimental.pallas import tpu as pltpu
from jax.sharding import PartitionSpec as P

SUB = 3
CHUNK = 32
GROUP = 8
EDGE = 8
PART = 4
SPARE = 16


def copies(pairs, sems, first):
    started = [pltpu.make_async_copy(a, b, sems.at[first + i]) for i, (a, b) in enumerate(pairs)]
    for copy in started:
        copy.start()
    return started


def arrivals(cap, rows, comp, tile, dest_ref, block_ref):
    lines = dest_ref.shape[0] // 2
    dest = dest_ref[pl.ds((1 - comp) * lines, lines), :]
    both = [jnp.concatenate([block_ref[c : c + 1, pl.ds(e * 128, 128)] for e in range(lines)], axis=0) for c in range(2)]
    place = jnp.where(comp == 1, both[0], both[1])
    mine = dest == tile
    earlier = lax.broadcasted_iota(jnp.int32, (128, 128), 0)
    later = lax.broadcasted_iota(jnp.int32, (128, 128), 1)
    before = (earlier < later) & (lax.div(earlier, rows) == lax.div(later, rows))
    rank = jnp.dot(
        mine.astype(jnp.float32).astype(jnp.bfloat16),
        before.astype(jnp.float32).astype(jnp.bfloat16),
        preferred_element_type=jnp.float32,
    )
    lane = lax.broadcasted_iota(jnp.int32, (lines, 128), 1)
    offset = (place - rows).astype(jnp.float32)
    target = jnp.zeros((lines, 128), jnp.float32)
    for h in range(128 // rows):
        here = mine & (lax.div(lane, rows) == h)
        for r in range(cap):
            found = jnp.sum(jnp.where(here & (rank == r), offset, 0.0), axis=1, keepdims=True)
            target = jnp.where(lane == h * cap + r, found, target)
    return jnp.where(target == 0.0, lax.rem(lane, SPARE), target.astype(jnp.int32)) + rows


def send_kernel(
    cap,
    tiles,
    dest_hbm,
    land_hbm,
    state_ref,
    weight_hbm,
    out_ref,
    head_ref,
    tail_ref,
    dest_ref,
    land_ref,
    surface,
    weights,
    slabs,
    blocks,
    count_ref,
    sems,
):
    rows, fields, cells = blocks.shape
    depth = slabs.shape[1]
    chunks = rows // CHUNK
    comp, tile = lax.axis_index("comp"), lax.axis_index("tile")
    ends = [*range(SUB), *range(rows - SUB, rows)]
    parts = [pl.ds(i * CHUNK, CHUNK) for i in range(chunks)]
    pairs = [
        (land_hbm, land_ref),
        (dest_hbm, dest_ref),
        (state_ref.at[pl.ds(0, fields)], surface.reshape(fields, rows, cells)),
        (weight_hbm.at[parts[0]], weights.at[parts[0]]),
    ]
    pairs += [(state_ref.at[:, x, :], slabs.at[r]) for r, x in enumerate(ends)]
    pairs += [(weight_hbm.at[part], weights.at[part]) for part in parts[1:]]
    get_land, get_dest, get_surface, first, *others = copies(pairs, sems, 0)
    loads, get_weight = others[: 2 * SUB], [first, *others[2 * SUB :]]

    get_land.wait()
    row_of = lax.broadcasted_iota(jnp.int32, (16, 128), 0)
    for ref, offset in ((head_ref, 0), (tail_ref, rows - SUB)):
        flags = jnp.zeros((16, 128), jnp.float32)
        for r in range(SUB):
            flag = jnp.where(comp == 1, land_ref[offset + r], 1).astype(jnp.float32)
            flags = jnp.where(row_of == r, flag, flags)
        ref[pl.ds(SUB * depth, 16), :] = flags.astype(jnp.bfloat16)
    for t in range(tiles):
        count_ref[t] = 0

    def remap(i, carry):
        for k in range(CHUNK):
            j = i * CHUNK + k
            values = surface[pl.ds(j, fields, stride=rows), :].astype(jnp.bfloat16)
            block = jnp.dot(values, weights[j], preferred_element_type=jnp.float32)
            blocks[j] = block.astype(jnp.bfloat16)
        return carry

    def place(j, carry):
        d = dest_ref[comp * (tiles * rows) + tile * rows + j]
        n = count_ref[d]
        out_ref[d * cap + n] = blocks[j]
        count_ref[d] = n + 1
        return carry

    def round_row(r, carry):
        @pl.when(r < SUB)
        def _():
            head_ref[pl.ds(pl.multiple_of(r * depth, depth), depth), :] = slabs[r].astype(jnp.bfloat16)

        @pl.when(r >= SUB)
        def _():
            at = pl.ds(pl.multiple_of((r - SUB) * depth, depth), depth)
            tail_ref[at, :] = slabs[r].astype(jnp.bfloat16)

        return carry

    get_surface.wait()

    def weight_sem(i):
        return sems.at[jnp.where(i == 0, 3, 3 + 2 * SUB + i)]

    get_dest.wait()

    def chunk(i, carry):
        pltpu.make_async_copy(weight_hbm.at[parts[0]], weights.at[parts[0]], weight_sem(i)).wait()
        remap(i, carry)
        lax.fori_loop(0, CHUNK, lambda k, c: place(i * CHUNK + k, c), 0, unroll=8)

        @pl.when(i == 0)
        def _():
            for copy in loads:
                copy.wait()
            lax.fori_loop(0, 2 * SUB, round_row, 0)

        return carry

    lax.fori_loop(0, chunks, chunk, 0)


def field_kernel(
    cap,
    lines_hbm,
    block_hbm,
    land_hbm,
    gain_hbm,
    state_ref,
    before_hbm,
    after_hbm,
    diffusion_hbm,
    column_hbm,
    out_ref,
    top_ref,
    target_ref,
    gain_ref,
    lines_ref,
    block_ref,
    land_ref,
    factors,
    before_ref,
    after_ref,
    diffusion_ref,
    column_ref,
    slabs,
    u0,
    u1,
    coef,
    right,
    flags,
    half0,
    half1,
    small_sems,
    in_sems,
    out_sems,
):
    depth, rows, cells = state_ref.shape
    groups = rows // GROUP
    comp, fields = lax.axis_index("comp"), top_ref.shape[1]
    inside = pl.ds(EDGE, cells)
    below = pl.ds(fields, depth - fields)

    def load(x, carry):
        pltpu.make_async_copy(state_ref.at[:, x, :], slabs.at[x], in_sems.at[lax.div(x, GROUP)]).start()
        return carry

    small = copies(
        (
            (lines_hbm, lines_ref),
            (block_hbm, block_ref),
            (diffusion_hbm, diffusion_ref),
            (column_hbm, column_ref),
            (land_hbm, land_ref),
            (gain_hbm, factors),
            (before_hbm, before_ref),
            (after_hbm, after_ref),
        ),
        small_sems,
        0,
    )
    lax.fori_loop(0, rows, load, 0, unroll=4)

    def border(x, carry):
        zeros = jnp.zeros((EDGE, depth), jnp.float32)
        for u in (u0, u1):
            u[x, pl.ds(0, EDGE), :] = zeros
            u[x, pl.ds(EDGE + cells, EDGE), :] = zeros
        return carry
    lax.fori_loop(0, u0.shape[0], border, 0, unroll=2)
    for copy in small:
        copy.wait()
    target_ref[...] = arrivals(cap, rows, comp, lax.axis_index("tile"), lines_ref, block_ref)
    field_of = lax.broadcasted_iota(jnp.int32, (fields, cells), 0)
    gain = jnp.zeros((fields, cells), jnp.float32)
    for f in range(fields):
        gain = jnp.where(field_of == f, factors[0, f], gain)
    gain_ref[...] = gain

    rate = diffusion_ref[...]
    coef[0, 0] = jnp.ones_like(coef[0, 0])
    coef[0, 1] = jnp.zeros_like(coef[0, 0])
    coef[1, 0] = jnp.broadcast_to(1.0 - 4.0 * rate, (16, depth))
    coef[1, 1] = jnp.broadcast_to(rate, (16, depth))
    column = jnp.transpose(column_ref[...])
    high = column.astype(jnp.bfloat16)
    low = (column - high.astype(jnp.float32)).astype(jnp.bfloat16)
    right[0:depth, 0:depth] = high
    right[depth : 2 * depth, 0:depth] = high
    right[0:depth, depth : 2 * depth] = low
    right[depth : 2 * depth, depth : 2 * depth] = jnp.zeros_like(low)

    def own_flag(i, carry):
        flags[i + SUB] = jnp.where(comp == 1, land_ref[i], 1)
        return carry
    lax.fori_loop(0, rows, own_flag, 0, unroll=8)
    for r in range(SUB):
        flags[r] = jnp.max(before_ref[pl.ds(SUB * depth, 16), :][r : r + 1, :].astype(jnp.float32)).astype(jnp.int32)
        flags[rows + SUB + r] = jnp.max(
            after_ref[pl.ds(SUB * depth, 16), :][r : r + 1, :].astype(jnp.float32)
        ).astype(jnp.int32)
        u0[r, inside, :] = jnp.transpose(before_ref[pl.ds(r * depth, depth), :].astype(jnp.float32))
        u0[rows + SUB + r, inside, :] = jnp.transpose(after_ref[pl.ds(r * depth, depth), :].astype(jnp.float32))
    for r in range(rows + 2 * SUB, flags.shape[0]):
        flags[r] = 0

    def wait_in(g):
        pltpu.make_async_copy(
            slabs.at[pl.ds(g * GROUP, GROUP)], slabs.at[pl.ds(g * GROUP, GROUP)], in_sems.at[g]
        ).wait()

    def turn(s):
        u0[s + SUB, inside, :] = jnp.transpose(slabs[s])

    def stencil(source, x, half):
        for side in range(GROUP):
            active = flags[x + side]
            keep, spread = coef[active, 0], coef[active, 1]
            for k in range(0, cells, 16):
                at = pl.ds(EDGE + k, 16)
                near = source[x + side - 1, at, :] + source[x + side + 1, at, :]
                near += source[x + side, pl.ds(EDGE + k - 1, 16), :] + source[x + side, pl.ds(EDGE + k + 1, 16), :]
                stepped = keep * source[x + side, at, :] + spread * near
                high = stepped.astype(jnp.bfloat16)
                half[pl.ds(side * cells + k, 16), 0:depth] = high
                half[pl.ds(side * cells + k, 16), depth : 2 * depth] = (
                    stepped - high.astype(jnp.float32)
                ).astype(jnp.bfloat16)

    def product(half, count, store):
        mixed = jnp.dot(half[0 : count * cells], right[...], preferred_element_type=jnp.float32)
        mixed = mixed[:, 0:depth] + mixed[:, depth : 2 * depth]
        for side in range(count):
            store(side, mixed[side * cells : (side + 1) * cells])

    def keep_in(target, x):
        def store(side, values):
            target[x + side, inside, :] = values
        return store

    def finish(x):
        def store(side, values):
            turned = jnp.transpose(values)
            top_ref[x + side] = turned[0:fields]
            slabs[x + side] = turned
        return store

    def send_out(x):
        for side in range(GROUP):
            pltpu.make_async_copy(
                slabs.at[x + side, below, :], out_ref.at[below, x + side, :], out_sems.at[lax.div(x, GROUP)]
            ).start()

    wait_in(0)
    wait_in(1)
    for s in range(2 * GROUP - 1):
        turn(s)
    span = 2 * GROUP
    bodies = rows // span

    stencil(u0, 1, half0)
    def body1(i, carry):
        x = 1 + span * i
        @pl.when(2 * i + 3 < groups)
        def _():
            wait_in(2 * i + 2)
            wait_in(2 * i + 3)
        product(half0, GROUP, keep_in(u1, x))
        stencil(u0, x + GROUP, half1)
        for s in range(GROUP):
            turn(jnp.minimum(span * i + span - 1 + s, rows - 1))
        product(half1, GROUP, keep_in(u1, x + GROUP))
        stencil(u0, x + span, half0)
        for s in range(GROUP, span):
            turn(jnp.minimum(span * i + span - 1 + s, rows - 1))
        return carry
    lax.fori_loop(0, bodies, body1, 0)
    product(half0, 4, keep_in(u1, rows + 1))

    stencil(u1, 2, half0)
    def body2(i, carry):
        x = 2 + span * i
        product(half0, GROUP, keep_in(u0, x))
        stencil(u1, x + GROUP, half1)
        product(half1, GROUP, keep_in(u0, x + GROUP))
        stencil(u1, x + span, half0)
        return carry
    lax.fori_loop(0, bodies, body2, 0)
    product(half0, 2, keep_in(u0, rows + 2))

    stencil(u0, SUB, half0)
    def body3(i, carry):
        x = span * i
        product(half0, GROUP, finish(x))
        stencil(u0, SUB + x + GROUP, half1)
        send_out(x)
        product(half1, GROUP, finish(x + GROUP))
        stencil(u0, SUB + x + span, half0)
        send_out(x + GROUP)
        return carry
    lax.fori_loop(0, bodies, body3, 0)

    def wait_out(i, carry):
        part = slabs.at[pl.ds(0, GROUP), below, :]
        pltpu.make_async_copy(part, part, out_sems.at[i]).wait()
        return carry
    lax.fori_loop(0, groups, wait_out, 0)


def forcing_kernel(target_hbm, gain_ref, arrived_ref, top_ref, field_ref, out_ref, target_ref, total, result, sems):
    slots, fields, _ = arrived_ref.shape
    rows, _, cells = top_ref.shape
    (get_target,) = copies(((target_hbm, target_ref),), sems, 0)

    def begin(x, carry):
        total[pl.ds(pl.multiple_of(x * fields, fields), fields), :] = top_ref[x]
        return carry

    lax.fori_loop(0, rows, begin, 0, unroll=8)
    spare = pl.ds(rows * fields, SPARE * fields)
    total[spare, :] = jnp.zeros((SPARE * fields, cells), jnp.float32)
    gain = gain_ref[...]
    get_target.wait()
    lines = target_ref.shape[0]
    count = slots // lines

    def add(e, carry):
        for s in range(count):
            at = pl.ds(pl.multiple_of(target_ref[e, s] * fields, fields), fields)
            total[at, :] += gain * arrived_ref[e * count + s].astype(jnp.float32)
        return carry

    lax.fori_loop(0, lines, add, 0)

    def store(i):
        part = pl.ds(i * PART, PART)
        return pltpu.make_async_copy(result.at[part], out_ref.at[part], sems.at[1 + i])

    def finish(i, carry):
        for k in range(PART):
            result[i * PART + k] = total[pl.ds(i * PART + k, rows, stride=fields), :]
        store(i).start()
        return carry

    def wait(i, carry):
        store(i).wait()
        return carry

    lax.fori_loop(0, fields // PART, finish, 0)
    lax.fori_loop(0, fields // PART, wait, 0)


def on_device(
    prognostic_state,
    remapping_weight,
    diffusion,
    column_op,
    couple_gain,
    land_mask,
    dest_tile,
    dest_block,
):
    tiles = lax.axis_size("tile")
    in_hbm = functools.partial(pltpu.with_memory_space_constraint, memory_space=pltpu.HBM)
    state = in_hbm(prognostic_state[0])
    depth, rows, cells = state.shape
    fields = couple_gain.shape[1]
    cap = max(2, 2 * rows // tiles)
    slots = tiles * cap
    halo_rows = SUB * depth + 16
    routes = in_hbm(dest_tile.reshape(-1))
    lines = tiles * rows // 128

    vmem = pl.BlockSpec(memory_space=pltpu.VMEM)
    anywhere = pl.BlockSpec(memory_space=pltpu.HBM)

    outgoing, head, tail = pl.pallas_call(
        functools.partial(send_kernel, cap, tiles),
        out_shape=(
            jax.ShapeDtypeStruct((slots, fields, cells), jnp.bfloat16),
            jax.ShapeDtypeStruct((halo_rows, cells), jnp.bfloat16),
            jax.ShapeDtypeStruct((halo_rows, cells), jnp.bfloat16),
        ),
        in_specs=[anywhere] * 4,
        out_specs=(vmem, vmem, vmem),
        scratch_shapes=[
            pltpu.SMEM(routes.shape, jnp.int32),
            pltpu.SMEM(land_mask.shape, jnp.int32),
            pltpu.VMEM((fields * rows, cells), jnp.float32),
            pltpu.VMEM((rows, cells, cells), jnp.bfloat16),
            pltpu.VMEM((2 * SUB, depth, cells), jnp.float32),
            pltpu.VMEM((rows, fields, cells), jnp.bfloat16),
            pltpu.SMEM((tiles,), jnp.int32),
            pltpu.SemaphoreType.DMA((3 + 2 * SUB + rows // CHUNK,)),
        ],
        compiler_params=pltpu.CompilerParams(vmem_limit_bytes=32 << 20),
        cost_estimate=pl.CostEstimate(
            flops=2 * rows * fields * cells * cells, bytes_accessed=8 << 20, transcendentals=0
        ),
        name="remap_and_pack",
    )(routes, in_hbm(land_mask), state, in_hbm(remapping_weight[0]))

    ring = [(i, (i + 1) % tiles) for i in range(tiles)]
    before = lax.ppermute(tail, "tile", ring)
    after = lax.ppermute(head, "tile", [(b, a) for a, b in ring])

    swapped = lax.ppermute(outgoing, "comp", [(0, 1), (1, 0)])
    arrived = lax.all_to_all(swapped, "tile", split_axis=0, concat_axis=0, tiled=True)

    total_rows = rows + 2 * SUB + GROUP
    field, top, target, gain = pl.pallas_call(
        functools.partial(field_kernel, cap),
        out_shape=(
            jax.ShapeDtypeStruct((depth, rows, cells), jnp.float32),
            jax.ShapeDtypeStruct((rows, fields, cells), jnp.float32),
            jax.ShapeDtypeStruct((lines, 128), jnp.int32),
            jax.ShapeDtypeStruct((fields, cells), jnp.float32),
        ),
        in_specs=[anywhere] * 9,
        out_specs=(anywhere, vmem, vmem, vmem),
        scratch_shapes=[
            pltpu.VMEM((2 * lines, 128), jnp.int32),
            pltpu.VMEM(dest_block.shape, jnp.int32),
            pltpu.SMEM((rows,), jnp.int32),
            pltpu.SMEM(couple_gain.shape, jnp.float32),
            pltpu.VMEM((halo_rows, cells), jnp.bfloat16),
            pltpu.VMEM((halo_rows, cells), jnp.bfloat16),
            pltpu.VMEM((1, depth), jnp.float32),
            pltpu.VMEM((depth, depth), jnp.float32),
            pltpu.VMEM((rows, depth, cells), jnp.float32),
            pltpu.VMEM((total_rows, cells + 2 * EDGE, depth), jnp.float32),
            pltpu.VMEM((total_rows, cells + 2 * EDGE, depth), jnp.float32),
            pltpu.VMEM((2, 2, 16, depth), jnp.float32),
            pltpu.VMEM((2 * depth, 2 * depth), jnp.bfloat16),
            pltpu.SMEM((total_rows,), jnp.int32),
            pltpu.VMEM((GROUP * cells, 2 * depth), jnp.bfloat16),
            pltpu.VMEM((GROUP * cells, 2 * depth), jnp.bfloat16),
            pltpu.SemaphoreType.DMA((8,)),
            pltpu.SemaphoreType.DMA((rows // GROUP,)),
            pltpu.SemaphoreType.DMA((rows // GROUP,)),
        ],
        compiler_params=pltpu.CompilerParams(vmem_limit_bytes=32 << 20),
        cost_estimate=pl.CostEstimate(
            flops=120 * depth * depth * rows * cells,
            bytes_accessed=8 * depth * rows * cells,
            transcendentals=0,
        ),
        name="substeps",
    )(
        in_hbm(dest_tile.reshape(2 * lines, 128)),
        in_hbm(dest_block),
        in_hbm(land_mask),
        in_hbm(couple_gain),
        state,
        before,
        after,
        in_hbm(diffusion),
        in_hbm(column_op[0]),
    )

    new_state = pl.pallas_call(
        forcing_kernel,
        out_shape=jax.ShapeDtypeStruct((depth, rows, cells), jnp.float32),
        in_specs=[anywhere, vmem, vmem, vmem, anywhere],
        out_specs=anywhere,
        input_output_aliases={4: 0},
        scratch_shapes=[
            pltpu.SMEM((lines, 128), jnp.int32),
            pltpu.VMEM(((rows + SPARE) * fields, cells), jnp.float32),
            pltpu.VMEM((fields, rows, cells), jnp.float32),
            pltpu.SemaphoreType.DMA((1 + fields // PART,)),
        ],
        compiler_params=pltpu.CompilerParams(vmem_limit_bytes=32 << 20),
        name="add_forcing",
    )(target, gain, arrived, top, field)
    return new_state[None]


def solution(mesh):
    placed = (
        P("comp", "member", "tile", None),
        P("comp", "tile", None, None),
        P("comp", "member"),
        P("comp", "member", None),
        P("comp", "member"),
        P("tile"),
        P(),
        P(),
    )
    return jax.shard_map(
        on_device,
        mesh=mesh,
        in_specs=placed,
        out_specs=P("comp", "member", "tile", None),
        check_vma=False,
    )
```

```python
import functools

import jax
import jax.numpy as jnp
from jax import lax
from jax.experimental import pallas as pl
from jax.experimental.pallas import tpu as pltpu
from jax.sharding import PartitionSpec as P

SUB = 3
CHUNK = 32
GROUP = 8
EDGE = 8
PART = 4
SPARE = 16


def copies(pairs, sems, first):
    started = [pltpu.make_async_copy(a, b, sems.at[first + i]) for i, (a, b) in enumerate(pairs)]
    for copy in started:
        copy.start()
    return started


def arrivals(cap, rows, comp, tile, dest_ref, block_ref):
    lines = dest_ref.shape[0] // 2
    dest = dest_ref[pl.ds((1 - comp) * lines, lines), :]
    both = [jnp.concatenate([block_ref[c : c + 1, pl.ds(e * 128, 128)] for e in range(lines)], axis=0) for c in range(2)]
    place = jnp.where(comp == 1, both[0], both[1])
    mine = dest == tile
    earlier = lax.broadcasted_iota(jnp.int32, (128, 128), 0)
    later = lax.broadcasted_iota(jnp.int32, (128, 128), 1)
    before = (earlier < later) & (lax.div(earlier, rows) == lax.div(later, rows))
    rank = jnp.dot(
        mine.astype(jnp.float32).astype(jnp.bfloat16),
        before.astype(jnp.float32).astype(jnp.bfloat16),
        preferred_element_type=jnp.float32,
    )
    lane = lax.broadcasted_iota(jnp.int32, (lines, 128), 1)
    offset = (place - rows).astype(jnp.float32)
    target = jnp.zeros((lines, 128), jnp.float32)
    for h in range(128 // rows):
        here = mine & (lax.div(lane, rows) == h)
        for r in range(cap):
            found = jnp.sum(jnp.where(here & (rank == r), offset, 0.0), axis=1, keepdims=True)
            target = jnp.where(lane == h * cap + r, found, target)
    return jnp.where(target == 0.0, lax.rem(lane, SPARE), target.astype(jnp.int32)) + rows


def send_kernel(
    cap,
    tiles,
    dest_hbm,
    land_hbm,
    state_ref,
    weight_hbm,
    out_ref,
    far_ref,
    near_ref,
    dest_ref,
    land_ref,
    surface,
    weights,
    slabs,
    blocks,
    count_ref,
    sems,
):
    rows, fields, cells = blocks.shape
    depth = slabs.shape[1]
    chunks = rows // CHUNK
    comp, tile = lax.axis_index("comp"), lax.axis_index("tile")
    ends = [*range(SUB), *range(rows - SUB, rows)]
    parts = [pl.ds(i * CHUNK, CHUNK) for i in range(chunks)]
    pairs = [
        (land_hbm, land_ref),
        (dest_hbm, dest_ref),
        (state_ref.at[pl.ds(0, fields)], surface.reshape(fields, rows, cells)),
        (weight_hbm.at[parts[0]], weights.at[parts[0]]),
    ]
    pairs += [(state_ref.at[:, x, :], slabs.at[r]) for r, x in enumerate(ends)]
    pairs += [(weight_hbm.at[part], weights.at[part]) for part in parts[1:]]
    get_land, get_dest, get_surface, first, *others = copies(pairs, sems, 0)
    loads, get_weight = others[: 2 * SUB], [first, *others[2 * SUB :]]

    get_land.wait()
    row_of = lax.broadcasted_iota(jnp.int32, (16, 128), 0)
    even = lax.rem(tile, 2) == 0
    for ref, last in ((far_ref, jnp.logical_not(even)), (near_ref, even)):
        flags = jnp.zeros((16, 128), jnp.float32)
        for r in range(SUB):
            flag = jnp.where(comp == 1, land_ref[jnp.where(last, rows - SUB, 0) + r], 1).astype(jnp.float32)
            flags = jnp.where(row_of == r, flag, flags)
        ref[pl.ds(SUB * depth, 16), :] = flags.astype(jnp.bfloat16)
    for t in range(tiles):
        count_ref[t] = 0

    def remap(i, carry):
        for k in range(CHUNK):
            j = i * CHUNK + k
            values = surface[pl.ds(j, fields, stride=rows), :].astype(jnp.bfloat16)
            block = jnp.dot(values, weights[j], preferred_element_type=jnp.float32)
            blocks[j] = block.astype(jnp.bfloat16)
        return carry

    def place(j, carry):
        d = dest_ref[comp * (tiles * rows) + tile * rows + j]
        n = count_ref[d]
        out_ref[d * cap + n] = blocks[j]
        count_ref[d] = n + 1
        return carry

    def round_row(r, carry):
        at = pl.ds(pl.multiple_of(r * depth, depth), depth)
        far_ref[at, :] = slabs[jnp.where(even, 0, SUB) + r].astype(jnp.bfloat16)
        near_ref[at, :] = slabs[jnp.where(even, SUB, 0) + r].astype(jnp.bfloat16)
        return carry

    get_surface.wait()

    def weight_sem(i):
        return sems.at[jnp.where(i == 0, 3, 3 + 2 * SUB + i)]

    get_dest.wait()

    def chunk(i, carry):
        pltpu.make_async_copy(weight_hbm.at[parts[0]], weights.at[parts[0]], weight_sem(i)).wait()
        remap(i, carry)
        lax.fori_loop(0, CHUNK, lambda k, c: place(i * CHUNK + k, c), 0, unroll=8)

        @pl.when(i == 0)
        def _():
            for copy in loads:
                copy.wait()
            lax.fori_loop(0, SUB, round_row, 0)

        return carry

    lax.fori_loop(0, chunks, chunk, 0)


def field_kernel(
    cap,
    lines_hbm,
    block_hbm,
    land_hbm,
    gain_hbm,
    state_ref,
    far_hbm,
    near_hbm,
    diffusion_hbm,
    column_hbm,
    out_ref,
    top_ref,
    target_ref,
    gain_ref,
    lines_ref,
    block_ref,
    land_ref,
    factors,
    halo_ref,
    diffusion_ref,
    column_ref,
    slabs,
    u0,
    u1,
    coef,
    right,
    flags,
    half0,
    half1,
    small_sems,
    in_sems,
    out_sems,
):
    depth, rows, cells = state_ref.shape
    groups = rows // GROUP
    comp, fields = lax.axis_index("comp"), top_ref.shape[1]
    even = lax.rem(lax.axis_index("tile"), 2) == 0
    before_ref, after_ref = halo_ref.at[0], halo_ref.at[1]
    inside = pl.ds(EDGE, cells)
    below = pl.ds(fields, depth - fields)

    def load(x, carry):
        pltpu.make_async_copy(state_ref.at[:, x, :], slabs.at[x], in_sems.at[lax.div(x, GROUP)]).start()
        return carry

    small = copies(
        (
            (lines_hbm, lines_ref),
            (block_hbm, block_ref),
            (diffusion_hbm, diffusion_ref),
            (column_hbm, column_ref),
            (land_hbm, land_ref),
            (gain_hbm, factors),
            (far_hbm, halo_ref.at[jnp.where(even, 0, 1)]),
            (near_hbm, halo_ref.at[jnp.where(even, 1, 0)]),
        ),
        small_sems,
        0,
    )
    lax.fori_loop(0, rows, load, 0, unroll=4)

    def border(x, carry):
        zeros = jnp.zeros((EDGE, depth), jnp.float32)
        for u in (u0, u1):
            u[x, pl.ds(0, EDGE), :] = zeros
            u[x, pl.ds(EDGE + cells, EDGE), :] = zeros
        return carry
    lax.fori_loop(0, u0.shape[0], border, 0, unroll=2)
    for copy in small:
        copy.wait()
    target_ref[...] = arrivals(cap, rows, comp, lax.axis_index("tile"), lines_ref, block_ref)
    field_of = lax.broadcasted_iota(jnp.int32, (fields, cells), 0)
    gain = jnp.zeros((fields, cells), jnp.float32)
    for f in range(fields):
        gain = jnp.where(field_of == f, factors[0, f], gain)
    gain_ref[...] = gain

    rate = diffusion_ref[...]
    coef[0, 0] = jnp.ones_like(coef[0, 0])
    coef[0, 1] = jnp.zeros_like(coef[0, 0])
    coef[1, 0] = jnp.broadcast_to(1.0 - 4.0 * rate, (16, depth))
    coef[1, 1] = jnp.broadcast_to(rate, (16, depth))
    column = jnp.transpose(column_ref[...])
    high = column.astype(jnp.bfloat16)
    low = (column - high.astype(jnp.float32)).astype(jnp.bfloat16)
    right[0:depth, 0:depth] = high
    right[depth : 2 * depth, 0:depth] = high
    right[0:depth, depth : 2 * depth] = low
    right[depth : 2 * depth, depth : 2 * depth] = jnp.zeros_like(low)

    def own_flag(i, carry):
        flags[i + SUB] = jnp.where(comp == 1, land_ref[i], 1)
        return carry
    lax.fori_loop(0, rows, own_flag, 0, unroll=8)
    for r in range(SUB):
        flags[r] = jnp.max(before_ref[pl.ds(SUB * depth, 16), :][r : r + 1, :].astype(jnp.float32)).astype(jnp.int32)
        flags[rows + SUB + r] = jnp.max(
            after_ref[pl.ds(SUB * depth, 16), :][r : r + 1, :].astype(jnp.float32)
        ).astype(jnp.int32)
        u0[r, inside, :] = jnp.transpose(before_ref[pl.ds(r * depth, depth), :].astype(jnp.float32))
        u0[rows + SUB + r, inside, :] = jnp.transpose(after_ref[pl.ds(r * depth, depth), :].astype(jnp.float32))
    for r in range(rows + 2 * SUB, flags.shape[0]):
        flags[r] = 0

    def wait_in(g):
        pltpu.make_async_copy(
            slabs.at[pl.ds(g * GROUP, GROUP)], slabs.at[pl.ds(g * GROUP, GROUP)], in_sems.at[g]
        ).wait()

    def turn(s):
        u0[s + SUB, inside, :] = jnp.transpose(slabs[s])

    def stencil(source, x, half):
        for side in range(GROUP):
            active = flags[x + side]
            keep, spread = coef[active, 0], coef[active, 1]
            for k in range(0, cells, 16):
                at = pl.ds(EDGE + k, 16)
                near = source[x + side - 1, at, :] + source[x + side + 1, at, :]
                near += source[x + side, pl.ds(EDGE + k - 1, 16), :] + source[x + side, pl.ds(EDGE + k + 1, 16), :]
                stepped = keep * source[x + side, at, :] + spread * near
                high = stepped.astype(jnp.bfloat16)
                half[pl.ds(side * cells + k, 16), 0:depth] = high
                half[pl.ds(side * cells + k, 16), depth : 2 * depth] = (
                    stepped - high.astype(jnp.float32)
                ).astype(jnp.bfloat16)

    def product(half, count, store):
        mixed = jnp.dot(half[0 : count * cells], right[...], preferred_element_type=jnp.float32)
        mixed = mixed[:, 0:depth] + mixed[:, depth : 2 * depth]
        for side in range(count):
            store(side, mixed[side * cells : (side + 1) * cells])

    def keep_in(target, x):
        def store(side, values):
            target[x + side, inside, :] = values
        return store

    def finish(x):
        def store(side, values):
            turned = jnp.transpose(values)
            top_ref[x + side] = turned[0:fields]
            slabs[x + side] = turned
        return store

    def send_out(x):
        for side in range(GROUP):
            pltpu.make_async_copy(
                slabs.at[x + side, below, :], out_ref.at[below, x + side, :], out_sems.at[lax.div(x, GROUP)]
            ).start()

    wait_in(0)
    wait_in(1)
    for s in range(2 * GROUP - 1):
        turn(s)
    span = 2 * GROUP
    bodies = rows // span

    stencil(u0, 1, half0)
    def body1(i, carry):
        x = 1 + span * i
        @pl.when(2 * i + 3 < groups)
        def _():
            wait_in(2 * i + 2)
            wait_in(2 * i + 3)
        product(half0, GROUP, keep_in(u1, x))
        stencil(u0, x + GROUP, half1)
        for s in range(GROUP):
            turn(jnp.minimum(span * i + span - 1 + s, rows - 1))
        product(half1, GROUP, keep_in(u1, x + GROUP))
        stencil(u0, x + span, half0)
        for s in range(GROUP, span):
            turn(jnp.minimum(span * i + span - 1 + s, rows - 1))
        return carry
    lax.fori_loop(0, bodies, body1, 0)
    product(half0, 4, keep_in(u1, rows + 1))

    stencil(u1, 2, half0)
    def body2(i, carry):
        x = 2 + span * i
        product(half0, GROUP, keep_in(u0, x))
        stencil(u1, x + GROUP, half1)
        product(half1, GROUP, keep_in(u0, x + GROUP))
        stencil(u1, x + span, half0)
        return carry
    lax.fori_loop(0, bodies, body2, 0)
    product(half0, 2, keep_in(u0, rows + 2))

    stencil(u0, SUB, half0)
    def body3(i, carry):
        x = span * i
        product(half0, GROUP, finish(x))
        stencil(u0, SUB + x + GROUP, half1)
        send_out(x)
        product(half1, GROUP, finish(x + GROUP))
        stencil(u0, SUB + x + span, half0)
        send_out(x + GROUP)
        return carry
    lax.fori_loop(0, bodies, body3, 0)

    def wait_out(i, carry):
        part = slabs.at[pl.ds(0, GROUP), below, :]
        pltpu.make_async_copy(part, part, out_sems.at[i]).wait()
        return carry
    lax.fori_loop(0, groups, wait_out, 0)


def forcing_kernel(target_hbm, gain_ref, arrived_ref, top_ref, field_ref, out_ref, target_ref, total, result, sems):
    slots, fields, _ = arrived_ref.shape
    rows, _, cells = top_ref.shape
    (get_target,) = copies(((target_hbm, target_ref),), sems, 0)

    def begin(x, carry):
        total[pl.ds(pl.multiple_of(x * fields, fields), fields), :] = top_ref[x]
        return carry

    lax.fori_loop(0, rows, begin, 0, unroll=8)
    spare = pl.ds(rows * fields, SPARE * fields)
    total[spare, :] = jnp.zeros((SPARE * fields, cells), jnp.float32)
    gain = gain_ref[...]
    get_target.wait()
    lines = target_ref.shape[0]
    count = slots // lines

    def add(e, carry):
        for s in range(count):
            at = pl.ds(pl.multiple_of(target_ref[e, s] * fields, fields), fields)
            total[at, :] += gain * arrived_ref[e * count + s].astype(jnp.float32)
        return carry

    lax.fori_loop(0, lines, add, 0)

    def store(i):
        part = pl.ds(i * PART, PART)
        return pltpu.make_async_copy(result.at[part], out_ref.at[part], sems.at[1 + i])

    def finish(i, carry):
        for k in range(PART):
            result[i * PART + k] = total[pl.ds(i * PART + k, rows, stride=fields), :]
        store(i).start()
        return carry

    def wait(i, carry):
        store(i).wait()
        return carry

    lax.fori_loop(0, fields // PART, finish, 0)
    lax.fori_loop(0, fields // PART, wait, 0)


def on_device(
    prognostic_state,
    remapping_weight,
    diffusion,
    column_op,
    couple_gain,
    land_mask,
    dest_tile,
    dest_block,
):
    tiles = lax.axis_size("tile")
    in_hbm = functools.partial(pltpu.with_memory_space_constraint, memory_space=pltpu.HBM)
    state = in_hbm(prognostic_state[0])
    depth, rows, cells = state.shape
    fields = couple_gain.shape[1]
    cap = max(2, 2 * rows // tiles)
    slots = tiles * cap
    halo_rows = SUB * depth + 16
    routes = in_hbm(dest_tile.reshape(-1))
    lines = tiles * rows // 128

    vmem = pl.BlockSpec(memory_space=pltpu.VMEM)
    anywhere = pl.BlockSpec(memory_space=pltpu.HBM)

    outgoing, far, near = pl.pallas_call(
        functools.partial(send_kernel, cap, tiles),
        out_shape=(
            jax.ShapeDtypeStruct((slots, fields, cells), jnp.bfloat16),
            jax.ShapeDtypeStruct((halo_rows, cells), jnp.bfloat16),
            jax.ShapeDtypeStruct((halo_rows, cells), jnp.bfloat16),
        ),
        in_specs=[anywhere] * 4,
        out_specs=(vmem, vmem, vmem),
        scratch_shapes=[
            pltpu.SMEM(routes.shape, jnp.int32),
            pltpu.SMEM(land_mask.shape, jnp.int32),
            pltpu.VMEM((fields * rows, cells), jnp.float32),
            pltpu.VMEM((rows, cells, cells), jnp.bfloat16),
            pltpu.VMEM((2 * SUB, depth, cells), jnp.float32),
            pltpu.VMEM((rows, fields, cells), jnp.bfloat16),
            pltpu.SMEM((tiles,), jnp.int32),
            pltpu.SemaphoreType.DMA((3 + 2 * SUB + rows // CHUNK,)),
        ],
        compiler_params=pltpu.CompilerParams(vmem_limit_bytes=32 << 20),
        cost_estimate=pl.CostEstimate(
            flops=2 * rows * fields * cells * cells, bytes_accessed=8 << 20, transcendentals=0
        ),
        name="remap_and_pack",
    )(routes, in_hbm(land_mask), state, in_hbm(remapping_weight[0]))

    odd = [(i, (i + 1) % tiles) for i in range(1, tiles, 2)]
    far = lax.ppermute(far, "tile", odd + [(b, a) for a, b in odd])
    near = lax.ppermute(near, "tile", [(i, i ^ 1) for i in range(tiles)])
    swapped = lax.ppermute(outgoing, "comp", [(0, 1), (1, 0)])
    arrived = lax.all_to_all(swapped, "tile", split_axis=0, concat_axis=0, tiled=True)

    total_rows = rows + 2 * SUB + GROUP
    field, top, target, gain = pl.pallas_call(
        functools.partial(field_kernel, cap),
        out_shape=(
            jax.ShapeDtypeStruct((depth, rows, cells), jnp.float32),
            jax.ShapeDtypeStruct((rows, fields, cells), jnp.float32),
            jax.ShapeDtypeStruct((lines, 128), jnp.int32),
            jax.ShapeDtypeStruct((fields, cells), jnp.float32),
        ),
        in_specs=[anywhere] * 9,
        out_specs=(anywhere, vmem, vmem, vmem),
        scratch_shapes=[
            pltpu.VMEM((2 * lines, 128), jnp.int32),
            pltpu.VMEM(dest_block.shape, jnp.int32),
            pltpu.SMEM((rows,), jnp.int32),
            pltpu.SMEM(couple_gain.shape, jnp.float32),
            pltpu.VMEM((2, halo_rows, cells), jnp.bfloat16),
            pltpu.VMEM((1, depth), jnp.float32),
            pltpu.VMEM((depth, depth), jnp.float32),
            pltpu.VMEM((rows, depth, cells), jnp.float32),
            pltpu.VMEM((total_rows, cells + 2 * EDGE, depth), jnp.float32),
            pltpu.VMEM((total_rows, cells + 2 * EDGE, depth), jnp.float32),
            pltpu.VMEM((2, 2, 16, depth), jnp.float32),
            pltpu.VMEM((2 * depth, 2 * depth), jnp.bfloat16),
            pltpu.SMEM((total_rows,), jnp.int32),
            pltpu.VMEM((GROUP * cells, 2 * depth), jnp.bfloat16),
            pltpu.VMEM((GROUP * cells, 2 * depth), jnp.bfloat16),
            pltpu.SemaphoreType.DMA((8,)),
            pltpu.SemaphoreType.DMA((rows // GROUP,)),
            pltpu.SemaphoreType.DMA((rows // GROUP,)),
        ],
        compiler_params=pltpu.CompilerParams(vmem_limit_bytes=32 << 20),
        cost_estimate=pl.CostEstimate(
            flops=120 * depth * depth * rows * cells,
            bytes_accessed=8 * depth * rows * cells,
            transcendentals=0,
        ),
        name="substeps",
    )(
        in_hbm(dest_tile.reshape(2 * lines, 128)),
        in_hbm(dest_block),
        in_hbm(land_mask),
        in_hbm(couple_gain),
        state,
        far,
        near,
        in_hbm(diffusion),
        in_hbm(column_op[0]),
    )

    new_state = pl.pallas_call(
        forcing_kernel,
        out_shape=jax.ShapeDtypeStruct((depth, rows, cells), jnp.float32),
        in_specs=[anywhere, vmem, vmem, vmem, anywhere],
        out_specs=anywhere,
        input_output_aliases={4: 0},
        scratch_shapes=[
            pltpu.SMEM((lines, 128), jnp.int32),
            pltpu.VMEM(((rows + SPARE) * fields, cells), jnp.float32),
            pltpu.VMEM((fields, rows, cells), jnp.float32),
            pltpu.SemaphoreType.DMA((1 + fields // PART,)),
        ],
        compiler_params=pltpu.CompilerParams(vmem_limit_bytes=32 << 20),
        name="add_forcing",
    )(target, gain, arrived, top, field)
    return new_state[None]


def solution(mesh):
    placed = (
        P("comp", "member", "tile", None),
        P("comp", "tile", None, None),
        P("comp", "member"),
        P("comp", "member", None),
        P("comp", "member"),
        P("tile"),
        P(),
        P(),
    )
    return jax.shard_map(
        on_device,
        mesh=mesh,
        in_specs=placed,
        out_specs=P("comp", "member", "tile", None),
        check_vma=False,
    )
```
